256 devices in a mesh: prow: 16 (over y, x), pcol: 16 (over z, core).
Axes of the slice: x: 4, y: 4, z: 8, core: 2. Of those that a mesh axis runs over, the one named last changes fastest.
Arguments:
- right_side: float32 [19, 16, 32768], P(None, 'pcol', 'prow'), may hold values from -6 to 6
- inverse_rows: float32 [19, 16, 512, 512], P(None, 'pcol', 'prow'), may hold values from -0.25 to 0.25
- panels: float32 [19, 16, 7, 512, 512], P(None, 'pcol', None, 'prow'), may hold values from -0.0625 to 0.0625
- pattern: int32 [19, 16, 7], P(None, 'pcol'), may hold values 0 or 1
- node_sizes: int32 [19, 16], P(None, 'pcol'), may hold values from 256 to 512
- parent: int32 [254], replicated, may hold values from 128 to 254, as said below
Outputs:
- solution: float32 [19, 16, 32768], P(None, 'pcol', 'prow')
The draws below stay inside these ranges and needn't reach their ends.
Inputs may be any that keep to these rules, and one draw needn't show every extreme that they name: Nodes are numbered level by level from the leaves (128 of them, halving up to one root); entry g is the number of node g's parent, which lies on the next level up, and every node above the leaves has exactly two children.
All inputs are finite; a program needn't handle non-finite values. No bound on the sum of `pattern` on one device may be relied on, other than what follows from the above.
Results may differ from the reference program's by a relative error of at most 0.0001.
Values sent between devices are 32-bit elements; how exact they have to be, the bound alone decides.
No kernel may reach another device: no remote copies, remote signals or barrier semaphores. Data moves between devices by JAX's collectives and lax.ppermute only.
A program may use at most 128 MiB of HBM per device.

```python
import jax
import jax.numpy as jnp
from jax import lax

W = 512
R = 64
LEVELS = 8
LEAVES = 128
ANC = 7
SLOTS = 19
N_PCOL = 16


def draw_parent(key, part):
    pieces = []
    for height in range(LEVELS - 1):
        level_nodes = LEAVES >> height
        shuffled = jax.random.permutation(jax.random.fold_in(key, height + 11), level_nodes).astype(jnp.int32)
        upper_base = 2 * LEAVES - (LEAVES >> height)
        pieces.append(upper_base + shuffled // 2)
    return jnp.concatenate(pieces, 0).astype(jnp.int32)


def touch_ends(drawn, rng, least, high):
    longest = drawn.shape.index(max(drawn.shape))
    spots = []
    for shift in (0, 1):
        where = [jax.random.randint(jax.random.fold_in(rng, axis), (), 0, length) for axis, length in enumerate(drawn.shape)]
        where[longest] = (where[longest] + shift) % drawn.shape[longest]
        spots.append(tuple(where))
    return drawn.at[spots[0]].set(least).at[spots[1]].set(high)


def level_of(stream_key, dims, cuts, least, largest):
    loudness, own = 1.0, jax.random.fold_in(stream_key, 6)
    for position, shards_of in cuts:
        heights = jnp.exp(jax.random.uniform(jax.random.fold_in(own, position), (shards_of,), jnp.float32, least / len(cuts), largest / len(cuts)))
        loudness = loudness * jnp.repeat(heights, dims[position] // shards_of).reshape([-1 if axis == position else 1 for axis in range(len(dims))])
    return loudness


def scatter_about(key, dims, spread, limit, cuts=(), kind=jnp.bfloat16):
    loudness = level_of(key, dims, cuts, -0.22, 0.18) if cuts else 1.0
    values = jax.random.normal(key, dims, jnp.float32) * spread * loudness
    return jnp.minimum(jnp.maximum(values, -limit), limit).astype(kind)


def setup_inputs(seed: int = 0) -> dict:
    keys = jax.random.split(jax.random.key(seed), 7)
    right_side = scatter_about(keys[0], (SLOTS, N_PCOL, W * R), 1.0, 6.0, ((1, 16), (2, 16)), jnp.float32)
    inverse_rows = scatter_about(keys[1], (SLOTS, N_PCOL, W, W), W ** -0.5, 0.25, ((1, 16), (2, 16)), jnp.float32)
    panels = scatter_about(keys[2], (SLOTS, N_PCOL, ANC, W, W), (W * 16) ** -0.5, 0.0625, ((1, 16), (3, 16)), jnp.float32)
    pattern = touch_ends((jax.random.randint(keys[3], (SLOTS, N_PCOL, ANC), 0, 2) < 1).astype(jnp.int32), jax.random.fold_in(keys[3], 1), 0, 1)
    node_sizes = touch_ends(jax.random.randint(keys[4], (SLOTS, N_PCOL), W // 2, W + 1), jax.random.fold_in(keys[4], 1), W // 2, W).astype(jnp.int32)
    parent = draw_parent(jax.random.fold_in(keys[6], 71), 0)
    return dict(right_side=right_side, inverse_rows=inverse_rows, panels=panels, pattern=pattern, node_sizes=node_sizes, parent=parent)


def level_offset(height):
    return 2 * LEAVES - 2 * (LEAVES >> height)


def reference(right_side, inverse_rows, panels, pattern, node_sizes, parent):
    col_count = N_PCOL
    solution = jnp.zeros_like(right_side)
    updates = {}
    for height in range(1, LEVELS):
        updates[height] = jnp.zeros((LEAVES >> height, W, R), jnp.float32)
    slot_base = 0
    for height in range(LEVELS):
        level_nodes = LEAVES >> height
        node_index = jnp.arange(level_nodes, dtype=jnp.int32)
        slot_index = slot_base + node_index // col_count
        col_index = node_index % col_count
        residue = right_side[slot_index, col_index].reshape(level_nodes, W, R)
        if height > 0:
            residue = residue - updates[height]
        live_rows = (jnp.arange(W, dtype=jnp.int32)[None, :] < node_sizes[slot_index, col_index][:, None]).astype(jnp.float32)
        residue = residue * live_rows[:, :, None]
        inverse = inverse_rows[slot_index, col_index]
        solved = jnp.einsum("nvw,nvq->nwq", inverse, residue, precision=lax.Precision.HIGHEST)
        solved = solved * live_rows[:, :, None]
        solution = solution.at[slot_index, col_index].set(solved.reshape(level_nodes, W * R))
        ancestor = level_offset(height) + node_index
        for distance in range(LEVELS - 1 - height):
            ancestor = parent[ancestor]
            target = height + 1 + distance
            block = panels[slot_index, col_index, distance]
            contrib = jnp.einsum("nwv,nvq->nwq", block, solved, precision=lax.Precision.HIGHEST)
            contrib = contrib * pattern[slot_index, col_index, distance].astype(jnp.float32)[:, None, None]
            onehot = ((ancestor - level_offset(target))[:, None] == jnp.arange(LEAVES >> target, dtype=jnp.int32)[None, :]).astype(jnp.float32)
            updates[target] = updates[target] + jnp.einsum("nt,nwq->twq", onehot, contrib, precision=lax.Precision.HIGHEST)
        slot_base = slot_base + max(1, level_nodes // col_count)
    return solution
```

```python
import functools

import jax
import jax.numpy as jnp
from jax import lax
from jax.experimental import pallas as pl
from jax.experimental.pallas import tpu as pltpu
from jax.sharding import PartitionSpec as P

LEVELS = 8
LEAVES = 128
GATHER_FROM = 1
VMEM_LIMIT = 24 * 1024 * 1024

NODES = [LEAVES >> h for h in range(LEVELS)]
NODE_BASE = [2 * LEAVES - 2 * (LEAVES >> h) for h in range(LEVELS)]


def split(x):
    high = x.astype(jnp.bfloat16)
    low = (x - high.astype(jnp.float32)).astype(jnp.bfloat16)
    return high, low


def dot3(a, b, dims):
    ah, al = split(a)
    bh, bl = split(b)
    dot = functools.partial(
        lax.dot_general, dimension_numbers=(dims, ((), ())), preferred_element_type=jnp.float32
    )
    return dot(ah, bh) + (dot(ah, bl) + dot(al, bh))


def unfold(x, scratch):
    n = x.shape[0]
    scratch[pl.ds(0, n, stride=2), :] = x
    scratch[pl.ds(1, n, stride=2), :] = pltpu.roll(x, 64, 1)
    return scratch[pl.ds(0, 2 * n), :][:, :64]


def fold(x, scratch):
    n = x.shape[0] // 2
    scratch[pl.ds(0, 2 * n), :] = jnp.concatenate([x, x], 1)
    even = scratch[pl.ds(0, n, stride=2), :]
    odd = scratch[pl.ds(1, n, stride=2), :]
    lane = lax.broadcasted_iota(jnp.int32, (n, 128), 1)
    return jnp.where(lane < 64, even, odd)


def own_mask(pos, sizes, slot, local, nodes):
    row = lax.broadcasted_iota(jnp.int32, (16, 128), 0)
    lane = lax.broadcasted_iota(jnp.int32, (16, 128), 1)
    row_id = pos[0] * 32 + 2 * row + (lane >= 64).astype(jnp.int32)
    limit = jnp.where(local * 16 + pos[1] < nodes, sizes[slot], 0)
    return row_id < limit


def residue_kernel(height, slots, slot_base, pos, parent, pattern, sizes, recv, rhs, out):
    for s in range(slots):
        total = recv[0, s]
        for i in range(1, 16):
            total = total + recv[i, s]
        keep = own_mask(pos, sizes, slot_base + s, s, NODES[height])
        z = jnp.where(keep, rhs[s] - total, 0.0)
        for i in range(16):
            out[i, s] = z


def partial_kernel(height, slots, slot_base, pos, parent, pattern, sizes, *refs):
    recv = None
    if height > 0:
        recv, *refs = refs
    rhs, inverse, out, scratch = refs
    s = pl.program_id(0)
    z = rhs[0]
    if recv is not None:
        total = recv[0, 0]
        for i in range(1, 16):
            total = total + recv[i, 0]
        z = z - total
    keep = own_mask(pos, sizes, slot_base + s, s, NODES[height])
    z = jnp.where(keep, z, 0.0)
    z = unfold(z, scratch)
    part = dot3(inverse[0, 0], z, ((0,), (0,)))
    out[:, 0] = fold(part, scratch).reshape(16, 16, 128)


def solved_kernel(height, slots, slot_base, pos, parent, pattern, sizes, recv, out, sol):
    for s in range(slots):
        total = recv[0, s]
        for i in range(1, 16):
            total = total + recv[i, s]
        keep = own_mask(pos, sizes, slot_base + s, s, NODES[height])
        y = jnp.where(keep, total, 0.0)
        sol[s] = y
        for i in range(16):
            out[i, s] = y


def spread_kernel(height, slots, slot_base, whole, pos, parent, pattern, sizes, *refs):
    reach = LEVELS - 1 - height
    refs = list(refs)
    gathered = refs.pop(0)
    inverse = refs.pop(0) if whole else None
    panels = refs.pop(0) if reach else None
    before = [refs.pop(0) for _ in range(reach)] if height > 0 else []
    sol = refs.pop(0) if whole else None
    after = [refs.pop(0) for _ in range(reach)]
    scratch = refs.pop(0)
    s = pl.program_id(0)

    @pl.when(s == 0)
    def _():
        for i, ref in enumerate(after):
            ref[...] = before[i][...] if before else jnp.zeros_like(ref)

    x = unfold(gathered[:, 0].reshape(256, 128), scratch)
    slot = slot_base + s
    if whole:
        y_t = dot3(x.T, inverse[:, 0].reshape(512, 512), ((1,), (0,)))
        limit = sizes[slot]
        y_t = jnp.where(lax.broadcasted_iota(jnp.int32, (64, 512), 1) < limit, y_t, 0.0)
        y = y_t.T
        scratch[...] = jnp.concatenate([y, y], 1)
        own = scratch[pl.ds(pl.multiple_of(pos[0] * 32, 32), 32), :]
        sol[0] = fold(own[:, :64], scratch)
    else:
        y_t = x.T
    if reach:
        block = panels[0, 0].reshape(reach * 32, 512)
        update = fold(dot3(block, y_t, ((1,), (1,))), scratch)
        node = NODE_BASE[height] + jnp.minimum(s * 16 + pos[1], NODES[height] - 1)
        for d in range(reach):
            node = parent[node]
            target = height + 1 + d
            j = node - NODE_BASE[target]
            where = (j % 16) * max(1, NODES[target] // 16) + j // 16
            scale = pattern[slot * 7 + d].astype(jnp.float32)
            after[d][where] += scale * update[d * 16 : (d + 1) * 16]


def on_device(right_side, inverse_rows, panels, pattern, node_sizes, parent):
    pos = jnp.stack([lax.axis_index("prow"), lax.axis_index("pcol")]).astype(jnp.int32)
    rhs = right_side.reshape(19, 16, 128)
    scalars = (pos, parent, pattern.reshape(-1), node_sizes.reshape(-1))
    slot_counts = [max(1, n // 16) for n in NODES]
    bases = [sum(slot_counts[:h]) for h in range(LEVELS)]
    first = bases[GATHER_FROM]
    cuts = [first, bases[min(GATHER_FROM + 1, LEVELS - 1)], 19]
    inverses = []
    for lo, hi in zip(cuts[:-1], cuts[1:]):
        inverses.append((lo, lax.all_gather(inverse_rows[lo:hi, 0], "prow", axis=0)))

    def call(kernel, scratch, grid, in_specs, out_specs, out_shape, aliases, *args):
        return pl.pallas_call(
            kernel,
            grid_spec=pltpu.PrefetchScalarGridSpec(
                num_scalar_prefetch=4,
                grid=grid,
                in_specs=in_specs,
                out_specs=out_specs,
                scratch_shapes=[pltpu.VMEM((512, 128), jnp.float32)] if scratch else [],
            ),
            out_shape=out_shape,
            input_output_aliases={k + 4: v for k, v in aliases.items()},
            compiler_params=pltpu.CompilerParams(vmem_limit_bytes=VMEM_LIMIT),
        )(*scalars, *args)

    def exchange(x, axis):
        return lax.all_to_all(x, axis, 0, 0, tiled=True)

    f32 = jnp.float32
    pending = []
    recv = None
    outputs = []
    for height in range(LEVELS):
        count = slot_counts[height]
        base = bases[height]
        reach = LEVELS - 1 - height
        info = (height, count, base)
        whole = height >= GATHER_FROM
        piece = jax.ShapeDtypeStruct((16, count, 16, 128), f32)
        own = jax.ShapeDtypeStruct((count, 16, 128), f32)
        every = pl.BlockSpec((16, count, 16, 128), lambda *_: (0, 0, 0, 0))
        every_own = pl.BlockSpec((count, 16, 128), lambda *_: (0, 0, 0))
        one = pl.BlockSpec((16, 1, 16, 128), lambda s, *_: (0, s, 0, 0))
        rhs_all = pl.BlockSpec((count, 16, 128), lambda *_, b=base // count: (b, 0, 0))
        if whole:
            z = call(
                functools.partial(residue_kernel, *info), False, (1,), [every, rhs_all], every, piece, {}, recv, rhs
            )
            gathered = exchange(z, "prow")
        else:
            in_specs = [
                pl.BlockSpec((1, 16, 128), lambda s, *_, b=base: (b + s, 0, 0)),
                pl.BlockSpec((1, 1, 32, 512), lambda s, *_, b=base: (b + s, 0, 0, 0)),
            ]
            args = [rhs, inverse_rows]
            if height > 0:
                in_specs, args = [one] + in_specs, [recv] + args
            parts = call(functools.partial(partial_kernel, *info), True, (count,), in_specs, one, piece, {}, *args)
            parts = exchange(parts, "prow")
            y, sol = call(
                functools.partial(solved_kernel, *info), False, (1,), [every], [every, every_own], [piece, own], {}, parts
            )
            outputs.append(sol)
            gathered = exchange(y, "prow")
        in_specs, args = [one], [gathered]
        out_specs, out_shape = [], []
        if whole:
            lo, inverse = [pair for pair in inverses if pair[0] <= base][-1]
            in_specs.append(pl.BlockSpec((16, 1, 32, 512), lambda s, *_, b=base - lo: (0, b + s, 0, 0)))
            args.append(inverse)
            out_specs.append(pl.BlockSpec((1, 16, 128), lambda s, *_: (s, 0, 0)))
            out_shape.append(own)
        if reach:
            in_specs.append(
                pl.BlockSpec((1, 1, reach, 32, 512), lambda s, *_, b=base: (b + s, 0, 0, 0, 0))
            )
            args.append(panels)
        aliases = {}
        for d in range(reach):
            shape = (16 * slot_counts[height + 1 + d], 16, 128)
            spec = pl.BlockSpec(shape, lambda *_: (0, 0, 0))
            if height > 0:
                aliases[len(in_specs)] = len(out_specs)
                in_specs.append(spec)
                args.append(pending[d])
            out_specs.append(spec)
            out_shape.append(jax.ShapeDtypeStruct(shape, f32))
        results = call(
            functools.partial(spread_kernel, *info, whole), True, (count,), in_specs, out_specs, out_shape, aliases, *args
        )
        results = list(results)
        if whole:
            outputs.append(results.pop(0))
        if reach:
            following = slot_counts[height + 1]
            recv = exchange(results[0].reshape(16, following, 16, 128), "pcol")
            pending = results[1:]
    return jnp.concatenate(outputs, 0).reshape(19, 1, 2048)


def solution(mesh):
    in_specs = (
        P(None, "pcol", "prow"),
        P(None, "pcol", "prow", None),
        P(None, "pcol", None, "prow", None),
        P(None, "pcol", None),
        P(None, "pcol"),
        P(),
    )
    out_specs = P(None, "pcol", "prow")
    return jax.shard_map(
        on_device, mesh=mesh, in_specs=in_specs, out_specs=out_specs, check_vma=False
    )
```

```python
import functools

import jax
import jax.numpy as jnp
from jax import lax
from jax.experimental import pallas as pl
from jax.experimental.pallas import tpu as pltpu
from jax.sharding import PartitionSpec as P

LEVELS = 8
LEAVES = 128
GATHER_FROM = 1
CUTS = (1, 5)
SCRATCH = [pltpu.VMEM((512, 128), jnp.float32)]
TOP = 5
VMEM_LIMIT = 24 * 1024 * 1024

NODES = [LEAVES >> h for h in range(LEVELS)]
NODE_BASE = [2 * LEAVES - 2 * (LEAVES >> h) for h in range(LEVELS)]


class Part:
    def __init__(self, ref, start):
        self.ref, self.start = ref, start

    def __getitem__(self, index):
        return self.ref[index + self.start]


def with_parts(kernel, *refs):
    return kernel(*[Part(refs[0], start) for start in (0, 2, 256, 389)], *refs[1:])


def split(x):
    high = x.astype(jnp.bfloat16)
    low = (x - high.astype(jnp.float32)).astype(jnp.bfloat16)
    return high, low


def dot3(a, b, dims):
    bh, bl = split(b)
    n = a.shape[0]
    if n <= 64 and dims[0] == (1,):
        high = a.astype(jnp.bfloat16).astype(jnp.float32)
        both = jnp.concatenate([high, a - high], 0).astype(jnp.bfloat16)
        dot = functools.partial(
            lax.dot_general, dimension_numbers=(dims, ((), ())), preferred_element_type=jnp.float32
        )
        first = dot(both, bh)
        second = dot(high.astype(jnp.bfloat16), bl)
        return first[:n] + (first[n:] + second)
    ah, al = split(a)
    dot = functools.partial(
        lax.dot_general, dimension_numbers=(dims, ((), ())), preferred_element_type=jnp.float32
    )
    return dot(ah, bh) + (dot(ah, bl) + dot(al, bh))


def unfold(x, scratch):
    n = x.shape[0]
    scratch[pl.ds(0, n, stride=2), :] = x
    scratch[pl.ds(1, n, stride=2), :] = pltpu.roll(x, 64, 1)
    return scratch[pl.ds(0, 2 * n), :][:, :64]


def fold(x, scratch):
    n = x.shape[0] // 2
    scratch[pl.ds(0, 2 * n), :] = jnp.concatenate([x, x], 1)
    even = scratch[pl.ds(0, n, stride=2), :]
    odd = scratch[pl.ds(1, n, stride=2), :]
    lane = lax.broadcasted_iota(jnp.int32, (n, 128), 1)
    return jnp.where(lane < 64, even, odd)


def own_mask(pos, sizes, slot, local, nodes):
    row = lax.broadcasted_iota(jnp.int32, (16, 128), 0)
    lane = lax.broadcasted_iota(jnp.int32, (16, 128), 1)
    row_id = pos[0] * 32 + 2 * row + (lane >= 64).astype(jnp.int32)
    limit = jnp.where(local * 16 + pos[1] < nodes, sizes[slot], 0)
    return row_id < limit


def residue_kernel(height, slots, slot_base, pos, parent, pattern, sizes, recv, rhs, out):
    for s in range(slots):
        total = recv[0, s]
        for i in range(1, 16):
            total = total + recv[i, s]
        keep = own_mask(pos, sizes, slot_base + s, s, NODES[height])
        z = jnp.where(keep, rhs[s] - total, 0.0)
        for i in range(16):
            out[i, s] = z


def partial_kernel(height, slots, slot_base, pos, parent, pattern, sizes, *refs):
    recv = None
    if height > 0:
        recv, *refs = refs
    rhs, inverse, out, scratch = refs
    s = pl.program_id(0)
    z = rhs[0]
    if recv is not None:
        total = recv[0, 0]
        for i in range(1, 16):
            total = total + recv[i, 0]
        z = z - total
    keep = own_mask(pos, sizes, slot_base + s, s, NODES[height])
    z = jnp.where(keep, z, 0.0)
    z = unfold(z, scratch)
    part = dot3(inverse[0, 0], z, ((0,), (0,)))
    out[:, 0] = fold(part, scratch).reshape(16, 16, 128)


def solved_kernel(height, slots, slot_base, pos, parent, pattern, sizes, recv, out, sol):
    for s in range(slots):
        total = recv[0, s]
        for i in range(1, 16):
            total = total + recv[i, s]
        keep = own_mask(pos, sizes, slot_base + s, s, NODES[height])
        y = jnp.where(keep, total, 0.0)
        sol[s] = y
        for i in range(16):
            out[i, s] = y


def spread_kernel(height, slots, slot_base, whole, pos, parent, pattern, sizes, *refs):
    reach = LEVELS - 1 - height
    refs = list(refs)
    gathered = refs.pop(0)
    inverse = refs.pop(0) if whole else None
    panels = refs.pop(0) if reach else None
    before = [refs.pop(0) for _ in range(reach)] if height > 0 else []
    sol = refs.pop(0) if whole else None
    after = [refs.pop(0) for _ in range(reach)]
    scratch = refs.pop(0)
    s = pl.program_id(0)

    @pl.when(s == 0)
    def _():
        for i, ref in enumerate(after):
            ref[...] = before[i][...] if before else jnp.zeros_like(ref)

    x = unfold(gathered[:, 0].reshape(256, 128), scratch)
    slot = slot_base + s
    if whole:
        y_t = dot3(x.T, inverse[:, 0].reshape(512, 512), ((1,), (0,)))
        limit = sizes[slot]
        y_t = jnp.where(lax.broadcasted_iota(jnp.int32, (64, 512), 1) < limit, y_t, 0.0)
        y = y_t.T
        scratch[...] = jnp.concatenate([y, y], 1)
        own = scratch[pl.ds(pl.multiple_of(pos[0] * 32, 32), 32), :]
        sol[0] = fold(own[:, :64], scratch)
    else:
        y_t = x.T
    if reach:
        block = panels[0, 0].reshape(reach * 32, 512)
        update = fold(dot3(block, y_t, ((1,), (1,))), scratch)
        node = NODE_BASE[height] + jnp.minimum(s * 16 + pos[1], NODES[height] - 1)
        for d in range(reach):
            node = parent[node]
            target = height + 1 + d
            j = node - NODE_BASE[target]
            where = (j % 16) * max(1, NODES[target] // 16) + j // 16
            scale = pattern[slot * 7 + d].astype(jnp.float32)
            after[d][where] += scale * update[d * 16 : (d + 1) * 16]


def pack_kernel(pos, parent, pattern, sizes, inv5, inv6, inv7, panel5, panel6, *refs):
    half = len(refs) // 2
    for source, target in zip(refs[:half], refs[half + 1 :]):
        target[...] = source[:, 0]
    out = refs[half]
    for level, inv, panel, at in ((0, inv5, panel5, 3), (1, inv6, panel6, 0), (2, inv7, None, 2)):
        slot = 16 + level
        size = sizes[slot]
        row = pos[0] * 32 + lax.broadcasted_iota(jnp.int32, (32, 512), 0)
        column = lax.broadcasted_iota(jnp.int32, (32, 512), 1)
        out[at] = jnp.where((row < size) & (column < size), inv[0, 0], 0.0)
        for d in range(2 - level):
            out[at + 1 + d] = panel[0, 0, d] * pattern[slot * 7 + d].astype(jnp.float32)


def choose_kernel(pos, parent, pattern, sizes, low, middle, high, out):
    for c in range(4):
        out[3 * c : 3 * c + 3] = low[c]
    for c in range(2):
        out[12 + 2 * c : 14 + 2 * c] = middle[c]
    out[16:17] = high[0]


def turn_kernel(pos, parent, pattern, sizes, p5, p6, p7, rhs, out, scratch):
    at = 0
    for level, ref in enumerate((p5, p6, p7)):
        for j in range(4 >> level):
            piece = ref[j] - jnp.where(pos[1] == j, rhs[16 + level], 0.0)
            scratch[pl.ds(at * 32, 16, stride=2), :] = piece
            scratch[pl.ds(at * 32 + 1, 16, stride=2), :] = pltpu.roll(piece, 64, 1)
            at += 1
    scratch[pl.ds(224, 32), :] = jnp.zeros((32, 128), jnp.float32)
    turned = scratch[pl.ds(0, 256), :].T
    for z in range(8):
        out[2 * z] = turned[8 * z : 8 * z + 8]
        out[2 * z + 1] = turned[8 * z : 8 * z + 8]


def sum_kernel(pos, parent, pattern, sizes, recv, out):
    total = recv[0]
    for i in range(1, 16):
        total = total + recv[i]
    for i in range(16):
        out[i] = total


def place(own, y, level, pos):
    lanes = pltpu.roll(y, (256 - (pos[0] % 8) * 32) % 256, 1)[:, :128]
    lane = lax.broadcasted_iota(jnp.int32, (8, 128), 1) // 32
    return jnp.where(lane == level, pltpu.roll(lanes, level * 32, 1), own)


def low_kernel(pos, parent, pattern, sizes, recv, block, out, left, z, y):
    step = pl.program_id(0)

    @pl.when(step == 0)
    def _():
        lane = lax.broadcasted_iota(jnp.int32, (8, 128), 1) // 32
        for n in range(7):
            for g in range(4):
                whole = jnp.zeros((8, 128), jnp.float32)
                for i in range(4):
                    piece = recv[4 * g + i][:, (n // 4) * 128 : (n // 4 + 1) * 128]
                    turned = pltpu.roll(piece, ((i - n % 4) * 32) % 128, 1)
                    whole = jnp.where(lane == i, turned, whole)
                if n < 4:
                    z[n, :, g * 128 : (g + 1) * 128] = -whole
                else:
                    left[n - 4, :, g * 128 : (g + 1) * 128] = jnp.where(pos[1] % 2 == 0, -whole, 0.0)
        out[...] = jnp.zeros_like(out)

    node, kind = step // 3, step % 3
    matrix = block[:, 0].reshape(512, 256)

    @pl.when(kind == 0)
    def _():
        solved = dot3(z[node], matrix, ((1,), (0,)))
        y[...] = solved
        out[node] = place(out[node], solved, 0, pos)

    @pl.when(kind > 0)
    def _():
        update = dot3(y[...], matrix, ((1,), (1,)))
        target = jnp.where(kind == 1, parent[NODE_BASE[TOP] + node] - NODE_BASE[TOP + 1], 2)
        left[target] = left[target] - update


def middle_kernel(pos, parent, pattern, sizes, left, other, before, block, out, after, y):
    step = pl.program_id(0)

    @pl.when(step == 0)
    def _():
        out[...] = before[...]
        after[...] = left[2]

    node, kind = step // 2, step % 2
    matrix = block[:, 0].reshape(512, 256)

    @pl.when(kind == 0)
    def _():
        solved = dot3(left[node] + other[node], matrix, ((1,), (0,)))
        y[...] = solved
        out[node] = place(out[node], solved, 1, pos)

    @pl.when(kind > 0)
    def _():
        after[...] = after[...] - dot3(y[...], matrix, ((1,), (1,)))


def root_kernel(pos, parent, pattern, sizes, left, other, before, block, out):
    solved = dot3(left[...] + other[...], block[:, 0].reshape(512, 256), ((1,), (0,)))
    out[...] = before[...]
    out[0] = place(before[0], solved, 2, pos)


def last_kernel(pos, parent, pattern, sizes, recv, out, scratch):
    columns = jnp.concatenate([recv[2 * i + pos[0] // 8] for i in range(8)], 0)
    scratch[pl.ds(0, 64), :] = columns
    scratch[pl.ds(64, 64), :] = columns
    turned = scratch[pl.ds(0, 128), :].T
    scratch[pl.ds(128, 128), :] = turned
    lane = lax.broadcasted_iota(jnp.int32, (16, 128), 1)
    for level in range(3):
        even = scratch[pl.ds(128 + level * 32, 16, stride=2), :]
        odd = scratch[pl.ds(129 + level * 32, 16, stride=2), :]
        out[level] = jnp.where(lane < 64, even, odd)


def on_device(right_side, inverse_rows, panels, pattern, node_sizes, parent):
    pos = jnp.stack([lax.axis_index("prow"), lax.axis_index("pcol")]).astype(jnp.int32)
    rhs = right_side.reshape(19, 16, 128)
    scalars = jnp.concatenate([pos, parent, pattern.reshape(-1), node_sizes.reshape(-1)])
    slot_counts = [max(1, n // 16) for n in NODES]
    bases = [sum(slot_counts[:h]) for h in range(LEVELS)]
    def call(kernel, scratch, grid, in_specs, out_specs, out_shape, aliases, *args):
        args = [pltpu.with_memory_space_constraint(a, pltpu.HBM) if a.size > 1 << 18 else a for a in args]
        return pl.pallas_call(
            functools.partial(with_parts, kernel),
            grid_spec=pltpu.PrefetchScalarGridSpec(
                num_scalar_prefetch=1,
                grid=grid,
                in_specs=in_specs,
                out_specs=out_specs,
                scratch_shapes=scratch,
            ),
            out_shape=out_shape,
            input_output_aliases={k + 1: v for k, v in aliases.items()},
            compiler_params=pltpu.CompilerParams(vmem_limit_bytes=VMEM_LIMIT),
        )(scalars, *args)

    def exchange(x, axis):
        return lax.all_to_all(x, axis, 0, 0, tiled=True)

    f32 = jnp.float32
    pending = []
    recv = None
    outputs = []
    cuts = [bases[h] for h in CUTS]
    rows = pl.BlockSpec((6, 32, 512), lambda *_: (0, 0, 0))

    def block(*lead):
        def spec(n, slot):
            return pl.BlockSpec((1, 1) + (n,) * len(lead) + (32, 512), lambda *_: (slot, 0) + lead + (0, 0))

        return spec

    spans = list(zip(cuts[:-1], cuts[1:]))
    top, *wholes = call(
        pack_kernel,
        [],
        (1,),
        [block()(0, 16), block()(0, 17), block()(0, 18), block(0)(2, 16), block(0)(1, 17)]
        + [pl.BlockSpec((hi - lo, 1, 32, 512), lambda *_, i=lo // (hi - lo): (i, 0, 0, 0)) for lo, hi in spans],
        [rows] + [pl.BlockSpec((hi - lo, 32, 512), lambda *_: (0, 0, 0)) for lo, hi in spans],
        [jax.ShapeDtypeStruct((6, 32, 512), f32)]
        + [jax.ShapeDtypeStruct((hi - lo, 32, 512), f32) for lo, hi in spans],
        {},
        *[inverse_rows] * 3,
        *[panels] * 2,
        *[inverse_rows] * len(spans),
    )
    inverses = [(lo, lax.all_gather(part, "prow", axis=0)) for lo, part in zip(cuts[:-1], wholes)]
    for height in range(TOP):
        count = slot_counts[height]
        base = bases[height]
        reach = LEVELS - 1 - height
        info = (height, count, base)
        whole = height >= GATHER_FROM
        piece = jax.ShapeDtypeStruct((16, count, 16, 128), f32)
        own = jax.ShapeDtypeStruct((count, 16, 128), f32)
        every = pl.BlockSpec((16, count, 16, 128), lambda *_: (0, 0, 0, 0))
        every_own = pl.BlockSpec((count, 16, 128), lambda *_: (0, 0, 0))
        one = pl.BlockSpec((16, 1, 16, 128), lambda s, *_: (0, s, 0, 0))
        rhs_all = pl.BlockSpec((count, 16, 128), lambda *_, b=base // count: (b, 0, 0))
        if whole:
            z = call(
                functools.partial(residue_kernel, *info), [], (1,), [every, rhs_all], every, piece, {}, recv, rhs
            )
            gathered = exchange(z, "prow")
        else:
            in_specs = [
                pl.BlockSpec((1, 16, 128), lambda s, *_, b=base: (b + s, 0, 0)),
                pl.BlockSpec((1, 1, 32, 512), lambda s, *_, b=base: (b + s, 0, 0, 0)),
            ]
            args = [rhs, inverse_rows]
            if height > 0:
                in_specs, args = [one] + in_specs, [recv] + args
            parts = call(functools.partial(partial_kernel, *info), SCRATCH, (count,), in_specs, one, piece, {}, *args)
            parts = exchange(parts, "prow")
            if height == 0:
                top, parts = lax.optimization_barrier((top, parts))
                top = lax.all_gather(top, "pcol", axis=0)
            y, sol = call(
                functools.partial(solved_kernel, *info), [], (1,), [every], [every, every_own], [piece, own], {}, parts
            )
            outputs.append(sol)
            gathered = exchange(y, "prow")
        in_specs, args = [one], [gathered]
        out_specs, out_shape = [], []
        if whole:
            lo, inverse = [pair for pair in inverses if pair[0] <= base][-1]
            in_specs.append(pl.BlockSpec((16, 1, 32, 512), lambda s, *_, b=base - lo: (0, b + s, 0, 0)))
            args.append(inverse)
            out_specs.append(pl.BlockSpec((1, 16, 128), lambda s, *_: (s, 0, 0)))
            out_shape.append(own)
        if reach:
            in_specs.append(
                pl.BlockSpec((1, 1, reach, 32, 512), lambda s, *_, b=base: (b + s, 0, 0, 0, 0))
            )
            args.append(panels)
        aliases = {}
        for d in range(reach):
            shape = (16 * slot_counts[height + 1 + d], 16, 128)
            spec = pl.BlockSpec(shape, lambda *_: (0, 0, 0))
            if height > 0:
                aliases[len(in_specs)] = len(out_specs)
                in_specs.append(spec)
                args.append(pending[d])
            out_specs.append(spec)
            out_shape.append(jax.ShapeDtypeStruct(shape, f32))
        results = call(
            functools.partial(spread_kernel, *info, whole), SCRATCH, (count,), in_specs, out_specs, out_shape, aliases, *args
        )
        results = list(results)
        if whole:
            outputs.append(results.pop(0))
        if height + 1 < TOP:
            following = slot_counts[height + 1]
            recv = exchange(results[0].reshape(16, following, 16, 128), "pcol")
            pending = results[1:]
        if height == 1:
            top, recv = lax.optimization_barrier((top, recv))
            halves = [(4, 3, 0, 1), (2, 2, 0, 0), (1, 1, 0, 2)]
            chosen = call(
                choose_kernel,
                [],
                (1,),
                [
                    pl.BlockSpec((m, n, 32, 256), lambda _, info, a=a, b=b: (a, b, 0, info[1] % 2))
                    for m, n, a, b in halves
                ],
                pl.BlockSpec((17, 32, 256), lambda *_: (0, 0, 0)),
                jax.ShapeDtypeStruct((17, 32, 256), f32),
                {},
                *[top] * 3,
            )
            top = lax.all_gather(chosen, "prow", axis=0)
    many = pl.BlockSpec((16, 16, 128), lambda *_: (0, 0, 0))
    sides = pl.BlockSpec((16, 8, 256), lambda *_: (0, 0, 0))
    sides_shape = jax.ShapeDtypeStruct((16, 8, 256), f32)
    turned = call(
        turn_kernel,
        SCRATCH,
        (1,),
        [many] * 3 + [pl.BlockSpec((19, 16, 128), lambda *_: (0, 0, 0))],
        sides,
        sides_shape,
        {},
        *results,
        rhs,
    )
    total = call(sum_kernel, [], (1,), [sides], sides, sides_shape, {}, exchange(turned, "pcol"))
    gathered = exchange(total, "prow")
    def halves_from(start):
        return pl.BlockSpec((16, 1, 32, 256), lambda s, *_: (0, start + s, 0, 0))

    def whole_of(*shape):
        return pl.BlockSpec(shape, lambda *_: (0,) * len(shape)), jax.ShapeDtypeStruct(shape, f32)

    def other_core(x):
        return lax.ppermute(x, "pcol", [(i, i ^ 1) for i in range(16)])

    found, found_shape = whole_of(16, 8, 128)
    three, three_shape = whole_of(3, 8, 512)
    single, single_shape = whole_of(8, 512)
    half_y = pltpu.VMEM((8, 256), f32)
    solved, left = call(
        low_kernel,
        [pltpu.VMEM((4, 8, 512), f32), half_y],
        (12,),
        [sides, halves_from(0)],
        [found, three],
        [found_shape, three_shape],
        {},
        gathered,
        top,
    )
    solved, left = call(
        middle_kernel,
        [half_y],
        (4,),
        [three, three, found, halves_from(12)],
        [found, single],
        [found_shape, single_shape],
        {},
        left,
        other_core(left),
        solved,
        top,
    )
    solved = call(
        root_kernel,
        [],
        (1,),
        [single, single, found, halves_from(16)],
        found,
        found_shape,
        {},
        left,
        other_core(left),
        solved,
        top,
    )
    outputs.append(
        call(
            last_kernel,
            SCRATCH,
            (1,),
            [pl.BlockSpec((16, 8, 128), lambda *_: (0, 0, 0))],
            pl.BlockSpec((3, 16, 128), lambda *_: (0, 0, 0)),
            jax.ShapeDtypeStruct((3, 16, 128), f32),
            {},
            exchange(solved, "pcol"),
        )
    )
    return jnp.concatenate(outputs, 0).reshape(19, 1, 2048)


def solution(mesh):
    in_specs = (
        P(None, "pcol", "prow"),
        P(None, "pcol", "prow", None),
        P(None, "pcol", None, "prow", None),
        P(None, "pcol", None),
        P(None, "pcol"),
        P(),
    )
    out_specs = P(None, "pcol", "prow")
    return jax.shard_map(
        on_device, mesh=mesh, in_specs=in_specs, out_specs=out_specs, check_vma=False
    )
```

```python
import functools

import jax
import jax.numpy as jnp
from jax import lax
from jax.experimental import pallas as pl
from jax.experimental.pallas import tpu as pltpu
from jax.sharding import PartitionSpec as P

LEVELS = 8
LEAVES = 128
GATHER_FROM = 2
CUTS = (2, 5)
SCRATCH = [pltpu.VMEM((192, 512), jnp.float32)]
TOP = 5
VMEM_LIMIT = 24 * 1024 * 1024

NODES = [LEAVES >> h for h in range(LEVELS)]
NODE_BASE = [2 * LEAVES - 2 * (LEAVES >> h) for h in range(LEVELS)]


class Part:
    def __init__(self, ref, start):
        self.ref, self.start = ref, start

    def __getitem__(self, index):
        return self.ref[index + self.start]


def with_parts(kernel, *refs):
    return kernel(*[Part(refs[0], start) for start in (0, 2, 256, 389)], *refs[1:])


def split(x):
    high = x.astype(jnp.bfloat16)
    low = (x - high.astype(jnp.float32)).astype(jnp.bfloat16)
    return high, low


def dot3(a, b, dims):
    bh, bl = split(b)
    n = a.shape[0]
    if n <= 64 and dims[0] == (1,):
        high = a.astype(jnp.bfloat16).astype(jnp.float32)
        both = jnp.concatenate([high, a - high], 0).astype(jnp.bfloat16)
        dot = functools.partial(
            lax.dot_general, dimension_numbers=(dims, ((), ())), preferred_element_type=jnp.float32
        )
        first = dot(both, bh)
        second = dot(high.astype(jnp.bfloat16), bl)
        return first[:n] + (first[n:] + second)
    ah, al = split(a)
    dot = functools.partial(
        lax.dot_general, dimension_numbers=(dims, ((), ())), preferred_element_type=jnp.float32
    )
    return dot(ah, bh) + (dot(ah, bl) + dot(al, bh))


def lower(shape):
    return lax.broadcasted_iota(jnp.int32, shape, len(shape) - 1) < 64


def from_own_order(x, scratch):
    n = x.shape[0]
    x = x.reshape(n * 16, 128)
    scratch[pl.ds(0, n * 16, stride=2), :] = x
    scratch[pl.ds(1, n * 16, stride=2), :] = pltpu.roll(x, 64, 1)
    rows = scratch[pl.ds(0, n * 32), :].reshape(n, 2, 16, 128)
    other = pltpu.roll(rows[:, 1].reshape(n * 16, 128), 64, 1).reshape(n, 16, 128)
    return jnp.where(lower((n, 16, 128)), rows[:, 0], other)


def to_own_order(x, scratch):
    n = x.shape[0]
    turned = pltpu.roll(x.reshape(n * 16, 128), 64, 1).reshape(n, 1, 16, 128)
    scratch[pl.ds(0, n * 32), :] = jnp.concatenate([x.reshape(n, 1, 16, 128), turned], 1).reshape(n * 32, 128)
    even = scratch[pl.ds(0, n * 16, stride=2), :]
    odd = pltpu.roll(scratch[pl.ds(1, n * 16, stride=2), :], 64, 1)
    return jnp.where(lower((n * 16, 128)), even, odd).reshape(n, 16, 128)


def fold(x):
    n = x.shape[0] // 32
    x = x.reshape(n, 2, 16, 128)
    return jnp.where(lower((n, 16, 128)), x[:, 0], x[:, 1])


def own_mask(pos, sizes, slot, local, nodes):
    row = lax.broadcasted_iota(jnp.int32, (16, 128), 0)
    lane = lax.broadcasted_iota(jnp.int32, (16, 128), 1)
    row_id = pos[0] * 32 + row + 16 * (lane >= 64).astype(jnp.int32)
    limit = jnp.where(local * 16 + pos[1] < nodes, sizes[slot], 0)
    return row_id < limit


def residue_kernel(height, slots, slot_base, pos, parent, pattern, sizes, recv, rhs, out):
    for s in range(slots):
        total = recv[0, s]
        for i in range(1, 16):
            total = total + recv[i, s]
        keep = own_mask(pos, sizes, slot_base + s, s, NODES[height])
        z = jnp.where(keep, rhs[s] - total, 0.0)
        for i in range(16):
            out[i, s] = z


def partial_kernel(height, slots, slot_base, pos, parent, pattern, sizes, *refs):
    recv = None
    if height > 0:
        recv, *refs = refs
    rhs, inverse, out = refs
    s = pl.program_id(0)
    z = rhs[0]
    if recv is not None:
        total = recv[0, 0]
        for i in range(1, 16):
            total = total + recv[i, 0]
        z = z - total
    keep = own_mask(pos, sizes, slot_base + s, s, NODES[height])
    z = jnp.where(keep, z, 0.0)
    turned = pltpu.roll(z, 64, 1)
    low = lower((16, 128))
    twice = jnp.concatenate([jnp.where(low, z, turned), jnp.where(low, turned, z)], 0)
    out[:, 0] = fold(dot3(inverse[0, 0], twice, ((0,), (0,))))


def solved_kernel(height, slots, slot_base, pos, parent, pattern, sizes, recv, out, sol):
    for s in range(slots):
        total = recv[0, s]
        for i in range(1, 16):
            total = total + recv[i, s]
        keep = own_mask(pos, sizes, slot_base + s, s, NODES[height])
        y = jnp.where(keep, total, 0.0)
        sol[s] = y
        for i in range(16):
            out[i, s] = y


def spread_kernel(height, slots, slot_base, whole, pos, parent, pattern, sizes, *refs):
    reach = LEVELS - 1 - height
    refs = list(refs)
    gathered = refs.pop(0)
    inverse = refs.pop(0) if whole else None
    panels = refs.pop(0) if reach else None
    before = [refs.pop(0) for _ in range(reach)] if height > 0 else []
    sol = refs.pop(0) if whole else None
    after = [refs.pop(0) for _ in range(reach)]
    scratch = refs.pop(0)
    s = pl.program_id(0)

    @pl.when(s == 0)
    def _():
        for i, ref in enumerate(after):
            ref[...] = before[i][...] if before else jnp.zeros_like(ref)

    x = gathered[:, 0].reshape(256, 128)
    slot = slot_base + s
    if whole:
        turned = x.T
        z_t = jnp.concatenate([turned[:64], turned[64:]], 1)
        rows = inverse[:, 0].reshape(16, 2, 16, 512)
        rows = jnp.concatenate([rows[:, 0].reshape(256, 512), rows[:, 1].reshape(256, 512)], 0)
        y_t = dot3(z_t, rows, ((1,), (0,)))
        limit = sizes[slot]
        y_t = jnp.where(lax.broadcasted_iota(jnp.int32, (64, 512), 1) < limit, y_t, 0.0)
        scratch[pl.ds(0, 64), :] = y_t
        lanes = scratch[pl.ds(0, 64), pl.ds(pl.multiple_of(pos[0] // 4 * 128, 128), 128)]
        own = jnp.concatenate([lanes, lanes], 0).T
        scratch[pl.ds(64, 128), pl.ds(0, 128)] = own
        own = scratch[pl.ds(pl.multiple_of(64 + pos[0] % 4 * 32, 32), 32), pl.ds(0, 128)]
        sol[...] = fold(own)
    else:
        turned = pltpu.roll(x, 64, 1).reshape(16, 1, 16, 128)
        y_t = jnp.concatenate([x.reshape(16, 1, 16, 128), turned], 1).reshape(512, 128).T[:64]
    if reach:
        block = panels[0, 0].reshape(reach * 32, 512)
        update = fold(dot3(block, jnp.concatenate([y_t, y_t], 0), ((1,), (1,))))
        node = NODE_BASE[height] + jnp.minimum(s * 16 + pos[1], NODES[height] - 1)
        for d in range(reach):
            node = parent[node]
            target = height + 1 + d
            j = node - NODE_BASE[target]
            where = (j % 16) * max(1, NODES[target] // 16) + j // 16
            scale = pattern[slot * 7 + d].astype(jnp.float32)
            after[d][where] += scale * update[d]


def pack_kernel(pos, parent, pattern, sizes, sides, inv5, inv6, inv7, panel5, panel6, *refs):
    *refs, scratch = refs
    half = len(refs) // 2 - 1
    folded, out = refs[half : half + 2]
    folded[...] = from_own_order(sides[...], scratch)
    for source, target in zip(refs[:half], refs[half + 2 :]):
        target[...] = source[:, 0]
    for level, inv, panel, at in ((0, inv5, panel5, 3), (1, inv6, panel6, 0), (2, inv7, None, 2)):
        slot = 16 + level
        size = sizes[slot]
        row = pos[0] * 32 + lax.broadcasted_iota(jnp.int32, (32, 512), 0)
        column = lax.broadcasted_iota(jnp.int32, (32, 512), 1)
        out[at] = jnp.where((row < size) & (column < size), inv[0, 0], 0.0)
        for d in range(2 - level):
            out[at + 1 + d] = panel[0, 0, d] * pattern[slot * 7 + d].astype(jnp.float32)


def choose_kernel(pos, parent, pattern, sizes, low, middle, high, out):
    for c in range(4):
        out[3 * c : 3 * c + 3] = low[c]
    for c in range(2):
        out[12 + 2 * c : 14 + 2 * c] = middle[c]
    out[16:17] = high[0]


def turn_kernel(pos, parent, pattern, sizes, p5, p6, p7, rhs, out, scratch):
    at = 0
    for level, ref in enumerate((p5, p6, p7)):
        for j in range(4 >> level):
            piece = ref[j] - jnp.where(pos[1] == j, rhs[16 + level], 0.0)
            scratch[pl.ds(at * 32, 16), :] = piece
            scratch[pl.ds(at * 32 + 16, 16), :] = pltpu.roll(piece, 64, 1)
            at += 1
    scratch[pl.ds(224, 32), :] = jnp.zeros((32, 128), jnp.float32)
    turned = scratch[pl.ds(0, 256), :].T
    for z in range(8):
        out[2 * z] = turned[8 * z : 8 * z + 8]
        out[2 * z + 1] = turned[8 * z : 8 * z + 8]


def sum_kernel(pos, parent, pattern, sizes, recv, out):
    total = recv[0]
    for i in range(1, 16):
        total = total + recv[i]
    for i in range(16):
        out[i] = total


def place(own, y, level, pos):
    lanes = pltpu.roll(y, (256 - (pos[0] % 8) * 32) % 256, 1)[:, :128]
    lane = lax.broadcasted_iota(jnp.int32, (8, 128), 1) // 32
    return jnp.where(lane == level, pltpu.roll(lanes, level * 32, 1), own)


def low_kernel(pos, parent, pattern, sizes, recv, block, out, left, z):
    step = pl.program_id(0)

    @pl.when(step == 0)
    def _():
        lane = lax.broadcasted_iota(jnp.int32, (8, 128), 1) // 32
        for n in range(7):
            for g in range(4):
                whole = jnp.zeros((8, 128), jnp.float32)
                for i in range(4):
                    piece = recv[4 * g + i][:, (n // 4) * 128 : (n // 4 + 1) * 128]
                    turned = pltpu.roll(piece, ((i - n % 4) * 32) % 128, 1)
                    whole = jnp.where(lane == i, turned, whole)
                if n < 4:
                    z[n, :, g * 128 : (g + 1) * 128] = -whole
                else:
                    left[n - 4, :, g * 128 : (g + 1) * 128] = jnp.where(pos[1] % 2 == 0, -whole, 0.0)
        out[...] = jnp.zeros_like(out)

    solved = dot3(z[step], block[:, 0].reshape(512, 256), ((1,), (0,)))
    out[step] = place(out[step], solved, 0, pos)
    target = parent[NODE_BASE[TOP] + step] - NODE_BASE[TOP + 1]
    left[target] = left[target] - dot3(solved, block[:, 1].reshape(512, 256), ((1,), (1,)))
    left[2] = left[2] - dot3(solved, block[:, 2].reshape(512, 256), ((1,), (1,)))


def middle_kernel(pos, parent, pattern, sizes, left, other, before, block, out, after):
    step = pl.program_id(0)

    @pl.when(step == 0)
    def _():
        out[...] = before[...]
        after[...] = left[2]

    solved = dot3(left[step] + other[step], block[:, 0].reshape(512, 256), ((1,), (0,)))
    out[step] = place(out[step], solved, 1, pos)
    after[...] = after[...] - dot3(solved, block[:, 1].reshape(512, 256), ((1,), (1,)))


def root_kernel(pos, parent, pattern, sizes, left, other, before, block, out):
    solved = dot3(left[...] + other[...], block[:, 0].reshape(512, 256), ((1,), (0,)))
    out[...] = before[...]
    out[0] = place(before[0], solved, 2, pos)


def last_kernel(pos, parent, pattern, sizes, recv, *refs):
    *parts, out, scratch = refs
    columns = jnp.concatenate([recv[2 * i + pos[0] // 8] for i in range(8)], 0)
    turned = jnp.concatenate([columns, columns], 0).T
    parts = [ref[...] for ref in parts] + [fold(turned[:96])]
    out[...] = to_own_order(jnp.concatenate(parts, 0), scratch)


def on_device(right_side, inverse_rows, panels, pattern, node_sizes, parent):
    pos = jnp.stack([lax.axis_index("prow"), lax.axis_index("pcol")]).astype(jnp.int32)
    rhs = right_side.reshape(19, 16, 128)
    scalars = jnp.concatenate([pos, parent, pattern.reshape(-1), node_sizes.reshape(-1)])
    slot_counts = [max(1, n // 16) for n in NODES]
    bases = [sum(slot_counts[:h]) for h in range(LEVELS)]
    def call(kernel, scratch, grid, in_specs, out_specs, out_shape, aliases, *args):
        args = [pltpu.with_memory_space_constraint(a, pltpu.HBM) if a.size > 1 << 18 else a for a in args]
        return pl.pallas_call(
            functools.partial(with_parts, kernel),
            grid_spec=pltpu.PrefetchScalarGridSpec(
                num_scalar_prefetch=1,
                grid=grid,
                in_specs=in_specs,
                out_specs=out_specs,
                scratch_shapes=scratch,
            ),
            out_shape=out_shape,
            input_output_aliases={k + 1: v for k, v in aliases.items()},
            compiler_params=pltpu.CompilerParams(vmem_limit_bytes=VMEM_LIMIT),
        )(scalars, *args)

    def exchange(x, axis):
        return lax.all_to_all(x, axis, 0, 0, tiled=True)

    f32 = jnp.float32
    pending = []
    recv = None
    outputs = []
    cuts = [bases[h] for h in CUTS]
    rows = pl.BlockSpec((6, 32, 512), lambda *_: (0, 0, 0))

    def block(*lead):
        def spec(n, slot):
            return pl.BlockSpec((1, 1) + (n,) * len(lead) + (32, 512), lambda *_: (slot, 0) + lead + (0, 0))

        return spec

    spans = list(zip(cuts[:-1], cuts[1:]))
    all_sides = pl.BlockSpec((19, 16, 128), lambda *_: (0, 0, 0))
    tall = [pltpu.VMEM((19 * 32, 128), f32)]
    rhs, top, *wholes = call(
        pack_kernel,
        tall,
        (1,),
        [all_sides, block()(0, 16), block()(0, 17), block()(0, 18), block(0)(2, 16), block(0)(1, 17)]
        + [pl.BlockSpec((hi - lo, 1, 32, 512), lambda *_, i=lo // (hi - lo): (i, 0, 0, 0)) for lo, hi in spans],
        [all_sides, rows] + [pl.BlockSpec((hi - lo, 32, 512), lambda *_: (0, 0, 0)) for lo, hi in spans],
        [jax.ShapeDtypeStruct((19, 16, 128), f32), jax.ShapeDtypeStruct((6, 32, 512), f32)]
        + [jax.ShapeDtypeStruct((hi - lo, 32, 512), f32) for lo, hi in spans],
        {},
        rhs,
        *[inverse_rows] * 3,
        *[panels] * 2,
        *[inverse_rows] * len(spans),
    )
    top = lax.all_gather(top, "pcol", axis=0)
    for height in range(TOP):
        count = slot_counts[height]
        base = bases[height]
        reach = LEVELS - 1 - height
        info = (height, count, base)
        whole = height >= GATHER_FROM
        piece = jax.ShapeDtypeStruct((16, count, 16, 128), f32)
        own = jax.ShapeDtypeStruct((count, 16, 128), f32)
        every = pl.BlockSpec((16, count, 16, 128), lambda *_: (0, 0, 0, 0))
        every_own = pl.BlockSpec((count, 16, 128), lambda *_: (0, 0, 0))
        one = pl.BlockSpec((16, 1, 16, 128), lambda s, *_: (0, s, 0, 0))
        rhs_all = pl.BlockSpec((count, 16, 128), lambda *_, b=base // count: (b, 0, 0))
        if whole:
            z = call(
                functools.partial(residue_kernel, *info), [], (1,), [every, rhs_all], every, piece, {}, recv, rhs
            )
            gathered = exchange(z, "prow")
        else:
            in_specs = [
                pl.BlockSpec((1, 16, 128), lambda s, *_, b=base: (b + s, 0, 0)),
                pl.BlockSpec((1, 1, 32, 512), lambda s, *_, b=base: (b + s, 0, 0, 0)),
            ]
            args = [rhs, inverse_rows]
            if height > 0:
                in_specs, args = [one] + in_specs, [recv] + args
            parts = call(functools.partial(partial_kernel, *info), [], (count,), in_specs, one, piece, {}, *args)
            parts = exchange(parts, "prow")
            if height == 0:
                wholes, parts = lax.optimization_barrier((wholes, parts))
                inverses = [(lo, lax.all_gather(part, "prow", axis=0)) for lo, part in zip(cuts[:-1], wholes)]
            y, sol = call(
                functools.partial(solved_kernel, *info), [], (1,), [every], [every, every_own], [piece, own], {}, parts
            )
            outputs.append(sol)
            gathered = exchange(y, "prow")
        in_specs, args = [one], [gathered]
        out_specs, out_shape = [], []
        if whole:
            lo, inverse = [pair for pair in inverses if pair[0] <= base][-1]
            in_specs.append(pl.BlockSpec((16, 1, 32, 512), lambda s, *_, b=base - lo: (0, b + s, 0, 0)))
            args.append(inverse)
            out_specs.append(pl.BlockSpec((1, 16, 128), lambda s, *_: (s, 0, 0)))
            out_shape.append(own)
        if reach:
            in_specs.append(
                pl.BlockSpec((1, 1, reach, 32, 512), lambda s, *_, b=base: (b + s, 0, 0, 0, 0))
            )
            args.append(panels)
        aliases = {}
        for d in range(reach):
            shape = (16 * slot_counts[height + 1 + d], 16, 128)
            spec = pl.BlockSpec(shape, lambda *_: (0, 0, 0))
            if height > 0:
                aliases[len(in_specs)] = len(out_specs)
                in_specs.append(spec)
                args.append(pending[d])
            out_specs.append(spec)
            out_shape.append(jax.ShapeDtypeStruct(shape, f32))
        results = call(
            functools.partial(spread_kernel, *info, whole), SCRATCH, (count,), in_specs, out_specs, out_shape, aliases, *args
        )
        results = list(results)
        if whole:
            outputs.append(results.pop(0))
        if height + 1 < TOP:
            following = slot_counts[height + 1]
            recv = exchange(results[0].reshape(16, following, 16, 128), "pcol")
            pending = results[1:]
        if height == 1:
            top, recv = lax.optimization_barrier((top, recv))
            halves = [(4, 3, 0, 1), (2, 2, 0, 0), (1, 1, 0, 2)]
            chosen = call(
                choose_kernel,
                [],
                (1,),
                [
                    pl.BlockSpec((m, n, 32, 256), lambda _, info, a=a, b=b: (a, b, 0, info[1] % 2))
                    for m, n, a, b in halves
                ],
                pl.BlockSpec((17, 32, 256), lambda *_: (0, 0, 0)),
                jax.ShapeDtypeStruct((17, 32, 256), f32),
                {},
                *[top] * 3,
            )
            top = lax.all_gather(chosen, "prow", axis=0)
    many = pl.BlockSpec((16, 16, 128), lambda *_: (0, 0, 0))
    sides = pl.BlockSpec((16, 8, 256), lambda *_: (0, 0, 0))
    sides_shape = jax.ShapeDtypeStruct((16, 8, 256), f32)
    turned = call(
        turn_kernel,
        [pltpu.VMEM((256, 128), f32)],
        (1,),
        [many] * 3 + [pl.BlockSpec((19, 16, 128), lambda *_: (0, 0, 0))],
        sides,
        sides_shape,
        {},
        *results,
        rhs,
    )
    total = call(sum_kernel, [], (1,), [sides], sides, sides_shape, {}, exchange(turned, "pcol"))
    gathered = exchange(total, "prow")
    def halves_from(start, n):
        return pl.BlockSpec((16, n, 32, 256), lambda s, *_: (0, start // n + s, 0, 0))

    def whole_of(*shape):
        return pl.BlockSpec(shape, lambda *_: (0,) * len(shape)), jax.ShapeDtypeStruct(shape, f32)

    def other_core(x):
        return lax.ppermute(x, "pcol", [(i, i ^ 1) for i in range(16)])

    found, found_shape = whole_of(16, 8, 128)
    three, three_shape = whole_of(3, 8, 512)
    single, single_shape = whole_of(8, 512)
    solved, left = call(
        low_kernel,
        [pltpu.VMEM((4, 8, 512), f32)],
        (4,),
        [sides, halves_from(0, 3)],
        [found, three],
        [found_shape, three_shape],
        {},
        gathered,
        top,
    )
    solved, left = call(
        middle_kernel,
        [],
        (2,),
        [three, three, found, halves_from(12, 2)],
        [found, single],
        [found_shape, single_shape],
        {},
        left,
        other_core(left),
        solved,
        top,
    )
    solved = call(
        root_kernel,
        [],
        (1,),
        [single, single, found, halves_from(16, 1)],
        found,
        found_shape,
        {},
        left,
        other_core(left),
        solved,
        top,
    )
    out = call(
        last_kernel,
        tall,
        (1,),
        [found] + [pl.BlockSpec(x.shape, lambda *_: (0, 0, 0)) for x in outputs],
        all_sides,
        jax.ShapeDtypeStruct((19, 16, 128), f32),
        {},
        exchange(solved, "pcol"),
        *outputs,
    )
    return out.reshape(19, 1, 2048)


def solution(mesh):
    in_specs = (
        P(None, "pcol", "prow"),
        P(None, "pcol", "prow", None),
        P(None, "pcol", None, "prow", None),
        P(None, "pcol", None),
        P(None, "pcol"),
        P(),
    )
    out_specs = P(None, "pcol", "prow")
    return jax.shard_map(
        on_device, mesh=mesh, in_specs=in_specs, out_specs=out_specs, check_vma=False
    )
```

```python
import functools

import jax
import jax.numpy as jnp
from jax import lax
from jax.experimental import pallas as pl
from jax.experimental.pallas import tpu as pltpu
from jax.sharding import PartitionSpec as P

LEVELS = 8
LEAVES = 128
GATHER_FROM = 2
CUTS = (2, 5)
SCRATCH = [pltpu.VMEM((192, 512), jnp.float32)]
TOP = 5
VMEM_LIMIT = 24 * 1024 * 1024

NODES = [LEAVES >> h for h in range(LEVELS)]
NODE_BASE = [2 * LEAVES - 2 * (LEAVES >> h) for h in range(LEVELS)]


class Part:
    def __init__(self, ref, start):
        self.ref, self.start = ref, start

    def __getitem__(self, index):
        return self.ref[index + self.start]


def with_parts(kernel, *refs):
    return kernel(*[Part(refs[0], start) for start in (0, 2, 256, 389)], *refs[1:])


def split(x):
    high = x.astype(jnp.bfloat16)
    low = (x - high.astype(jnp.float32)).astype(jnp.bfloat16)
    return high, low


def dot3(a, b, dims):
    bh, bl = split(b)
    n = a.shape[0]
    if n <= 64 and dims[0] == (1,):
        high = a.astype(jnp.bfloat16).astype(jnp.float32)
        both = jnp.concatenate([high, a - high], 0).astype(jnp.bfloat16)
        dot = functools.partial(
            lax.dot_general, dimension_numbers=(dims, ((), ())), preferred_element_type=jnp.float32
        )
        first = dot(both, bh)
        second = dot(high.astype(jnp.bfloat16), bl)
        return first[:n] + (first[n:] + second)
    ah, al = split(a)
    dot = functools.partial(
        lax.dot_general, dimension_numbers=(dims, ((), ())), preferred_element_type=jnp.float32
    )
    return dot(ah, bh) + (dot(ah, bl) + dot(al, bh))


def lower(shape):
    return lax.broadcasted_iota(jnp.int32, shape, len(shape) - 1) < 64


def from_own_order(x, scratch):
    n = x.shape[0]
    x = x.reshape(n * 16, 128)
    scratch[pl.ds(0, n * 16, stride=2), :] = x
    scratch[pl.ds(1, n * 16, stride=2), :] = pltpu.roll(x, 64, 1)
    rows = scratch[pl.ds(0, n * 32), :].reshape(n, 2, 16, 128)
    other = pltpu.roll(rows[:, 1].reshape(n * 16, 128), 64, 1).reshape(n, 16, 128)
    return jnp.where(lower((n, 16, 128)), rows[:, 0], other)


def to_own_order(x, scratch):
    n = x.shape[0]
    turned = pltpu.roll(x.reshape(n * 16, 128), 64, 1).reshape(n, 1, 16, 128)
    scratch[pl.ds(0, n * 32), :] = jnp.concatenate([x.reshape(n, 1, 16, 128), turned], 1).reshape(n * 32, 128)
    even = scratch[pl.ds(0, n * 16, stride=2), :]
    odd = pltpu.roll(scratch[pl.ds(1, n * 16, stride=2), :], 64, 1)
    return jnp.where(lower((n * 16, 128)), even, odd).reshape(n, 16, 128)


def fold(x):
    n = x.shape[0] // 32
    x = x.reshape(n, 2, 16, 128)
    return jnp.where(lower((n, 16, 128)), x[:, 0], x[:, 1])


def own_mask(pos, sizes, slot, local, nodes):
    row = lax.broadcasted_iota(jnp.int32, (16, 128), 0)
    lane = lax.broadcasted_iota(jnp.int32, (16, 128), 1)
    row_id = pos[0] * 32 + row + 16 * (lane >= 64).astype(jnp.int32)
    limit = jnp.where(local * 16 + pos[1] < nodes, sizes[slot], 0)
    return row_id < limit


def residue_kernel(height, slots, slot_base, pos, parent, pattern, sizes, recv, rhs, out):
    for s in range(slots):
        total = recv[0, s]
        for i in range(1, 16):
            total = total + recv[i, s]
        keep = own_mask(pos, sizes, slot_base + s, s, NODES[height])
        z = jnp.where(keep, rhs[s] - total, 0.0)
        for i in range(16):
            out[i, s] = z


def partial_kernel(height, slots, slot_base, pos, parent, pattern, sizes, *refs):
    recv = None
    if height > 0:
        recv, *refs = refs
    rhs, inverse, out = refs
    low = lower((16, 128))
    for i in range(rhs.shape[0]):
        s = pl.program_id(0) * rhs.shape[0] + i
        z = rhs[i]
        if recv is not None:
            total = recv[0, i]
            for k in range(1, recv.shape[0]):
                total = total + recv[k, i]
            z = z - total
        keep = own_mask(pos, sizes, slot_base + s, s, NODES[height])
        z = jnp.where(keep, z, 0.0)
        turned = pltpu.roll(z, 64, 1)
        twice = jnp.concatenate([jnp.where(low, z, turned), jnp.where(low, turned, z)], 0)
        out[:, i] = fold(dot3(inverse[i, 0], twice, ((0,), (0,))))


def solved_kernel(height, slots, slot_base, pos, parent, pattern, sizes, recv, out, sol):
    for s in range(slots):
        total = recv[0, s]
        for i in range(1, 16):
            total = total + recv[i, s]
        keep = own_mask(pos, sizes, slot_base + s, s, NODES[height])
        y = jnp.where(keep, total, 0.0)
        sol[s] = y
        for i in range(16):
            out[i, s] = y


def spread_kernel(height, slots, slot_base, source, first, end, pos, parent, pattern, sizes, *refs):
    refs = list(refs)
    given = refs.pop(0)
    inverse = refs.pop(0) if source == "z" else None
    panels = refs.pop(0)
    before = [refs.pop(0) for _ in range(first, end)] if height > 0 else []
    sol = refs.pop(0) if source == "z" else None
    kept = refs.pop(0) if source == "z" and end < LEVELS - 1 - height else None
    after = [refs.pop(0) for _ in range(first, end)]
    scratch = refs.pop(0)

    @pl.when(pl.program_id(0) == 0)
    def _():
        for i, ref in enumerate(after):
            ref[...] = before[i][...] if before else jnp.zeros_like(ref)

    for k in range(panels.shape[0]):
        s = pl.program_id(0) * panels.shape[0] + k
        slot = slot_base + s
        if source == "z":
            turned = given[:, k].reshape(256, 128).T
            z_t = jnp.concatenate([turned[:64], turned[64:]], 1)
            rows = inverse[:, k].reshape(16, 2, 16, 512)
            rows = jnp.concatenate([rows[:, 0].reshape(256, 512), rows[:, 1].reshape(256, 512)], 0)
            y_t = dot3(z_t, rows, ((1,), (0,)))
            limit = sizes[slot]
            y_t = jnp.where(lax.broadcasted_iota(jnp.int32, (64, 512), 1) < limit, y_t, 0.0)
            scratch[pl.ds(0, 64), :] = y_t
            lanes = scratch[pl.ds(0, 64), pl.ds(pl.multiple_of(pos[0] // 4 * 128, 128), 128)]
            own = jnp.concatenate([lanes, lanes], 0).T
            scratch[pl.ds(64, 128), pl.ds(0, 128)] = own
            own = scratch[pl.ds(pl.multiple_of(64 + pos[0] % 4 * 32, 32), 32), pl.ds(0, 128)]
            sol[k] = fold(own)[0]
            if kept is not None:
                kept[k] = y_t
        elif source == "y":
            x = given[:, k].reshape(256, 128)
            turned = pltpu.roll(x, 64, 1).reshape(16, 1, 16, 128)
            y_t = jnp.concatenate([x.reshape(16, 1, 16, 128), turned], 1).reshape(512, 128).T[:64]
        else:
            y_t = given[k]
        block = panels[k, 0, first:end].reshape((end - first) * 32, 512)
        update = fold(dot3(block, jnp.concatenate([y_t, y_t], 0), ((1,), (1,))))
        node = NODE_BASE[height] + jnp.minimum(s * 16 + pos[1], NODES[height] - 1)
        for d in range(end):
            node = parent[node]
            if d < first:
                continue
            target = height + 1 + d
            j = node - NODE_BASE[target]
            if target == 1:
                where = ((j + pos[1]) % 2 * 8 + j % 16 // 2) * 4 + j // 16
            else:
                where = (j % 16) * max(1, NODES[target] // 16) + j // 16
            scale = pattern[slot * 7 + d].astype(jnp.float32)
            after[d - first][where] += scale * update[d - first]


def join_kernel(pos, parent, pattern, sizes, here, there, out):
    out[...] = (here[...] + there[...]).reshape(out.shape)


def pack_kernel(pos, parent, pattern, sizes, sides, inv5, inv6, inv7, panel5, panel6, *refs):
    *refs, scratch = refs
    half = len(refs) // 2 - 1
    folded, out = refs[half : half + 2]
    folded[...] = from_own_order(sides[...], scratch)
    for source, target in zip(refs[:half], refs[half + 2 :]):
        target[...] = source[:, 0]
    for level, inv, panel, at in ((0, inv5, panel5, 3), (1, inv6, panel6, 0), (2, inv7, None, 2)):
        slot = 16 + level
        size = sizes[slot]
        row = pos[0] * 32 + lax.broadcasted_iota(jnp.int32, (32, 512), 0)
        column = lax.broadcasted_iota(jnp.int32, (32, 512), 1)
        out[at] = jnp.where((row < size) & (column < size), inv[0, 0], 0.0)
        for d in range(2 - level):
            out[at + 1 + d] = panel[0, 0, d] * pattern[slot * 7 + d].astype(jnp.float32)


def choose_kernel(pos, parent, pattern, sizes, low, middle, high, out):
    for c in range(4):
        out[3 * c : 3 * c + 3] = low[c]
    for c in range(2):
        out[12 + 2 * c : 14 + 2 * c] = middle[c]
    out[16:17] = high[0]


def turn_kernel(pos, parent, pattern, sizes, p5, p6, p7, rhs, out, scratch):
    at = 0
    for level, ref in enumerate((p5, p6, p7)):
        for j in range(4 >> level):
            piece = ref[j] - jnp.where(pos[1] == j, rhs[16 + level], 0.0)
            scratch[pl.ds(at * 32, 16), :] = piece
            scratch[pl.ds(at * 32 + 16, 16), :] = pltpu.roll(piece, 64, 1)
            at += 1
    scratch[pl.ds(224, 32), :] = jnp.zeros((32, 128), jnp.float32)
    turned = scratch[pl.ds(0, 256), :].T
    for z in range(8):
        out[2 * z] = turned[8 * z : 8 * z + 8]
        out[2 * z + 1] = turned[8 * z : 8 * z + 8]


def sum_kernel(pos, parent, pattern, sizes, recv, out):
    total = recv[0]
    for i in range(1, 16):
        total = total + recv[i]
    for i in range(16):
        out[i] = total


def place(own, y, level, pos):
    lanes = pltpu.roll(y, (256 - (pos[0] % 8) * 32) % 256, 1)[:, :128]
    lane = lax.broadcasted_iota(jnp.int32, (8, 128), 1) // 32
    return jnp.where(lane == level, pltpu.roll(lanes, level * 32, 1), own)


def low_kernel(pos, parent, pattern, sizes, recv, block, out, left, z):
    step = pl.program_id(0)

    @pl.when(step == 0)
    def _():
        lane = lax.broadcasted_iota(jnp.int32, (8, 128), 1) // 32
        for n in range(7):
            for g in range(4):
                whole = jnp.zeros((8, 128), jnp.float32)
                for i in range(4):
                    piece = recv[4 * g + i][:, (n // 4) * 128 : (n // 4 + 1) * 128]
                    turned = pltpu.roll(piece, ((i - n % 4) * 32) % 128, 1)
                    whole = jnp.where(lane == i, turned, whole)
                if n < 4:
                    z[n, :, g * 128 : (g + 1) * 128] = -whole
                else:
                    left[n - 4, :, g * 128 : (g + 1) * 128] = jnp.where(pos[1] % 2 == 0, -whole, 0.0)
        out[...] = jnp.zeros_like(out)

    solved = dot3(z[step], block[:, 0].reshape(512, 256), ((1,), (0,)))
    out[step] = place(out[step], solved, 0, pos)
    target = parent[NODE_BASE[TOP] + step] - NODE_BASE[TOP + 1]
    left[target] = left[target] - dot3(solved, block[:, 1].reshape(512, 256), ((1,), (1,)))
    left[2] = left[2] - dot3(solved, block[:, 2].reshape(512, 256), ((1,), (1,)))


def middle_kernel(pos, parent, pattern, sizes, left, other, before, block, out, after):
    step = pl.program_id(0)

    @pl.when(step == 0)
    def _():
        out[...] = before[...]
        after[...] = left[2]

    solved = dot3(left[step] + other[step], block[:, 0].reshape(512, 256), ((1,), (0,)))
    out[step] = place(out[step], solved, 1, pos)
    after[...] = after[...] - dot3(solved, block[:, 1].reshape(512, 256), ((1,), (1,)))


def root_kernel(pos, parent, pattern, sizes, left, other, before, block, out):
    solved = dot3(left[...] + other[...], block[:, 0].reshape(512, 256), ((1,), (0,)))
    out[...] = before[...]
    out[0] = place(before[0], solved, 2, pos)


def last_kernel(pos, parent, pattern, sizes, recv, *refs):
    *parts, out, scratch = refs
    columns = jnp.concatenate([recv[2 * i + pos[0] // 8] for i in range(8)], 0)
    turned = jnp.concatenate([columns, columns], 0).T
    parts = [ref[...] for ref in parts] + [fold(turned[:96])]
    out[...] = to_own_order(jnp.concatenate(parts, 0), scratch)


def on_device(right_side, inverse_rows, panels, pattern, node_sizes, parent):
    pos = jnp.stack([lax.axis_index("prow"), lax.axis_index("pcol")]).astype(jnp.int32)
    rhs = right_side.reshape(19, 16, 128)
    scalars = jnp.concatenate([pos, parent, pattern.reshape(-1), node_sizes.reshape(-1)])
    slot_counts = [max(1, n // 16) for n in NODES]
    bases = [sum(slot_counts[:h]) for h in range(LEVELS)]
    def call(kernel, scratch, grid, in_specs, out_specs, out_shape, aliases, *args):
        args = [pltpu.with_memory_space_constraint(a, pltpu.HBM) if a.size > 1 << 18 else a for a in args]
        return pl.pallas_call(
            functools.partial(with_parts, kernel),
            grid_spec=pltpu.PrefetchScalarGridSpec(
                num_scalar_prefetch=1,
                grid=grid,
                in_specs=in_specs,
                out_specs=out_specs,
                scratch_shapes=scratch,
            ),
            out_shape=out_shape,
            input_output_aliases={k + 1: v for k, v in aliases.items()},
            compiler_params=pltpu.CompilerParams(vmem_limit_bytes=VMEM_LIMIT),
        )(scalars, *args)

    def exchange(x, axis):
        return lax.all_to_all(x, axis, 0, 0, tiled=True)

    f32 = jnp.float32
    pending = []
    recv = None
    outputs = []
    cuts = [bases[h] for h in CUTS]
    rows = pl.BlockSpec((6, 32, 512), lambda *_: (0, 0, 0))

    def block(*lead):
        def spec(n, slot):
            return pl.BlockSpec((1, 1) + (n,) * len(lead) + (32, 512), lambda *_: (slot, 0) + lead + (0, 0))

        return spec

    spans = list(zip(cuts[:-1], cuts[1:]))
    all_sides = pl.BlockSpec((19, 16, 128), lambda *_: (0, 0, 0))
    tall = [pltpu.VMEM((19 * 32, 128), f32)]
    rhs, top, *wholes = call(
        pack_kernel,
        tall,
        (1,),
        [all_sides, block()(0, 16), block()(0, 17), block()(0, 18), block(0)(2, 16), block(0)(1, 17)]
        + [pl.BlockSpec((hi - lo, 1, 32, 512), lambda *_, i=lo // (hi - lo): (i, 0, 0, 0)) for lo, hi in spans],
        [all_sides, rows] + [pl.BlockSpec((hi - lo, 32, 512), lambda *_: (0, 0, 0)) for lo, hi in spans],
        [jax.ShapeDtypeStruct((19, 16, 128), f32), jax.ShapeDtypeStruct((6, 32, 512), f32)]
        + [jax.ShapeDtypeStruct((hi - lo, 32, 512), f32) for lo, hi in spans],
        {},
        rhs,
        *[inverse_rows] * 3,
        *[panels] * 2,
        *[inverse_rows] * len(spans),
    )
    top = lax.all_gather(top, "pcol", axis=0)
    for height in range(TOP):
        count = slot_counts[height]
        base = bases[height]
        reach = LEVELS - 1 - height
        info = (height, count, base)
        whole = height >= GATHER_FROM
        piece = jax.ShapeDtypeStruct((16, count, 16, 128), f32)
        own = jax.ShapeDtypeStruct((count, 16, 128), f32)
        every = pl.BlockSpec((16, count, 16, 128), lambda *_: (0, 0, 0, 0))
        every_own = pl.BlockSpec((count, 16, 128), lambda *_: (0, 0, 0))
        rhs_all = pl.BlockSpec((count, 16, 128), lambda *_, b=base // count: (b, 0, 0))
        if whole:
            z = call(
                functools.partial(residue_kernel, *info), [], (1,), [every, rhs_all], every, piece, {}, recv, rhs
            )
            gathered = exchange(z, "prow")
        else:
            per = min(4, count)
            in_specs = [
                pl.BlockSpec((per, 16, 128), lambda s, *_, b=base // per: (b + s, 0, 0)),
                pl.BlockSpec((per, 1, 32, 512), lambda s, *_, b=base // per: (b + s, 0, 0, 0)),
            ]
            args = [rhs, inverse_rows]
            if height > 0:
                in_specs = [pl.BlockSpec((recv.shape[0], per, 16, 128), lambda s, *_: (0, s, 0, 0))] + in_specs
                args = [recv] + args
            some = pl.BlockSpec((16, per, 16, 128), lambda s, *_: (0, s, 0, 0))
            kernel = functools.partial(partial_kernel, *info)
            parts = call(kernel, [], (count // per,), in_specs, some, piece, {}, *args)
            parts = exchange(parts, "prow")
            if height == 0:
                wholes, parts = lax.optimization_barrier((wholes, parts))
                inverses = [(lo, lax.all_gather(part, "prow", axis=0)) for lo, part in zip(cuts[:-1], wholes)]
            y, sol = call(
                functools.partial(solved_kernel, *info), [], (1,), [every], [every, every_own], [piece, own], {}, parts
            )
            outputs.append(sol)
            gathered = exchange(y, "prow")
        steps = [(0, 1), (1, reach)] if height + 1 < TOP else [(0, reach)]
        updated = []
        given, source = gathered, "z" if whole else "y"
        for start, end in steps:
            per = 1 if source == "z" else min(2, count)
            in_specs = [pl.BlockSpec((16, per, 16, 128), lambda s, *_: (0, s, 0, 0))]
            if source == "t":
                in_specs = [pl.BlockSpec((per, 64, 512), lambda s, *_: (s, 0, 0))]
            args = [given]
            out_specs, out_shape = [], []
            if source == "z":
                lo, inverse = [pair for pair in inverses if pair[0] <= base][-1]
                in_specs.append(pl.BlockSpec((16, 1, 32, 512), lambda s, *_, b=base - lo: (0, b + s, 0, 0)))
                args.append(inverse)
                out_specs.append(pl.BlockSpec((1, 16, 128), lambda s, *_: (s, 0, 0)))
                out_shape.append(own)
                if end < reach:
                    out_specs.append(pl.BlockSpec((1, 64, 512), lambda s, *_: (s, 0, 0)))
                    out_shape.append(jax.ShapeDtypeStruct((count, 64, 512), f32))
            in_specs.append(
                pl.BlockSpec((per, 1, end, 32, 512), lambda s, *_, b=base // per: (b + s, 0, 0, 0, 0))
            )
            args.append(panels)
            aliases = {}
            for d in range(start, end):
                shape = (16 * slot_counts[height + 1 + d], 16, 128)
                spec = pl.BlockSpec(shape, lambda *_: (0, 0, 0))
                if height > 0:
                    aliases[len(in_specs)] = len(out_specs)
                    in_specs.append(spec)
                    args.append(pending[d])
                out_specs.append(spec)
                out_shape.append(jax.ShapeDtypeStruct(shape, f32))
            results = call(
                functools.partial(spread_kernel, *info, source, start, end),
                SCRATCH,
                (count // per,),
                in_specs,
                out_specs,
                out_shape,
                aliases,
                *args,
            )
            results = list(results)
            if source == "z":
                outputs.append(results.pop(0))
                if end < reach:
                    given, source = results.pop(0), "t"
            updated += results
        results = updated
        if height + 1 < TOP:
            following = slot_counts[height + 1]
            pending = results[1:]
            if height == 0:
                half = pl.BlockSpec((32, 16, 128), lambda *_: (0, 0, 0))
                there = lax.ppermute(results[0][32:], "pcol", [(i, i ^ 1) for i in range(16)])
                joined = call(
                    join_kernel,
                    [],
                    (1,),
                    [half, half],
                    pl.BlockSpec((8, 4, 16, 128), lambda *_: (0, 0, 0, 0)),
                    jax.ShapeDtypeStruct((8, 4, 16, 128), f32),
                    {},
                    results[0],
                    there,
                )
                recv = lax.all_to_all(
                    joined,
                    "pcol",
                    0,
                    0,
                    tiled=True,
                    axis_index_groups=[[core + 2 * z for z in range(8)] for core in range(2)],
                )
            else:
                recv = exchange(results[0].reshape(16, following, 16, 128), "pcol")
        if height == 1:
            top, recv = lax.optimization_barrier((top, recv))
            halves = [(4, 3, 0, 1), (2, 2, 0, 0), (1, 1, 0, 2)]
            chosen = call(
                choose_kernel,
                [],
                (1,),
                [
                    pl.BlockSpec((m, n, 32, 256), lambda _, info, a=a, b=b: (a, b, 0, info[1] % 2))
                    for m, n, a, b in halves
                ],
                pl.BlockSpec((17, 32, 256), lambda *_: (0, 0, 0)),
                jax.ShapeDtypeStruct((17, 32, 256), f32),
                {},
                *[top] * 3,
            )
            top = lax.all_gather(chosen, "prow", axis=0)
    many = pl.BlockSpec((16, 16, 128), lambda *_: (0, 0, 0))
    sides = pl.BlockSpec((16, 8, 256), lambda *_: (0, 0, 0))
    sides_shape = jax.ShapeDtypeStruct((16, 8, 256), f32)
    turned = call(
        turn_kernel,
        [pltpu.VMEM((256, 128), f32)],
        (1,),
        [many] * 3 + [pl.BlockSpec((19, 16, 128), lambda *_: (0, 0, 0))],
        sides,
        sides_shape,
        {},
        *results,
        rhs,
    )
    total = call(sum_kernel, [], (1,), [sides], sides, sides_shape, {}, exchange(turned, "pcol"))
    gathered = exchange(total, "prow")
    def halves_from(start, n):
        return pl.BlockSpec((16, n, 32, 256), lambda s, *_: (0, start // n + s, 0, 0))

    def whole_of(*shape):
        return pl.BlockSpec(shape, lambda *_: (0,) * len(shape)), jax.ShapeDtypeStruct(shape, f32)

    def other_core(x):
        return lax.ppermute(x, "pcol", [(i, i ^ 1) for i in range(16)])

    found, found_shape = whole_of(16, 8, 128)
    three, three_shape = whole_of(3, 8, 512)
    single, single_shape = whole_of(8, 512)
    solved, left = call(
        low_kernel,
        [pltpu.VMEM((4, 8, 512), f32)],
        (4,),
        [sides, halves_from(0, 3)],
        [found, three],
        [found_shape, three_shape],
        {},
        gathered,
        top,
    )
    solved, left = call(
        middle_kernel,
        [],
        (2,),
        [three, three, found, halves_from(12, 2)],
        [found, single],
        [found_shape, single_shape],
        {},
        left,
        other_core(left),
        solved,
        top,
    )
    solved = call(
        root_kernel,
        [],
        (1,),
        [single, single, found, halves_from(16, 1)],
        found,
        found_shape,
        {},
        left,
        other_core(left),
        solved,
        top,
    )
    out = call(
        last_kernel,
        tall,
        (1,),
        [found] + [pl.BlockSpec(x.shape, lambda *_: (0, 0, 0)) for x in outputs],
        all_sides,
        jax.ShapeDtypeStruct((19, 16, 128), f32),
        {},
        exchange(solved, "pcol"),
        *outputs,
    )
    return out.reshape(19, 1, 2048)


def solution(mesh):
    in_specs = (
        P(None, "pcol", "prow"),
        P(None, "pcol", "prow", None),
        P(None, "pcol", None, "prow", None),
        P(None, "pcol", None),
        P(None, "pcol"),
        P(),
    )
    out_specs = P(None, "pcol", "prow")
    return jax.shard_map(
        on_device, mesh=mesh, in_specs=in_specs, out_specs=out_specs, check_vma=False
    )
```

```python
import functools

import jax
import jax.numpy as jnp
from jax import lax
from jax.experimental import pallas as pl
from jax.experimental.pallas import tpu as pltpu
from jax.sharding import PartitionSpec as P

LEVELS = 8
LEAVES = 128
GATHER_FROM = 2
CUTS = (2, 5)
SCRATCH = [pltpu.VMEM((192, 512), jnp.float32)]
TOP = 5
VMEM_LIMIT = 24 * 1024 * 1024

NODES = [LEAVES >> h for h in range(LEVELS)]
NODE_BASE = [2 * LEAVES - 2 * (LEAVES >> h) for h in range(LEVELS)]


class Part:
    def __init__(self, ref, start):
        self.ref, self.start = ref, start

    def __getitem__(self, index):
        return self.ref[index + self.start]


def with_parts(kernel, *refs):
    return kernel(*[Part(refs[0], start) for start in (0, 2, 256, 389)], *refs[1:])


def split(x):
    high = x.astype(jnp.bfloat16)
    low = (x - high.astype(jnp.float32)).astype(jnp.bfloat16)
    return high, low


def dot3(a, b, dims):
    bh, bl = b if isinstance(b, tuple) else split(b)
    dot = functools.partial(
        lax.dot_general, dimension_numbers=(dims, ((), ())), preferred_element_type=jnp.float32
    )
    n = a.shape[0]
    if n <= 64 and dims[0] == (1,):
        high = a.astype(jnp.bfloat16).astype(jnp.float32)
        both = jnp.concatenate([high, a - high], 0).astype(jnp.bfloat16)
        first = dot(both, bh)
        second = dot(high.astype(jnp.bfloat16), bl)
        return first[:n] + (first[n:] + second)
    ah, al = split(a)
    return dot(ah, bh) + (dot(ah, bl) + dot(al, bh))


def lower(shape):
    return lax.broadcasted_iota(jnp.int32, shape, len(shape) - 1) < 64


def from_own_order(x, scratch):
    n = x.shape[0]
    x = x.reshape(n * 16, 128)
    scratch[pl.ds(0, n * 16, stride=2), :] = x
    scratch[pl.ds(1, n * 16, stride=2), :] = pltpu.roll(x, 64, 1)
    rows = scratch[pl.ds(0, n * 32), :].reshape(n, 2, 16, 128)
    other = pltpu.roll(rows[:, 1].reshape(n * 16, 128), 64, 1).reshape(n, 16, 128)
    return jnp.where(lower((n, 16, 128)), rows[:, 0], other)


def to_own_order(x, scratch):
    n = x.shape[0]
    turned = pltpu.roll(x.reshape(n * 16, 128), 64, 1).reshape(n, 1, 16, 128)
    scratch[pl.ds(0, n * 32), :] = jnp.concatenate([x.reshape(n, 1, 16, 128), turned], 1).reshape(n * 32, 128)
    even = scratch[pl.ds(0, n * 16, stride=2), :]
    odd = pltpu.roll(scratch[pl.ds(1, n * 16, stride=2), :], 64, 1)
    return jnp.where(lower((n * 16, 128)), even, odd).reshape(n, 16, 128)


def fold(x):
    n = x.shape[0] // 32
    x = x.reshape(n, 2, 16, 128)
    return jnp.where(lower((n, 16, 128)), x[:, 0], x[:, 1])


def own_mask(pos, sizes, slot, local, nodes):
    row = lax.broadcasted_iota(jnp.int32, (16, 128), 0)
    lane = lax.broadcasted_iota(jnp.int32, (16, 128), 1)
    row_id = pos[0] * 32 + row + 16 * (lane >= 64).astype(jnp.int32)
    limit = jnp.where(local * 16 + pos[1] < nodes, sizes[slot], 0)
    return row_id < limit


def residue_kernel(height, slots, slot_base, pos, parent, pattern, sizes, recv, rhs, out):
    for s in range(slots):
        total = recv[0, s]
        for i in range(1, 16):
            total = total + recv[i, s]
        keep = own_mask(pos, sizes, slot_base + s, s, NODES[height])
        z = jnp.where(keep, rhs[s] - total, 0.0)
        for i in range(16):
            out[i, s] = z


def partial_kernel(height, slots, slot_base, pos, parent, pattern, sizes, *refs):
    recv = None
    if height > 0:
        recv, *refs = refs
    rhs, inverse, out, scratch = refs
    low = lower((16, 128))
    sides = from_own_order(rhs[...], scratch)
    for i in range(rhs.shape[0]):
        s = pl.program_id(0) * rhs.shape[0] + i
        z = sides[i]
        if recv is not None:
            total = recv[0, i]
            for k in range(1, recv.shape[0]):
                total = total + recv[k, i]
            z = z - total
        keep = own_mask(pos, sizes, slot_base + s, s, NODES[height])
        z = jnp.where(keep, z, 0.0)
        turned = pltpu.roll(z, 64, 1)
        twice = jnp.concatenate([jnp.where(low, z, turned), jnp.where(low, turned, z)], 0)
        out[:, i] = fold(dot3(inverse[i, 0], twice, ((0,), (0,))))


def solved_kernel(height, slots, slot_base, pos, parent, pattern, sizes, recv, out, sol):
    for s in range(slots):
        total = recv[0, s]
        for i in range(1, 16):
            total = total + recv[i, s]
        keep = own_mask(pos, sizes, slot_base + s, s, NODES[height])
        y = jnp.where(keep, total, 0.0)
        sol[s] = y
        for i in range(16):
            out[i, s] = y


def spread_kernel(height, slots, slot_base, source, first, end, pos, parent, pattern, sizes, *refs):
    refs = list(refs)
    given = refs.pop(0)
    inverse = (refs.pop(0), refs.pop(0)) if source == "z" else None
    panels = refs.pop(0)
    before = [refs.pop(0) for _ in range(first, end)] if height > 0 else []
    sol = refs.pop(0) if source == "z" else None
    kept = refs.pop(0) if source == "z" and end < LEVELS - 1 - height else None
    after = [refs.pop(0) for _ in range(first, end)]
    scratch = refs.pop(0)

    @pl.when(pl.program_id(0) == 0)
    def _():
        for i, ref in enumerate(after):
            ref[...] = before[i][...] if before else jnp.zeros_like(ref)

    for k in range(panels.shape[0]):
        s = pl.program_id(0) * panels.shape[0] + k
        slot = slot_base + s
        if source == "z":
            turned = given[:, k].reshape(256, 128).T
            z_t = jnp.concatenate([turned[:64], turned[64:]], 1)
            y_t = dot3(z_t, (inverse[0][k], inverse[1][k]), ((1,), (0,)))
            limit = sizes[slot]
            y_t = jnp.where(lax.broadcasted_iota(jnp.int32, (64, 512), 1) < limit, y_t, 0.0)
            scratch[pl.ds(0, 64), :] = y_t
            lanes = scratch[pl.ds(0, 64), pl.ds(pl.multiple_of(pos[0] // 4 * 128, 128), 128)]
            own = jnp.concatenate([lanes, lanes], 0).T
            scratch[pl.ds(64, 128), pl.ds(0, 128)] = own
            own = scratch[pl.ds(pl.multiple_of(64 + pos[0] % 4 * 32, 32), 32), pl.ds(0, 128)]
            sol[k] = fold(own)[0]
            if kept is not None:
                kept[k] = y_t
        elif source == "y":
            x = given[:, k].reshape(256, 128)
            turned = pltpu.roll(x, 64, 1).reshape(16, 1, 16, 128)
            y_t = jnp.concatenate([x.reshape(16, 1, 16, 128), turned], 1).reshape(512, 128).T[:64]
        else:
            y_t = given[k]
        block = panels[k, 0, first:end].reshape((end - first) * 32, 512)
        update = fold(dot3(block, jnp.concatenate([y_t, y_t], 0), ((1,), (1,))))
        node = NODE_BASE[height] + jnp.minimum(s * 16 + pos[1], NODES[height] - 1)
        for d in range(end):
            node = parent[node]
            if d < first:
                continue
            target = height + 1 + d
            j = node - NODE_BASE[target]
            if target == 1:
                where = ((j + pos[1]) % 2 * 8 + j % 16 // 2) * 4 + j // 16
            else:
                where = (j % 16) * max(1, NODES[target] // 16) + j // 16
            scale = pattern[slot * 7 + d].astype(jnp.float32)
            after[d - first][where] += scale * update[d - first]


def split_inverse_kernel(pos, parent, pattern, sizes, inverse, high, low):
    rows = inverse[:, 0].reshape(16, 2, 16, 512)
    rows = jnp.concatenate([rows[:, 0].reshape(256, 512), rows[:, 1].reshape(256, 512)], 0)
    high[0], low[0] = split(rows)


def split_top_kernel(pos, parent, pattern, sizes, block, high, low):
    high[0], low[0] = split(block[:, 0].reshape(512, 256))


def join_kernel(pos, parent, pattern, sizes, here, there, out):
    out[...] = (here[...] + there[...]).reshape(out.shape)


def pack_kernel(pos, parent, pattern, sizes, sides, inv5, inv6, inv7, panel5, panel6, *refs):
    *refs, scratch = refs
    half = len(refs) // 2 - 1
    folded, out = refs[half : half + 2]
    folded[...] = from_own_order(sides[...], scratch)
    for source, target in zip(refs[:half], refs[half + 2 :]):
        target[...] = source[:, 0]
    for level, inv, panel, at in ((0, inv5, panel5, 3), (1, inv6, panel6, 0), (2, inv7, None, 2)):
        slot = 16 + level
        size = sizes[slot]
        row = pos[0] * 32 + lax.broadcasted_iota(jnp.int32, (32, 512), 0)
        column = lax.broadcasted_iota(jnp.int32, (32, 512), 1)
        out[at] = jnp.where((row < size) & (column < size), inv[0, 0], 0.0)
        for d in range(2 - level):
            out[at + 1 + d] = panel[0, 0, d] * pattern[slot * 7 + d].astype(jnp.float32)


def choose_kernel(pos, parent, pattern, sizes, low, middle, high, out):
    for c in range(4):
        out[3 * c : 3 * c + 3] = low[c]
    for c in range(2):
        out[12 + 2 * c : 14 + 2 * c] = middle[c]
    out[16:17] = high[0]


def turn_kernel(pos, parent, pattern, sizes, p5, p6, p7, rhs, out, scratch):
    at = 0
    for level, ref in enumerate((p5, p6, p7)):
        for j in range(4 >> level):
            piece = ref[j] - jnp.where(pos[1] == j, rhs[16 + level], 0.0)
            scratch[pl.ds(at * 32, 16), :] = piece
            scratch[pl.ds(at * 32 + 16, 16), :] = pltpu.roll(piece, 64, 1)
            at += 1
    scratch[pl.ds(224, 32), :] = jnp.zeros((32, 128), jnp.float32)
    turned = scratch[pl.ds(0, 256), :].T
    for z in range(8):
        out[2 * z] = turned[8 * z : 8 * z + 8]
        out[2 * z + 1] = turned[8 * z : 8 * z + 8]


def sum_kernel(pos, parent, pattern, sizes, recv, out):
    total = recv[0]
    for i in range(1, 16):
        total = total + recv[i]
    for i in range(16):
        out[i] = total


def place(own, y, level, pos):
    lanes = pltpu.roll(y, (256 - (pos[0] % 8) * 32) % 256, 1)[:, :128]
    lane = lax.broadcasted_iota(jnp.int32, (8, 128), 1) // 32
    return jnp.where(lane == level, pltpu.roll(lanes, level * 32, 1), own)


def low_kernel(pos, parent, pattern, sizes, recv, high, low, out, left, z):
    step = pl.program_id(0)

    @pl.when(step == 0)
    def _():
        lane = lax.broadcasted_iota(jnp.int32, (8, 128), 1) // 32
        for n in range(7):
            for g in range(4):
                whole = jnp.zeros((8, 128), jnp.float32)
                for i in range(4):
                    piece = recv[4 * g + i][:, (n // 4) * 128 : (n // 4 + 1) * 128]
                    turned = pltpu.roll(piece, ((i - n % 4) * 32) % 128, 1)
                    whole = jnp.where(lane == i, turned, whole)
                if n < 4:
                    z[n, :, g * 128 : (g + 1) * 128] = -whole
                else:
                    left[n - 4, :, g * 128 : (g + 1) * 128] = jnp.where(pos[1] % 2 == 0, -whole, 0.0)
        out[...] = jnp.zeros_like(out)

    solved = dot3(z[step], (high[0], low[0]), ((1,), (0,)))
    out[step] = place(out[step], solved, 0, pos)
    target = parent[NODE_BASE[TOP] + step] - NODE_BASE[TOP + 1]
    left[target] = left[target] - dot3(solved, (high[1], low[1]), ((1,), (1,)))
    left[2] = left[2] - dot3(solved, (high[2], low[2]), ((1,), (1,)))


def middle_kernel(pos, parent, pattern, sizes, left, other, before, high, low, out, after):
    step = pl.program_id(0)

    @pl.when(step == 0)
    def _():
        out[...] = before[...]
        after[...] = left[2]

    solved = dot3(left[step] + other[step], (high[0], low[0]), ((1,), (0,)))
    out[step] = place(out[step], solved, 1, pos)
    after[...] = after[...] - dot3(solved, (high[1], low[1]), ((1,), (1,)))


def root_kernel(pos, parent, pattern, sizes, left, other, before, high, low, out):
    solved = dot3(left[...] + other[...], (high[0], low[0]), ((1,), (0,)))
    out[...] = before[...]
    out[0] = place(before[0], solved, 2, pos)


def last_kernel(pos, parent, pattern, sizes, recv, *refs):
    *parts, out, scratch = refs
    columns = jnp.concatenate([recv[2 * i + pos[0] // 8] for i in range(8)], 0)
    turned = jnp.concatenate([columns, columns], 0).T
    parts = [ref[...] for ref in parts] + [fold(turned[:96])]
    out[...] = to_own_order(jnp.concatenate(parts, 0), scratch)


def on_device(right_side, inverse_rows, panels, pattern, node_sizes, parent):
    pos = jnp.stack([lax.axis_index("prow"), lax.axis_index("pcol")]).astype(jnp.int32)
    natural = right_side.reshape(19, 16, 128)
    scalars = jnp.concatenate([pos, parent, pattern.reshape(-1), node_sizes.reshape(-1)])
    slot_counts = [max(1, n // 16) for n in NODES]
    bases = [sum(slot_counts[:h]) for h in range(LEVELS)]
    def call(kernel, scratch, grid, in_specs, out_specs, out_shape, aliases, *args):
        args = [pltpu.with_memory_space_constraint(a, pltpu.HBM) if a.size > 1 << 18 else a for a in args]
        return pl.pallas_call(
            functools.partial(with_parts, kernel),
            grid_spec=pltpu.PrefetchScalarGridSpec(
                num_scalar_prefetch=1,
                grid=grid,
                in_specs=in_specs,
                out_specs=out_specs,
                scratch_shapes=scratch,
            ),
            out_shape=out_shape,
            input_output_aliases={k + 1: v for k, v in aliases.items()},
            compiler_params=pltpu.CompilerParams(vmem_limit_bytes=VMEM_LIMIT),
        )(scalars, *args)

    def exchange(x, axis):
        return lax.all_to_all(x, axis, 0, 0, tiled=True)

    f32 = jnp.float32
    pending = []
    recv = None
    outputs = []
    cuts = [bases[h] for h in CUTS]
    rows = pl.BlockSpec((6, 32, 512), lambda *_: (0, 0, 0))

    def block(*lead):
        def spec(n, slot):
            return pl.BlockSpec((1, 1) + (n,) * len(lead) + (32, 512), lambda *_: (slot, 0) + lead + (0, 0))

        return spec

    spans = list(zip(cuts[:-1], cuts[1:]))
    all_sides = pl.BlockSpec((19, 16, 128), lambda *_: (0, 0, 0))
    tall = [pltpu.VMEM((19 * 32, 128), f32)]
    rhs, top, *wholes = call(
        pack_kernel,
        tall,
        (1,),
        [all_sides, block()(0, 16), block()(0, 17), block()(0, 18), block(0)(2, 16), block(0)(1, 17)]
        + [pl.BlockSpec((hi - lo, 1, 32, 512), lambda *_, i=lo // (hi - lo): (i, 0, 0, 0)) for lo, hi in spans],
        [all_sides, rows] + [pl.BlockSpec((hi - lo, 32, 512), lambda *_: (0, 0, 0)) for lo, hi in spans],
        [jax.ShapeDtypeStruct((19, 16, 128), f32), jax.ShapeDtypeStruct((6, 32, 512), f32)]
        + [jax.ShapeDtypeStruct((hi - lo, 32, 512), f32) for lo, hi in spans],
        {},
        natural,
        *[inverse_rows] * 3,
        *[panels] * 2,
        *[inverse_rows] * len(spans),
    )
    top = lax.all_gather(top, "pcol", axis=0)
    for height in range(TOP):
        count = slot_counts[height]
        base = bases[height]
        reach = LEVELS - 1 - height
        info = (height, count, base)
        whole = height >= GATHER_FROM
        piece = jax.ShapeDtypeStruct((16, count, 16, 128), f32)
        own = jax.ShapeDtypeStruct((count, 16, 128), f32)
        every = pl.BlockSpec((16, count, 16, 128), lambda *_: (0, 0, 0, 0))
        every_own = pl.BlockSpec((count, 16, 128), lambda *_: (0, 0, 0))
        rhs_all = pl.BlockSpec((count, 16, 128), lambda *_, b=base // count: (b, 0, 0))
        if whole:
            z = call(
                functools.partial(residue_kernel, *info), [], (1,), [every, rhs_all], every, piece, {}, recv, rhs
            )
            gathered = exchange(z, "prow")
            lo, inverse = [pair for pair in inverses if pair[0] <= base][-1]
            inverse, _ = lax.optimization_barrier((inverse, z))
            inverse = call(
                split_inverse_kernel,
                [],
                (count,),
                [pl.BlockSpec((16, 1, 32, 512), lambda s, *_, b=base - lo: (0, b + s, 0, 0))],
                [pl.BlockSpec((1, 512, 512), lambda s, *_: (s, 0, 0))] * 2,
                [jax.ShapeDtypeStruct((count, 512, 512), jnp.bfloat16)] * 2,
                {},
                inverse,
            )
        else:
            per = min(4, count)
            in_specs = [
                pl.BlockSpec((per, 16, 128), lambda s, *_, b=base // per: (b + s, 0, 0)),
                pl.BlockSpec((per, 1, 32, 512), lambda s, *_, b=base // per: (b + s, 0, 0, 0)),
            ]
            args = [natural, inverse_rows]
            if height > 0:
                in_specs = [pl.BlockSpec((recv.shape[0], per, 16, 128), lambda s, *_: (0, s, 0, 0))] + in_specs
                args = [recv] + args
            some = pl.BlockSpec((16, per, 16, 128), lambda s, *_: (0, s, 0, 0))
            kernel = functools.partial(partial_kernel, *info)
            parts = call(kernel, [pltpu.VMEM((per * 32, 128), f32)], (count // per,), in_specs, some, piece, {}, *args)
            parts = exchange(parts, "prow")
            if height == 0:
                wholes, parts = lax.optimization_barrier((wholes, parts))
                inverses = [(lo, lax.all_gather(part, "prow", axis=0)) for lo, part in zip(cuts[:-1], wholes)]
            y, sol = call(
                functools.partial(solved_kernel, *info), [], (1,), [every], [every, every_own], [piece, own], {}, parts
            )
            outputs.append(sol)
            gathered = exchange(y, "prow")
        if height == 1:
            chosen_from, _ = lax.optimization_barrier((top, y))
            halves = [(4, 3, 0, 1), (2, 2, 0, 0), (1, 1, 0, 2)]
            chosen = call(
                choose_kernel,
                [],
                (1,),
                [
                    pl.BlockSpec((m, n, 32, 256), lambda _, info, a=a, b=b: (a, b, 0, info[1] % 2))
                    for m, n, a, b in halves
                ],
                pl.BlockSpec((17, 32, 256), lambda *_: (0, 0, 0)),
                jax.ShapeDtypeStruct((17, 32, 256), f32),
                {},
                *[chosen_from] * 3,
            )
            top = lax.all_gather(chosen, "prow", axis=0)
        steps = [(0, 1), (1, reach)] if height + 1 < TOP else [(0, reach)]
        updated = []
        given, source = gathered, "z" if whole else "y"
        for start, end in steps:
            per = 1 if source == "z" else min(2, count)
            in_specs = [pl.BlockSpec((16, per, 16, 128), lambda s, *_: (0, s, 0, 0))]
            if source == "t":
                in_specs = [pl.BlockSpec((per, 64, 512), lambda s, *_: (s, 0, 0))]
            args = [given]
            out_specs, out_shape = [], []
            if source == "z":
                in_specs += [pl.BlockSpec((1, 512, 512), lambda s, *_: (s, 0, 0))] * 2
                args += inverse
                out_specs.append(pl.BlockSpec((1, 16, 128), lambda s, *_: (s, 0, 0)))
                out_shape.append(own)
                if end < reach:
                    out_specs.append(pl.BlockSpec((1, 64, 512), lambda s, *_: (s, 0, 0)))
                    out_shape.append(jax.ShapeDtypeStruct((count, 64, 512), f32))
            in_specs.append(
                pl.BlockSpec((per, 1, end, 32, 512), lambda s, *_, b=base // per: (b + s, 0, 0, 0, 0))
            )
            args.append(panels)
            aliases = {}
            for d in range(start, end):
                shape = (16 * slot_counts[height + 1 + d], 16, 128)
                spec = pl.BlockSpec(shape, lambda *_: (0, 0, 0))
                if height > 0:
                    aliases[len(in_specs)] = len(out_specs)
                    in_specs.append(spec)
                    args.append(pending[d])
                out_specs.append(spec)
                out_shape.append(jax.ShapeDtypeStruct(shape, f32))
            results = call(
                functools.partial(spread_kernel, *info, source, start, end),
                SCRATCH,
                (count // per,),
                in_specs,
                out_specs,
                out_shape,
                aliases,
                *args,
            )
            results = list(results)
            if source == "z":
                outputs.append(results.pop(0))
                if end < reach:
                    given, source = results.pop(0), "t"
            updated += results
        results = updated
        if height + 1 < TOP:
            following = slot_counts[height + 1]
            pending = results[1:]
            if height == 0:
                half = pl.BlockSpec((32, 16, 128), lambda *_: (0, 0, 0))
                there = lax.ppermute(results[0][32:], "pcol", [(i, i ^ 1) for i in range(16)])
                joined = call(
                    join_kernel,
                    [],
                    (1,),
                    [half, half],
                    pl.BlockSpec((8, 4, 16, 128), lambda *_: (0, 0, 0, 0)),
                    jax.ShapeDtypeStruct((8, 4, 16, 128), f32),
                    {},
                    results[0],
                    there,
                )
                recv = lax.all_to_all(
                    joined,
                    "pcol",
                    0,
                    0,
                    tiled=True,
                    axis_index_groups=[[core + 2 * z for z in range(8)] for core in range(2)],
                )
            else:
                recv = exchange(results[0].reshape(16, following, 16, 128), "pcol")
    many = pl.BlockSpec((16, 16, 128), lambda *_: (0, 0, 0))
    sides = pl.BlockSpec((16, 8, 256), lambda *_: (0, 0, 0))
    sides_shape = jax.ShapeDtypeStruct((16, 8, 256), f32)
    turned = call(
        turn_kernel,
        [pltpu.VMEM((256, 128), f32)],
        (1,),
        [many] * 3 + [pl.BlockSpec((19, 16, 128), lambda *_: (0, 0, 0))],
        sides,
        sides_shape,
        {},
        *results,
        rhs,
    )
    total = call(sum_kernel, [], (1,), [sides], sides, sides_shape, {}, exchange(turned, "pcol"))
    gathered = exchange(total, "prow")
    top, _ = lax.optimization_barrier((top, total))
    top = call(
        split_top_kernel,
        [],
        (17,),
        [pl.BlockSpec((16, 1, 32, 256), lambda s, *_: (0, s, 0, 0))],
        [pl.BlockSpec((1, 512, 256), lambda s, *_: (s, 0, 0))] * 2,
        [jax.ShapeDtypeStruct((17, 512, 256), jnp.bfloat16)] * 2,
        {},
        top,
    )
    def halves_from(start, n):
        return [pl.BlockSpec((n, 512, 256), lambda s, *_: (start // n + s, 0, 0))] * 2

    def whole_of(*shape):
        return pl.BlockSpec(shape, lambda *_: (0,) * len(shape)), jax.ShapeDtypeStruct(shape, f32)

    def other_core(x):
        return lax.ppermute(x, "pcol", [(i, i ^ 1) for i in range(16)])

    found, found_shape = whole_of(16, 8, 128)
    three, three_shape = whole_of(3, 8, 512)
    single, single_shape = whole_of(8, 512)
    solved, left = call(
        low_kernel,
        [pltpu.VMEM((4, 8, 512), f32)],
        (4,),
        [sides] + halves_from(0, 3),
        [found, three],
        [found_shape, three_shape],
        {},
        gathered,
        *top,
    )
    solved, left = call(
        middle_kernel,
        [],
        (2,),
        [three, three, found] + halves_from(12, 2),
        [found, single],
        [found_shape, single_shape],
        {},
        left,
        other_core(left),
        solved,
        *top,
    )
    solved = call(
        root_kernel,
        [],
        (1,),
        [single, single, found] + halves_from(16, 1),
        found,
        found_shape,
        {},
        left,
        other_core(left),
        solved,
        *top,
    )
    out = call(
        last_kernel,
        tall,
        (1,),
        [found] + [pl.BlockSpec(x.shape, lambda *_: (0, 0, 0)) for x in outputs],
        all_sides,
        jax.ShapeDtypeStruct((19, 16, 128), f32),
        {},
        exchange(solved, "pcol"),
        *outputs,
    )
    return out.reshape(19, 1, 2048)


def solution(mesh):
    in_specs = (
        P(None, "pcol", "prow"),
        P(None, "pcol", "prow", None),
        P(None, "pcol", None, "prow", None),
        P(None, "pcol", None),
        P(None, "pcol"),
        P(),
    )
    out_specs = P(None, "pcol", "prow")
    return jax.shard_map(
        on_device, mesh=mesh, in_specs=in_specs, out_specs=out_specs, check_vma=False
    )
```

```python
import functools

import jax
import jax.numpy as jnp
from jax import lax
from jax.experimental import pallas as pl
from jax.experimental.pallas import tpu as pltpu
from jax.sharding import PartitionSpec as P

LEVELS = 8
LEAVES = 128
GATHER_FROM = 2
CUTS = (2, 5)
SCRATCH = [pltpu.VMEM((192, 512), jnp.float32)]
TOP = 5
VMEM_LIMIT = 24 * 1024 * 1024

NODES = [LEAVES >> h for h in range(LEVELS)]
NODE_BASE = [2 * LEAVES - 2 * (LEAVES >> h) for h in range(LEVELS)]


class Part:
    def __init__(self, ref, start):
        self.ref, self.start = ref, start

    def __getitem__(self, index):
        return self.ref[index + self.start]


def with_parts(kernel, *refs):
    return kernel(*[Part(refs[0], start) for start in (0, 2, 256, 389)], *refs[1:])


def split(x):
    high = x.astype(jnp.bfloat16)
    low = (x - high.astype(jnp.float32)).astype(jnp.bfloat16)
    return high, low


def dot3(a, b, dims):
    bh, bl = b if isinstance(b, tuple) else split(b)
    dot = functools.partial(
        lax.dot_general, dimension_numbers=(dims, ((), ())), preferred_element_type=jnp.float32
    )
    n = a.shape[0]
    if n <= 64 and dims[0] == (1,):
        high = a.astype(jnp.bfloat16).astype(jnp.float32)
        both = jnp.concatenate([high, a - high], 0).astype(jnp.bfloat16)
        first = dot(both, bh)
        second = dot(high.astype(jnp.bfloat16), bl)
        return first[:n] + (first[n:] + second)
    ah, al = split(a)
    return dot(ah, bh) + (dot(ah, bl) + dot(al, bh))


def lower(shape):
    return lax.broadcasted_iota(jnp.int32, shape, len(shape) - 1) < 64


def from_own_order(x, scratch):
    n = x.shape[0]
    x = x.reshape(n * 16, 128)
    scratch[pl.ds(0, n * 16, stride=2), :] = x
    scratch[pl.ds(1, n * 16, stride=2), :] = pltpu.roll(x, 64, 1)
    rows = scratch[pl.ds(0, n * 32), :].reshape(n, 2, 16, 128)
    other = pltpu.roll(rows[:, 1].reshape(n * 16, 128), 64, 1).reshape(n, 16, 128)
    return jnp.where(lower((n, 16, 128)), rows[:, 0], other)


def to_own_order(x, scratch):
    n = x.shape[0]
    turned = pltpu.roll(x.reshape(n * 16, 128), 64, 1).reshape(n, 1, 16, 128)
    scratch[pl.ds(0, n * 32), :] = jnp.concatenate([x.reshape(n, 1, 16, 128), turned], 1).reshape(n * 32, 128)
    even = scratch[pl.ds(0, n * 16, stride=2), :]
    odd = pltpu.roll(scratch[pl.ds(1, n * 16, stride=2), :], 64, 1)
    return jnp.where(lower((n * 16, 128)), even, odd).reshape(n, 16, 128)


def fold(x):
    n = x.shape[0] // 32
    x = x.reshape(n, 2, 16, 128)
    return jnp.where(lower((n, 16, 128)), x[:, 0], x[:, 1])


def own_mask(pos, sizes, slot, local, nodes):
    row = lax.broadcasted_iota(jnp.int32, (16, 128), 0)
    lane = lax.broadcasted_iota(jnp.int32, (16, 128), 1)
    row_id = pos[0] * 32 + row + 16 * (lane >= 64).astype(jnp.int32)
    limit = jnp.where(local * 16 + pos[1] < nodes, sizes[slot], 0)
    return row_id < limit


def residue_kernel(height, slots, slot_base, pos, parent, pattern, sizes, recv, rhs, out):
    for s in range(slots):
        total = recv[0, s]
        for i in range(1, 16):
            total = total + recv[i, s]
        keep = own_mask(pos, sizes, slot_base + s, s, NODES[height])
        z = jnp.where(keep, rhs[s] - total, 0.0)
        for i in range(16):
            out[i, s] = z


def partial_kernel(height, slots, slot_base, pos, parent, pattern, sizes, *refs):
    recv = None
    if height > 0:
        recv, *refs = refs
    rhs, inverse, out, scratch = refs
    low = lower((16, 128))
    sides = from_own_order(rhs[...], scratch)
    for i in range(rhs.shape[0]):
        s = pl.program_id(0) * rhs.shape[0] + i
        z = sides[i]
        if recv is not None:
            total = recv[0, i]
            for k in range(1, recv.shape[0]):
                total = total + recv[k, i]
            z = z - total
        keep = own_mask(pos, sizes, slot_base + s, s, NODES[height])
        z = jnp.where(keep, z, 0.0)
        turned = pltpu.roll(z, 64, 1)
        twice = jnp.concatenate([jnp.where(low, z, turned), jnp.where(low, turned, z)], 0)
        out[:, i] = fold(dot3(inverse[i, 0], twice, ((0,), (0,))))


def solved_kernel(height, slots, slot_base, pos, parent, pattern, sizes, recv, out, sol):
    for s in range(slots):
        total = recv[0, s]
        for i in range(1, 16):
            total = total + recv[i, s]
        keep = own_mask(pos, sizes, slot_base + s, s, NODES[height])
        y = jnp.where(keep, total, 0.0)
        sol[s] = y
        for i in range(16):
            out[i, s] = y


def spread_kernel(height, slots, slot_base, source, first, end, pos, parent, pattern, sizes, *refs):
    refs = list(refs)
    given = refs.pop(0)
    inverse = (refs.pop(0), refs.pop(0)) if source == "z" else None
    panels = refs.pop(0)
    before = [refs.pop(0) for _ in range(first, end)] if height > 0 else []
    sol = refs.pop(0) if source == "z" else None
    kept = refs.pop(0) if source == "z" and end < LEVELS - 1 - height else None
    after = [refs.pop(0) for _ in range(first, end)]
    scratch = refs.pop(0)

    @pl.when(pl.program_id(0) == 0)
    def _():
        for i, ref in enumerate(after):
            ref[...] = before[i][...] if before else jnp.zeros_like(ref)

    for k in range(panels.shape[0]):
        s = pl.program_id(0) * panels.shape[0] + k
        slot = slot_base + s
        if source == "z":
            turned = given[:, k].reshape(256, 128).T
            z_t = jnp.concatenate([turned[:64], turned[64:]], 1)
            y_t = dot3(z_t, (inverse[0][k], inverse[1][k]), ((1,), (0,)))
            limit = sizes[slot]
            y_t = jnp.where(lax.broadcasted_iota(jnp.int32, (64, 512), 1) < limit, y_t, 0.0)
            scratch[pl.ds(0, 64), :] = y_t
            lanes = scratch[pl.ds(0, 64), pl.ds(pl.multiple_of(pos[0] // 4 * 128, 128), 128)]
            own = jnp.concatenate([lanes, lanes], 0).T
            scratch[pl.ds(64, 128), pl.ds(0, 128)] = own
            own = scratch[pl.ds(pl.multiple_of(64 + pos[0] % 4 * 32, 32), 32), pl.ds(0, 128)]
            sol[k] = fold(own)[0]
            if kept is not None:
                kept[k] = y_t
        elif source == "t":
            y_t = given[k]
        block = panels[k, 0, first:end].reshape((end - first) * 32, 512)
        if source == "y":
            x = given[:, k]
            turned = pltpu.roll(x.reshape(256, 128), 64, 1).reshape(16, 16, 128)
            low = lower((16, 16, 128))
            halves = [jnp.where(low, x, turned)[:, None], jnp.where(low, turned, x)[:, None]]
            y = jnp.concatenate(halves, 1).reshape(512, 128)
            update = fold(dot3(block, y, ((1,), (0,))))
        else:
            update = fold(dot3(block, jnp.concatenate([y_t, y_t], 0), ((1,), (1,))))
        node = NODE_BASE[height] + jnp.minimum(s * 16 + pos[1], NODES[height] - 1)
        for d in range(end):
            node = parent[node]
            if d < first:
                continue
            target = height + 1 + d
            j = node - NODE_BASE[target]
            if target == 1:
                where = ((j + pos[1]) % 2 * 8 + j % 16 // 2) * 4 + j // 16
            else:
                where = (j % 16) * max(1, NODES[target] // 16) + j // 16
            scale = pattern[slot * 7 + d].astype(jnp.float32)
            after[d - first][where] += scale * update[d - first]


def split_inverse_kernel(pos, parent, pattern, sizes, inverse, high, low):
    rows = inverse[:, 0].reshape(16, 2, 16, 512)
    rows = jnp.concatenate([rows[:, 0].reshape(256, 512), rows[:, 1].reshape(256, 512)], 0)
    high[0], low[0] = split(rows)


def join_kernel(pos, parent, pattern, sizes, here, there, out):
    out[...] = (here[...] + there[...]).reshape(out.shape)


def pack_kernel(pos, parent, pattern, sizes, sides, inv5, inv6, inv7, panel5, panel6, *refs):
    *refs, scratch = refs
    half = len(refs) // 2 - 1
    folded, out = refs[half : half + 2]
    folded[...] = from_own_order(sides[...], scratch)
    for source, target in zip(refs[:half], refs[half + 2 :]):
        target[...] = source[:, 0]
    for level, inv, panel, at in ((0, inv5, panel5, 3), (1, inv6, panel6, 0), (2, inv7, None, 2)):
        slot = 16 + level
        size = sizes[slot]
        row = pos[0] * 32 + lax.broadcasted_iota(jnp.int32, (32, 512), 0)
        column = lax.broadcasted_iota(jnp.int32, (32, 512), 1)
        out[at] = jnp.where((row < size) & (column < size), inv[0, 0], 0.0)
        for d in range(2 - level):
            out[at + 1 + d] = panel[0, 0, d] * pattern[slot * 7 + d].astype(jnp.float32)


def choose_kernel(pos, parent, pattern, sizes, low, middle, high, out):
    for c in range(4):
        out[3 * c : 3 * c + 3] = low[c]
    for c in range(2):
        out[12 + 2 * c : 14 + 2 * c] = middle[c]
    out[16:17] = high[0]


def turn_kernel(pos, parent, pattern, sizes, p5, p6, p7, rhs, out, scratch):
    at = 0
    for level, ref in enumerate((p5, p6, p7)):
        for j in range(4 >> level):
            piece = ref[j] - jnp.where(pos[1] == j, rhs[16 + level], 0.0)
            scratch[pl.ds(at * 32, 16), :] = piece
            scratch[pl.ds(at * 32 + 16, 16), :] = pltpu.roll(piece, 64, 1)
            at += 1
    scratch[pl.ds(224, 32), :] = jnp.zeros((32, 128), jnp.float32)
    turned = scratch[pl.ds(0, 256), :].T
    for z in range(8):
        out[2 * z] = turned[8 * z : 8 * z + 8]
        out[2 * z + 1] = turned[8 * z : 8 * z + 8]


def sum_kernel(pos, parent, pattern, sizes, recv, out):
    total = recv[0]
    for i in range(1, 16):
        total = total + recv[i]
    for i in range(16):
        out[i] = total


def place(own, y, level, pos):
    lanes = pltpu.roll(y, (256 - (pos[0] % 8) * 32) % 256, 1)[:, :128]
    lane = lax.broadcasted_iota(jnp.int32, (8, 128), 1) // 32
    return jnp.where(lane == level, pltpu.roll(lanes, level * 32, 1), own)


def low_kernel(pos, parent, pattern, sizes, recv, block, out, left, z):
    step = pl.program_id(0)

    @pl.when(step == 0)
    def _():
        lane = lax.broadcasted_iota(jnp.int32, (8, 128), 1) // 32
        for n in range(7):
            for g in range(4):
                whole = jnp.zeros((8, 128), jnp.float32)
                for i in range(4):
                    piece = recv[4 * g + i][:, (n // 4) * 128 : (n // 4 + 1) * 128]
                    turned = pltpu.roll(piece, ((i - n % 4) * 32) % 128, 1)
                    whole = jnp.where(lane == i, turned, whole)
                if n < 4:
                    z[n, :, g * 128 : (g + 1) * 128] = -whole
                else:
                    left[n - 4, :, g * 128 : (g + 1) * 128] = jnp.where(pos[1] % 2 == 0, -whole, 0.0)
        out[...] = jnp.zeros_like(out)

    def matrix(i):
        return block[:, i].reshape(512, 256)

    solved = [dot3(z[2 * step + k], matrix(3 * k), ((1,), (0,))) for k in range(2)]
    near = [dot3(solved[k], matrix(3 * k + 1), ((1,), (1,))) for k in range(2)]
    far = [dot3(solved[k], matrix(3 * k + 2), ((1,), (1,))) for k in range(2)]
    left[2] = left[2] - (far[0] + far[1])
    for k in range(2):
        node = 2 * step + k
        out[node] = place(out[node], solved[k], 0, pos)
        target = parent[NODE_BASE[TOP] + node] - NODE_BASE[TOP + 1]
        left[target] = left[target] - near[k]


def middle_kernel(pos, parent, pattern, sizes, left, other, before, block, out, after):
    def matrix(i):
        return block[:, i].reshape(512, 256)

    solved = [dot3(left[k] + other[k], matrix(2 * k), ((1,), (0,))) for k in range(2)]
    update = [dot3(solved[k], matrix(2 * k + 1), ((1,), (1,))) for k in range(2)]
    out[...] = before[...]
    for k in range(2):
        out[k] = place(before[k], solved[k], 1, pos)
    after[...] = left[2] - (update[0] + update[1])


def root_kernel(pos, parent, pattern, sizes, left, other, before, block, out):
    solved = dot3(left[...] + other[...], block[:, 0].reshape(512, 256), ((1,), (0,)))
    out[...] = before[...]
    out[0] = place(before[0], solved, 2, pos)


def last_kernel(pos, parent, pattern, sizes, recv, *refs):
    *parts, out, scratch = refs
    columns = jnp.concatenate([recv[2 * i + pos[0] // 8] for i in range(8)], 0)
    turned = jnp.concatenate([columns, columns], 0).T
    parts = [ref[...] for ref in parts] + [fold(turned[:96])]
    out[...] = to_own_order(jnp.concatenate(parts, 0), scratch)


def on_device(right_side, inverse_rows, panels, pattern, node_sizes, parent):
    pos = jnp.stack([lax.axis_index("prow"), lax.axis_index("pcol")]).astype(jnp.int32)
    natural = right_side.reshape(19, 16, 128)
    scalars = jnp.concatenate([pos, parent, pattern.reshape(-1), node_sizes.reshape(-1)])
    slot_counts = [max(1, n // 16) for n in NODES]
    bases = [sum(slot_counts[:h]) for h in range(LEVELS)]
    def call(kernel, scratch, grid, in_specs, out_specs, out_shape, aliases, *args):
        args = [pltpu.with_memory_space_constraint(a, pltpu.HBM) if a.size > 1 << 18 and a.dtype == f32 else a for a in args]
        return pl.pallas_call(
            functools.partial(with_parts, kernel),
            grid_spec=pltpu.PrefetchScalarGridSpec(
                num_scalar_prefetch=1,
                grid=grid,
                in_specs=in_specs,
                out_specs=out_specs,
                scratch_shapes=scratch,
            ),
            out_shape=out_shape,
            input_output_aliases={k + 1: v for k, v in aliases.items()},
            compiler_params=pltpu.CompilerParams(vmem_limit_bytes=VMEM_LIMIT),
        )(scalars, *args)

    def exchange(x, axis):
        return lax.all_to_all(x, axis, 0, 0, tiled=True)

    f32 = jnp.float32
    pending = []
    recv = None
    outputs = []
    cuts = [bases[h] for h in CUTS]
    rows = pl.BlockSpec((6, 32, 512), lambda *_: (0, 0, 0))

    def block(*lead):
        def spec(n, slot):
            return pl.BlockSpec((1, 1) + (n,) * len(lead) + (32, 512), lambda *_: (slot, 0) + lead + (0, 0))

        return spec

    spans = list(zip(cuts[:-1], cuts[1:]))
    all_sides = pl.BlockSpec((19, 16, 128), lambda *_: (0, 0, 0))
    tall = [pltpu.VMEM((19 * 32, 128), f32)]
    rhs, top, *wholes = call(
        pack_kernel,
        tall,
        (1,),
        [all_sides, block()(0, 16), block()(0, 17), block()(0, 18), block(0)(2, 16), block(0)(1, 17)]
        + [pl.BlockSpec((hi - lo, 1, 32, 512), lambda *_, i=lo // (hi - lo): (i, 0, 0, 0)) for lo, hi in spans],
        [all_sides, rows] + [pl.BlockSpec((hi - lo, 32, 512), lambda *_: (0, 0, 0)) for lo, hi in spans],
        [jax.ShapeDtypeStruct((19, 16, 128), f32), jax.ShapeDtypeStruct((6, 32, 512), f32)]
        + [jax.ShapeDtypeStruct((hi - lo, 32, 512), f32) for lo, hi in spans],
        {},
        natural,
        *[inverse_rows] * 3,
        *[panels] * 2,
        *[inverse_rows] * len(spans),
    )
    top = lax.all_gather(top, "pcol", axis=0)
    for height in range(TOP):
        count = slot_counts[height]
        base = bases[height]
        reach = LEVELS - 1 - height
        info = (height, count, base)
        whole = height >= GATHER_FROM
        piece = jax.ShapeDtypeStruct((16, count, 16, 128), f32)
        own = jax.ShapeDtypeStruct((count, 16, 128), f32)
        every = pl.BlockSpec((16, count, 16, 128), lambda *_: (0, 0, 0, 0))
        every_own = pl.BlockSpec((count, 16, 128), lambda *_: (0, 0, 0))
        rhs_all = pl.BlockSpec((count, 16, 128), lambda *_, b=base // count: (b, 0, 0))
        if whole:
            z = call(
                functools.partial(residue_kernel, *info), [], (1,), [every, rhs_all], every, piece, {}, recv, rhs
            )
            gathered = exchange(z, "prow")
            lo, inverse = [pair for pair in inverses if pair[0] <= base][-1]
            inverse, _ = lax.optimization_barrier((inverse, z))
            inverse = call(
                split_inverse_kernel,
                [],
                (count,),
                [pl.BlockSpec((16, 1, 32, 512), lambda s, *_, b=base - lo: (0, b + s, 0, 0))],
                [pl.BlockSpec((1, 512, 512), lambda s, *_: (s, 0, 0))] * 2,
                [jax.ShapeDtypeStruct((count, 512, 512), jnp.bfloat16)] * 2,
                {},
                inverse,
            )
        else:
            per = min(4, count)
            in_specs = [
                pl.BlockSpec((per, 16, 128), lambda s, *_, b=base // per: (b + s, 0, 0)),
                pl.BlockSpec((per, 1, 32, 512), lambda s, *_, b=base // per: (b + s, 0, 0, 0)),
            ]
            args = [natural, inverse_rows]
            if height > 0:
                in_specs = [pl.BlockSpec((recv.shape[0], per, 16, 128), lambda s, *_: (0, s, 0, 0))] + in_specs
                args = [recv] + args
            some = pl.BlockSpec((16, per, 16, 128), lambda s, *_: (0, s, 0, 0))
            kernel = functools.partial(partial_kernel, *info)
            parts = call(kernel, [pltpu.VMEM((per * 32, 128), f32)], (count // per,), in_specs, some, piece, {}, *args)
            parts = exchange(parts, "prow")
            if height == 0:
                wholes, parts = lax.optimization_barrier((wholes, parts))
                inverses = [(lo, lax.all_gather(part, "prow", axis=0)) for lo, part in zip(cuts[:-1], wholes)]
            y, sol = call(
                functools.partial(solved_kernel, *info), [], (1,), [every], [every, every_own], [piece, own], {}, parts
            )
            outputs.append(sol)
            gathered = exchange(y, "prow")
        if height == 1:
            chosen_from, _ = lax.optimization_barrier((top, y))
            halves = [(4, 3, 0, 1), (2, 2, 0, 0), (1, 1, 0, 2)]
            chosen = call(
                choose_kernel,
                [],
                (1,),
                [
                    pl.BlockSpec((m, n, 32, 256), lambda _, info, a=a, b=b: (a, b, 0, info[1] % 2))
                    for m, n, a, b in halves
                ],
                pl.BlockSpec((17, 32, 256), lambda *_: (0, 0, 0)),
                jax.ShapeDtypeStruct((17, 32, 256), f32),
                {},
                *[chosen_from] * 3,
            )
            top = lax.all_gather(chosen, "prow", axis=0)
        steps = [(0, 1), (1, reach)] if height + 1 < TOP else [(0, reach)]
        updated = []
        given, source = gathered, "z" if whole else "y"
        for start, end in steps:
            per = 1 if source == "z" else min(2, count)
            in_specs = [pl.BlockSpec((16, per, 16, 128), lambda s, *_: (0, s, 0, 0))]
            if source == "t":
                in_specs = [pl.BlockSpec((per, 64, 512), lambda s, *_: (s, 0, 0))]
            args = [given]
            out_specs, out_shape = [], []
            if source == "z":
                in_specs += [pl.BlockSpec((1, 512, 512), lambda s, *_: (s, 0, 0))] * 2
                args += inverse
                out_specs.append(pl.BlockSpec((1, 16, 128), lambda s, *_: (s, 0, 0)))
                out_shape.append(own)
                if end < reach:
                    out_specs.append(pl.BlockSpec((1, 64, 512), lambda s, *_: (s, 0, 0)))
                    out_shape.append(jax.ShapeDtypeStruct((count, 64, 512), f32))
            in_specs.append(
                pl.BlockSpec((per, 1, end, 32, 512), lambda s, *_, b=base // per: (b + s, 0, 0, 0, 0))
            )
            args.append(panels)
            aliases = {}
            for d in range(start, end):
                shape = (16 * slot_counts[height + 1 + d], 16, 128)
                spec = pl.BlockSpec(shape, lambda *_: (0, 0, 0))
                if height > 0:
                    aliases[len(in_specs)] = len(out_specs)
                    in_specs.append(spec)
                    args.append(pending[d])
                out_specs.append(spec)
                out_shape.append(jax.ShapeDtypeStruct(shape, f32))
            results = call(
                functools.partial(spread_kernel, *info, source, start, end),
                SCRATCH,
                (count // per,),
                in_specs,
                out_specs,
                out_shape,
                aliases,
                *args,
            )
            results = list(results)
            if source == "z":
                outputs.append(results.pop(0))
                if end < reach:
                    given, source = results.pop(0), "t"
            updated += results
        results = updated
        if height + 1 < TOP:
            following = slot_counts[height + 1]
            pending = results[1:]
            if height == 0:
                half = pl.BlockSpec((32, 16, 128), lambda *_: (0, 0, 0))
                there = lax.ppermute(results[0][32:], "pcol", [(i, i ^ 1) for i in range(16)])
                joined = call(
                    join_kernel,
                    [],
                    (1,),
                    [half, half],
                    pl.BlockSpec((8, 4, 16, 128), lambda *_: (0, 0, 0, 0)),
                    jax.ShapeDtypeStruct((8, 4, 16, 128), f32),
                    {},
                    results[0],
                    there,
                )
                recv = lax.all_to_all(
                    joined,
                    "pcol",
                    0,
                    0,
                    tiled=True,
                    axis_index_groups=[[core + 2 * z for z in range(8)] for core in range(2)],
                )
            else:
                recv = exchange(results[0].reshape(16, following, 16, 128), "pcol")
    many = pl.BlockSpec((16, 16, 128), lambda *_: (0, 0, 0))
    sides = pl.BlockSpec((16, 8, 256), lambda *_: (0, 0, 0))
    sides_shape = jax.ShapeDtypeStruct((16, 8, 256), f32)
    turned = call(
        turn_kernel,
        [pltpu.VMEM((256, 128), f32)],
        (1,),
        [many] * 3 + [pl.BlockSpec((19, 16, 128), lambda *_: (0, 0, 0))],
        sides,
        sides_shape,
        {},
        *results,
        rhs,
    )
    total = call(sum_kernel, [], (1,), [sides], sides, sides_shape, {}, exchange(turned, "pcol"))
    gathered = exchange(total, "prow")
    def halves_from(start, n):
        return [pl.BlockSpec((16, n, 32, 256), lambda s, *_: (0, start // n + s, 0, 0))]

    def whole_of(*shape):
        return pl.BlockSpec(shape, lambda *_: (0,) * len(shape)), jax.ShapeDtypeStruct(shape, f32)

    def other_core(x):
        return lax.ppermute(x, "pcol", [(i, i ^ 1) for i in range(16)])

    found, found_shape = whole_of(16, 8, 128)
    three, three_shape = whole_of(3, 8, 512)
    single, single_shape = whole_of(8, 512)
    solved, left = call(
        low_kernel,
        [pltpu.VMEM((4, 8, 512), f32)],
        (2,),
        [sides] + halves_from(0, 6),
        [found, three],
        [found_shape, three_shape],
        {},
        gathered,
        top,
    )
    solved, left = call(
        middle_kernel,
        [],
        (1,),
        [three, three, found] + halves_from(12, 4),
        [found, single],
        [found_shape, single_shape],
        {},
        left,
        other_core(left),
        solved,
        top,
    )
    solved = call(
        root_kernel,
        [],
        (1,),
        [single, single, found] + halves_from(16, 1),
        found,
        found_shape,
        {},
        left,
        other_core(left),
        solved,
        top,
    )
    out = call(
        last_kernel,
        tall,
        (1,),
        [found] + [pl.BlockSpec(x.shape, lambda *_: (0, 0, 0)) for x in outputs],
        all_sides,
        jax.ShapeDtypeStruct((19, 16, 128), f32),
        {},
        exchange(solved, "pcol"),
        *outputs,
    )
    return out.reshape(19, 1, 2048)


def solution(mesh):
    in_specs = (
        P(None, "pcol", "prow"),
        P(None, "pcol", "prow", None),
        P(None, "pcol", None, "prow", None),
        P(None, "pcol", None),
        P(None, "pcol"),
        P(),
    )
    out_specs = P(None, "pcol", "prow")
    return jax.shard_map(
        on_device, mesh=mesh, in_specs=in_specs, out_specs=out_specs, check_vma=False
    )
```

```python
import functools

import jax
import jax.numpy as jnp
from jax import lax
from jax.experimental import pallas as pl
from jax.experimental.pallas import tpu as pltpu
from jax.sharding import PartitionSpec as P

LEVELS = 8
LEAVES = 128
GATHER_FROM = 2
CUTS = (2, 5)
SCRATCH = [pltpu.VMEM((192, 512), jnp.float32)]
PAIRED = 2
TOP = 5
VMEM_LIMIT = 24 * 1024 * 1024

NODES = [LEAVES >> h for h in range(LEVELS)]
NODE_BASE = [2 * LEAVES - 2 * (LEAVES >> h) for h in range(LEVELS)]


class Part:
    def __init__(self, ref, start):
        self.ref, self.start = ref, start

    def __getitem__(self, index):
        return self.ref[index + self.start]


def with_parts(kernel, *refs):
    return kernel(*[Part(refs[0], start) for start in (0, 2, 256, 389)], *refs[1:])


def split(x):
    high = x.astype(jnp.bfloat16)
    low = (x - high.astype(jnp.float32)).astype(jnp.bfloat16)
    return high, low


def dot3(a, b, dims):
    bh, bl = b if isinstance(b, tuple) else split(b)
    dot = functools.partial(
        lax.dot_general, dimension_numbers=(dims, ((), ())), preferred_element_type=jnp.float32
    )
    n = a.shape[0]
    if n <= 64 and dims[0] == (1,):
        high = a.astype(jnp.bfloat16).astype(jnp.float32)
        both = jnp.concatenate([high, a - high], 0).astype(jnp.bfloat16)
        first = dot(both, bh)
        second = dot(high.astype(jnp.bfloat16), bl)
        return first[:n] + (first[n:] + second)
    ah, al = split(a)
    return dot(ah, bh) + (dot(ah, bl) + dot(al, bh))


def lower(shape):
    return lax.broadcasted_iota(jnp.int32, shape, len(shape) - 1) < 64


def from_own_order(x, scratch):
    n = x.shape[0]
    x = x.reshape(n * 16, 128)
    scratch[pl.ds(0, n * 16, stride=2), :] = x
    scratch[pl.ds(1, n * 16, stride=2), :] = pltpu.roll(x, 64, 1)
    rows = scratch[pl.ds(0, n * 32), :].reshape(n, 2, 16, 128)
    other = pltpu.roll(rows[:, 1].reshape(n * 16, 128), 64, 1).reshape(n, 16, 128)
    return jnp.where(lower((n, 16, 128)), rows[:, 0], other)


def to_own_order(x, scratch):
    n = x.shape[0]
    turned = pltpu.roll(x.reshape(n * 16, 128), 64, 1).reshape(n, 1, 16, 128)
    scratch[pl.ds(0, n * 32), :] = jnp.concatenate([x.reshape(n, 1, 16, 128), turned], 1).reshape(n * 32, 128)
    even = scratch[pl.ds(0, n * 16, stride=2), :]
    odd = pltpu.roll(scratch[pl.ds(1, n * 16, stride=2), :], 64, 1)
    return jnp.where(lower((n * 16, 128)), even, odd).reshape(n, 16, 128)


def fold(x):
    n = x.shape[0] // 32
    x = x.reshape(n, 2, 16, 128)
    return jnp.where(lower((n, 16, 128)), x[:, 0], x[:, 1])


def own_mask(pos, sizes, slot, local, nodes):
    row = lax.broadcasted_iota(jnp.int32, (16, 128), 0)
    lane = lax.broadcasted_iota(jnp.int32, (16, 128), 1)
    row_id = pos[0] * 32 + row + 16 * (lane >= 64).astype(jnp.int32)
    limit = jnp.where(local * 16 + pos[1] < nodes, sizes[slot], 0)
    return row_id < limit


def residue_kernel(height, slots, slot_base, pos, parent, pattern, sizes, recv, rhs, out):
    for s in range(slots):
        total = recv[0, s]
        for i in range(1, recv.shape[0]):
            total = total + recv[i, s]
        keep = own_mask(pos, sizes, slot_base + s, s, NODES[height])
        z = jnp.where(keep, rhs[s] - total, 0.0)
        for i in range(16):
            out[i, s] = z


def partial_kernel(height, slots, slot_base, pos, parent, pattern, sizes, *refs):
    recv = None
    if height > 0:
        recv, *refs = refs
    rhs, inverse, out, scratch = refs
    low = lower((16, 128))
    sides = from_own_order(rhs[...], scratch)
    for i in range(rhs.shape[0]):
        s = pl.program_id(0) * rhs.shape[0] + i
        z = sides[i]
        if recv is not None:
            total = recv[0, i]
            for k in range(1, recv.shape[0]):
                total = total + recv[k, i]
            z = z - total
        keep = own_mask(pos, sizes, slot_base + s, s, NODES[height])
        z = jnp.where(keep, z, 0.0)
        turned = pltpu.roll(z, 64, 1)
        twice = jnp.concatenate([jnp.where(low, z, turned), jnp.where(low, turned, z)], 0)
        out[:, i] = fold(dot3(inverse[i, 0], twice, ((0,), (0,))))


def solved_kernel(height, slots, slot_base, pos, parent, pattern, sizes, recv, out, sol):
    for s in range(slots):
        total = recv[0, s]
        for i in range(1, 16):
            total = total + recv[i, s]
        keep = own_mask(pos, sizes, slot_base + s, s, NODES[height])
        y = jnp.where(keep, total, 0.0)
        sol[s] = y
        for i in range(16):
            out[i, s] = y


def spread_kernel(height, slots, slot_base, source, first, end, pos, parent, pattern, sizes, *refs):
    refs = list(refs)
    given = refs.pop(0)
    inverse = refs.pop(0) if source == "z" else None
    panels = refs.pop(0)
    before = [refs.pop(0) for _ in range(first, end)] if height > 0 else []
    sol = refs.pop(0) if source == "z" else None
    kept = refs.pop(0) if source == "z" and end < LEVELS - 1 - height else None
    after = [refs.pop(0) for _ in range(first, end)]
    scratch = refs.pop(0)

    @pl.when(pl.program_id(0) == 0)
    def _():
        for i, ref in enumerate(after):
            ref[...] = before[i][...] if before else jnp.zeros_like(ref)

    for k in range(panels.shape[0]):
        s = pl.program_id(0) * panels.shape[0] + k
        slot = slot_base + s
        if source == "z":
            turned = given[:, k].reshape(256, 128).T
            z_t = jnp.concatenate([turned[:64], turned[64:]], 1)
            y_t = dot3(z_t, (inverse[k, :512], inverse[k, 512:]), ((1,), (0,)))
            limit = sizes[slot]
            y_t = jnp.where(lax.broadcasted_iota(jnp.int32, (64, 512), 1) < limit, y_t, 0.0)
            scratch[pl.ds(0, 64), :] = y_t
            lanes = scratch[pl.ds(0, 64), pl.ds(pl.multiple_of(pos[0] // 4 * 128, 128), 128)]
            own = jnp.concatenate([lanes, lanes], 0).T
            scratch[pl.ds(64, 128), pl.ds(0, 128)] = own
            own = scratch[pl.ds(pl.multiple_of(64 + pos[0] % 4 * 32, 32), 32), pl.ds(0, 128)]
            sol[k] = fold(own)[0]
            if kept is not None:
                kept[k] = y_t
        elif source == "t":
            y_t = given[k]
        block = panels[k, 0, first:end].reshape((end - first) * 32, 512)
        if source == "y":
            x = given[:, k]
            turned = pltpu.roll(x.reshape(256, 128), 64, 1).reshape(16, 16, 128)
            low = lower((16, 16, 128))
            halves = [jnp.where(low, x, turned)[:, None], jnp.where(low, turned, x)[:, None]]
            y = jnp.concatenate(halves, 1).reshape(512, 128)
            update = fold(dot3(block, y, ((1,), (0,))))
        else:
            update = fold(dot3(block, jnp.concatenate([y_t, y_t], 0), ((1,), (1,))))
        node = NODE_BASE[height] + jnp.minimum(s * 16 + pos[1], NODES[height] - 1)
        for d in range(end):
            node = parent[node]
            if d < first:
                continue
            target = height + 1 + d
            j = node - NODE_BASE[target]
            many = max(1, NODES[target] // 16)
            if target <= PAIRED:
                where = ((j + pos[1]) % 2 * 8 + j % 16 // 2) * many + j // 16
            else:
                where = (j % 16) * many + j // 16
            scale = pattern[slot * 7 + d].astype(jnp.float32)
            after[d - first][where] += scale * update[d - first]


def split_inverse_kernel(pos, parent, pattern, sizes, inverse, both):
    rows = inverse[:, 0].reshape(16, 2, 16, 512)
    rows = jnp.concatenate([rows[:, 0].reshape(256, 512), rows[:, 1].reshape(256, 512)], 0)
    both[0, :512], both[0, 512:] = split(rows)


def join_kernel(pos, parent, pattern, sizes, here, there, out):
    out[...] = (here[...] + there[...]).reshape(out.shape)


def pack_kernel(pos, parent, pattern, sizes, sides, inv5, inv6, inv7, panel5, panel6, *refs):
    *refs, scratch = refs
    half = len(refs) // 2 - 1
    folded, out = refs[half : half + 2]
    folded[...] = from_own_order(sides[...], scratch)
    for source, target in zip(refs[:half], refs[half + 2 :]):
        target[...] = source[:, 0]
    for level, inv, panel, at in ((0, inv5, panel5, 3), (1, inv6, panel6, 0), (2, inv7, None, 2)):
        slot = 16 + level
        size = sizes[slot]
        row = pos[0] * 32 + lax.broadcasted_iota(jnp.int32, (32, 512), 0)
        column = lax.broadcasted_iota(jnp.int32, (32, 512), 1)
        out[at] = jnp.where((row < size) & (column < size), inv[0, 0], 0.0)
        for d in range(2 - level):
            out[at + 1 + d] = panel[0, 0, d] * pattern[slot * 7 + d].astype(jnp.float32)


def choose_kernel(pos, parent, pattern, sizes, low, middle, high, out):
    for c in range(4):
        out[3 * c : 3 * c + 3] = low[c]
    for c in range(2):
        out[12 + 2 * c : 14 + 2 * c] = middle[c]
    out[16:17] = high[0]


def turn_kernel(pos, parent, pattern, sizes, p5, p6, p7, rhs, out, scratch):
    at = 0
    for level, ref in enumerate((p5, p6, p7)):
        for j in range(4 >> level):
            piece = ref[j] - jnp.where(pos[1] == j, rhs[16 + level], 0.0)
            scratch[pl.ds(at * 32, 16), :] = piece
            scratch[pl.ds(at * 32 + 16, 16), :] = pltpu.roll(piece, 64, 1)
            at += 1
    scratch[pl.ds(224, 32), :] = jnp.zeros((32, 128), jnp.float32)
    turned = scratch[pl.ds(0, 256), :].T
    for z in range(8):
        out[2 * z] = turned[8 * z : 8 * z + 8]
        out[2 * z + 1] = turned[8 * z : 8 * z + 8]


def sum_kernel(pos, parent, pattern, sizes, recv, out):
    total = recv[0]
    for i in range(1, 16):
        total = total + recv[i]
    for i in range(16):
        out[i] = total


def place(own, y, level, pos):
    lanes = pltpu.roll(y, (256 - (pos[0] % 8) * 32) % 256, 1)[:, :128]
    lane = lax.broadcasted_iota(jnp.int32, (8, 128), 1) // 32
    return jnp.where(lane == level, pltpu.roll(lanes, level * 32, 1), own)


def low_kernel(pos, parent, pattern, sizes, recv, block, out, left, z):
    step = pl.program_id(0)

    @pl.when(step == 0)
    def _():
        lane = lax.broadcasted_iota(jnp.int32, (8, 128), 1) // 32
        for n in range(7):
            for g in range(4):
                whole = jnp.zeros((8, 128), jnp.float32)
                for i in range(4):
                    piece = recv[4 * g + i][:, (n // 4) * 128 : (n // 4 + 1) * 128]
                    turned = pltpu.roll(piece, ((i - n % 4) * 32) % 128, 1)
                    whole = jnp.where(lane == i, turned, whole)
                if n < 4:
                    z[n, :, g * 128 : (g + 1) * 128] = -whole
                else:
                    left[n - 4, :, g * 128 : (g + 1) * 128] = jnp.where(pos[1] % 2 == 0, -whole, 0.0)
        out[...] = jnp.zeros_like(out)

    def matrix(i):
        return block[:, i].reshape(512, 256)

    solved = [dot3(z[2 * step + k], matrix(3 * k), ((1,), (0,))) for k in range(2)]
    near = [dot3(solved[k], matrix(3 * k + 1), ((1,), (1,))) for k in range(2)]
    far = [dot3(solved[k], matrix(3 * k + 2), ((1,), (1,))) for k in range(2)]
    left[2] = left[2] - (far[0] + far[1])
    for k in range(2):
        node = 2 * step + k
        out[node] = place(out[node], solved[k], 0, pos)
        target = parent[NODE_BASE[TOP] + node] - NODE_BASE[TOP + 1]
        left[target] = left[target] - near[k]


def middle_kernel(pos, parent, pattern, sizes, left, other, before, block, out, after):
    def matrix(i):
        return block[:, i].reshape(512, 256)

    solved = [dot3(left[k] + other[k], matrix(2 * k), ((1,), (0,))) for k in range(2)]
    update = [dot3(solved[k], matrix(2 * k + 1), ((1,), (1,))) for k in range(2)]
    out[...] = before[...]
    for k in range(2):
        out[k] = place(before[k], solved[k], 1, pos)
    after[...] = left[2] - (update[0] + update[1])


def root_kernel(pos, parent, pattern, sizes, left, other, before, block, out):
    solved = dot3(left[...] + other[...], block[:, 0].reshape(512, 256), ((1,), (0,)))
    out[...] = before[...]
    out[0] = place(before[0], solved, 2, pos)


def last_kernel(pos, parent, pattern, sizes, recv, *refs):
    *parts, out, scratch = refs
    columns = jnp.concatenate([recv[2 * i + pos[0] // 8] for i in range(8)], 0)
    turned = jnp.concatenate([columns, columns], 0).T
    parts = [ref[...] for ref in parts] + [fold(turned[:96])]
    out[...] = to_own_order(jnp.concatenate(parts, 0), scratch)


def on_device(right_side, inverse_rows, panels, pattern, node_sizes, parent):
    pos = jnp.stack([lax.axis_index("prow"), lax.axis_index("pcol")]).astype(jnp.int32)
    natural = right_side.reshape(19, 16, 128)
    scalars = jnp.concatenate([pos, parent, pattern.reshape(-1), node_sizes.reshape(-1)])
    slot_counts = [max(1, n // 16) for n in NODES]
    bases = [sum(slot_counts[:h]) for h in range(LEVELS)]
    def call(kernel, scratch, grid, in_specs, out_specs, out_shape, aliases, *args):
        args = [
            pltpu.with_memory_space_constraint(a, pltpu.HBM)
            if a.size > 1 << 18 and a.dtype == f32
            else a
            for a in args
        ]
        return pl.pallas_call(
            functools.partial(with_parts, kernel),
            grid_spec=pltpu.PrefetchScalarGridSpec(
                num_scalar_prefetch=1,
                grid=grid,
                in_specs=in_specs,
                out_specs=out_specs,
                scratch_shapes=scratch,
            ),
            out_shape=out_shape,
            input_output_aliases={k + 1: v for k, v in aliases.items()},
            compiler_params=pltpu.CompilerParams(vmem_limit_bytes=VMEM_LIMIT),
        )(scalars, *args)

    def exchange(x, axis):
        return lax.all_to_all(x, axis, 0, 0, tiled=True)

    f32 = jnp.float32
    pending = []
    recv = None
    outputs = []
    cuts = [bases[h] for h in CUTS]
    rows = pl.BlockSpec((6, 32, 512), lambda *_: (0, 0, 0))

    def block(*lead):
        def spec(n, slot):
            return pl.BlockSpec((1, 1) + (n,) * len(lead) + (32, 512), lambda *_: (slot, 0) + lead + (0, 0))

        return spec

    spans = list(zip(cuts[:-1], cuts[1:]))
    all_sides = pl.BlockSpec((19, 16, 128), lambda *_: (0, 0, 0))
    tall = [pltpu.VMEM((19 * 32, 128), f32)]
    rhs, top, *wholes = call(
        pack_kernel,
        tall,
        (1,),
        [all_sides, block()(0, 16), block()(0, 17), block()(0, 18), block(0)(2, 16), block(0)(1, 17)]
        + [pl.BlockSpec((hi - lo, 1, 32, 512), lambda *_, i=lo // (hi - lo): (i, 0, 0, 0)) for lo, hi in spans],
        [all_sides, rows] + [pl.BlockSpec((hi - lo, 32, 512), lambda *_: (0, 0, 0)) for lo, hi in spans],
        [jax.ShapeDtypeStruct((19, 16, 128), f32), jax.ShapeDtypeStruct((6, 32, 512), f32)]
        + [jax.ShapeDtypeStruct((hi - lo, 32, 512), f32) for lo, hi in spans],
        {},
        natural,
        *[inverse_rows] * 3,
        *[panels] * 2,
        *[inverse_rows] * len(spans),
    )
    top = lax.all_gather(top, "pcol", axis=0)
    for height in range(TOP):
        count = slot_counts[height]
        base = bases[height]
        reach = LEVELS - 1 - height
        info = (height, count, base)
        whole = height >= GATHER_FROM
        piece = jax.ShapeDtypeStruct((16, count, 16, 128), f32)
        own = jax.ShapeDtypeStruct((count, 16, 128), f32)
        every = pl.BlockSpec((16, count, 16, 128), lambda *_: (0, 0, 0, 0))
        every_own = pl.BlockSpec((count, 16, 128), lambda *_: (0, 0, 0))
        rhs_all = pl.BlockSpec((count, 16, 128), lambda *_, b=base // count: (b, 0, 0))
        if whole:
            z = call(
                functools.partial(residue_kernel, *info),
                [],
                (1,),
                [pl.BlockSpec(recv.shape, lambda *_: (0, 0, 0, 0)), rhs_all],
                every,
                piece,
                {},
                recv,
                rhs,
            )
            gathered = exchange(z, "prow")
            lo, inverse = [pair for pair in inverses if pair[0] <= base][-1]
            inverse, _ = lax.optimization_barrier((inverse, z))
            inverse = call(
                split_inverse_kernel,
                [],
                (count,),
                [pl.BlockSpec((16, 1, 32, 512), lambda s, *_, b=base - lo: (0, b + s, 0, 0))],
                pl.BlockSpec((1, 1024, 512), lambda s, *_: (s, 0, 0)),
                jax.ShapeDtypeStruct((count, 1024, 512), jnp.bfloat16),
                {},
                inverse,
            )
        else:
            per = min(4, count)
            in_specs = [
                pl.BlockSpec((per, 16, 128), lambda s, *_, b=base // per: (b + s, 0, 0)),
                pl.BlockSpec((per, 1, 32, 512), lambda s, *_, b=base // per: (b + s, 0, 0, 0)),
            ]
            args = [natural, inverse_rows]
            if height > 0:
                in_specs = [pl.BlockSpec((recv.shape[0], per, 16, 128), lambda s, *_: (0, s, 0, 0))] + in_specs
                args = [recv] + args
            some = pl.BlockSpec((16, per, 16, 128), lambda s, *_: (0, s, 0, 0))
            kernel = functools.partial(partial_kernel, *info)
            parts = call(kernel, [pltpu.VMEM((per * 32, 128), f32)], (count // per,), in_specs, some, piece, {}, *args)
            parts = exchange(parts, "prow")
            if height == 0:
                wholes, parts = lax.optimization_barrier((wholes, parts))
                inverses = [(lo, lax.all_gather(part, "prow", axis=0)) for lo, part in zip(cuts[:-1], wholes)]
            y, sol = call(
                functools.partial(solved_kernel, *info), [], (1,), [every], [every, every_own], [piece, own], {}, parts
            )
            outputs.append(sol)
            gathered = exchange(y, "prow")
        if height == 1:
            chosen_from, _ = lax.optimization_barrier((top, y))
            halves = [(4, 3, 0, 1), (2, 2, 0, 0), (1, 1, 0, 2)]
            chosen = call(
                choose_kernel,
                [],
                (1,),
                [
                    pl.BlockSpec((m, n, 32, 256), lambda _, info, a=a, b=b: (a, b, 0, info[1] % 2))
                    for m, n, a, b in halves
                ],
                pl.BlockSpec((17, 32, 256), lambda *_: (0, 0, 0)),
                jax.ShapeDtypeStruct((17, 32, 256), f32),
                {},
                *[chosen_from] * 3,
            )
            top = lax.all_gather(chosen, "prow", axis=0)
        steps = [(0, 1), (1, reach)] if height + 1 < TOP else [(0, reach)]
        updated = []
        given, source = gathered, "z" if whole else "y"
        for start, end in steps:
            per = 1 if source == "z" else min(2, count)
            in_specs = [pl.BlockSpec((16, per, 16, 128), lambda s, *_: (0, s, 0, 0))]
            if source == "t":
                in_specs = [pl.BlockSpec((per, 64, 512), lambda s, *_: (s, 0, 0))]
            args = [given]
            out_specs, out_shape = [], []
            if source == "z":
                in_specs.append(pl.BlockSpec((1, 1024, 512), lambda s, *_: (s, 0, 0)))
                args.append(inverse)
                out_specs.append(pl.BlockSpec((1, 16, 128), lambda s, *_: (s, 0, 0)))
                out_shape.append(own)
                if end < reach:
                    out_specs.append(pl.BlockSpec((1, 64, 512), lambda s, *_: (s, 0, 0)))
                    out_shape.append(jax.ShapeDtypeStruct((count, 64, 512), f32))
            in_specs.append(
                pl.BlockSpec((per, 1, end, 32, 512), lambda s, *_, b=base // per: (b + s, 0, 0, 0, 0))
            )
            args.append(panels)
            aliases = {}
            for d in range(start, end):
                shape = (16 * slot_counts[height + 1 + d], 16, 128)
                spec = pl.BlockSpec(shape, lambda *_: (0, 0, 0))
                if height > 0:
                    aliases[len(in_specs)] = len(out_specs)
                    in_specs.append(spec)
                    args.append(pending[d])
                out_specs.append(spec)
                out_shape.append(jax.ShapeDtypeStruct(shape, f32))
            results = call(
                functools.partial(spread_kernel, *info, source, start, end),
                SCRATCH,
                (count // per,),
                in_specs,
                out_specs,
                out_shape,
                aliases,
                *args,
            )
            results = list(results)
            if source == "z":
                outputs.append(results.pop(0))
                if end < reach:
                    given, source = results.pop(0), "t"
            updated += results
        results = updated
        if height + 1 < TOP:
            following = slot_counts[height + 1]
            pending = results[1:]
            if height < PAIRED:
                half = pl.BlockSpec((8 * following, 16, 128), lambda *_: (0, 0, 0))
                there = lax.ppermute(results[0][8 * following :], "pcol", [(i, i ^ 1) for i in range(16)])
                joined = call(
                    join_kernel,
                    [],
                    (1,),
                    [half, half],
                    pl.BlockSpec((8, following, 16, 128), lambda *_: (0, 0, 0, 0)),
                    jax.ShapeDtypeStruct((8, following, 16, 128), f32),
                    {},
                    results[0],
                    there,
                )
                recv = lax.all_to_all(
                    joined,
                    "pcol",
                    0,
                    0,
                    tiled=True,
                    axis_index_groups=[[core + 2 * z for z in range(8)] for core in range(2)],
                )
            else:
                recv = exchange(results[0].reshape(16, following, 16, 128), "pcol")
    many = pl.BlockSpec((16, 16, 128), lambda *_: (0, 0, 0))
    sides = pl.BlockSpec((16, 8, 256), lambda *_: (0, 0, 0))
    sides_shape = jax.ShapeDtypeStruct((16, 8, 256), f32)
    turned = call(
        turn_kernel,
        [pltpu.VMEM((256, 128), f32)],
        (1,),
        [many] * 3 + [pl.BlockSpec((19, 16, 128), lambda *_: (0, 0, 0))],
        sides,
        sides_shape,
        {},
        *results,
        rhs,
    )
    total = call(sum_kernel, [], (1,), [sides], sides, sides_shape, {}, exchange(turned, "pcol"))
    gathered = exchange(total, "prow")
    def halves_from(start, n):
        return [pl.BlockSpec((16, n, 32, 256), lambda s, *_: (0, start // n + s, 0, 0))]

    def whole_of(*shape):
        return pl.BlockSpec(shape, lambda *_: (0,) * len(shape)), jax.ShapeDtypeStruct(shape, f32)

    def other_core(x):
        return lax.ppermute(x, "pcol", [(i, i ^ 1) for i in range(16)])

    found, found_shape = whole_of(16, 8, 128)
    three, three_shape = whole_of(3, 8, 512)
    single, single_shape = whole_of(8, 512)
    solved, left = call(
        low_kernel,
        [pltpu.VMEM((4, 8, 512), f32)],
        (2,),
        [sides] + halves_from(0, 6),
        [found, three],
        [found_shape, three_shape],
        {},
        gathered,
        top,
    )
    solved, left = call(
        middle_kernel,
        [],
        (1,),
        [three, three, found] + halves_from(12, 4),
        [found, single],
        [found_shape, single_shape],
        {},
        left,
        other_core(left),
        solved,
        top,
    )
    solved = call(
        root_kernel,
        [],
        (1,),
        [single, single, found] + halves_from(16, 1),
        found,
        found_shape,
        {},
        left,
        other_core(left),
        solved,
        top,
    )
    out = call(
        last_kernel,
        tall,
        (1,),
        [found] + [pl.BlockSpec(x.shape, lambda *_: (0, 0, 0)) for x in outputs],
        all_sides,
        jax.ShapeDtypeStruct((19, 16, 128), f32),
        {},
        exchange(solved, "pcol"),
        *outputs,
    )
    return out.reshape(19, 1, 2048)


def solution(mesh):
    in_specs = (
        P(None, "pcol", "prow"),
        P(None, "pcol", "prow", None),
        P(None, "pcol", None, "prow", None),
        P(None, "pcol", None),
        P(None, "pcol"),
        P(),
    )
    out_specs = P(None, "pcol", "prow")
    return jax.shard_map(
        on_device, mesh=mesh, in_specs=in_specs, out_specs=out_specs, check_vma=False
    )
```

```python
import functools

import jax
import jax.numpy as jnp
from jax import lax
from jax.experimental import pallas as pl
from jax.experimental.pallas import tpu as pltpu
from jax.sharding import PartitionSpec as P

LEVELS = 8
LEAVES = 128
GATHER_FROM = 2
CUTS = (2, 5)
SCRATCH = [pltpu.VMEM((384, 512), jnp.float32)]
PAIRED = 2
TOP = 5
VMEM_LIMIT = 24 * 1024 * 1024

NODES = [LEAVES >> h for h in range(LEVELS)]
NODE_BASE = [2 * LEAVES - 2 * (LEAVES >> h) for h in range(LEVELS)]


class Part:
    def __init__(self, ref, start):
        self.ref, self.start = ref, start

    def __getitem__(self, index):
        return self.ref[index + self.start]


def with_parts(kernel, *refs):
    return kernel(*[Part(refs[0], start) for start in (0, 2, 256, 389)], *refs[1:])


def split(x):
    high = x.astype(jnp.bfloat16)
    low = (x - high.astype(jnp.float32)).astype(jnp.bfloat16)
    return high, low


def dot3(a, b, dims):
    bh, bl = b if isinstance(b, tuple) else split(b)
    dot = functools.partial(
        lax.dot_general, dimension_numbers=(dims, ((), ())), preferred_element_type=jnp.float32
    )
    n = a.shape[0]
    if n <= 64 and dims[0] == (1,):
        high = a.astype(jnp.bfloat16).astype(jnp.float32)
        both = jnp.concatenate([high, a - high], 0).astype(jnp.bfloat16)
        first = dot(both, bh)
        second = dot(high.astype(jnp.bfloat16), bl)
        return first[:n] + (first[n:] + second)
    ah, al = split(a)
    return dot(ah, bh) + (dot(ah, bl) + dot(al, bh))


def lower(shape):
    return lax.broadcasted_iota(jnp.int32, shape, len(shape) - 1) < 64


def from_own_order(x, scratch):
    n = x.shape[0]
    x = x.reshape(n * 16, 128)
    scratch[pl.ds(0, n * 16, stride=2), :] = x
    scratch[pl.ds(1, n * 16, stride=2), :] = pltpu.roll(x, 64, 1)
    rows = scratch[pl.ds(0, n * 32), :].reshape(n, 2, 16, 128)
    other = pltpu.roll(rows[:, 1].reshape(n * 16, 128), 64, 1).reshape(n, 16, 128)
    return jnp.where(lower((n, 16, 128)), rows[:, 0], other)


def to_own_order(x, scratch):
    n = x.shape[0]
    turned = pltpu.roll(x.reshape(n * 16, 128), 64, 1).reshape(n, 1, 16, 128)
    scratch[pl.ds(0, n * 32), :] = jnp.concatenate([x.reshape(n, 1, 16, 128), turned], 1).reshape(n * 32, 128)
    even = scratch[pl.ds(0, n * 16, stride=2), :]
    odd = pltpu.roll(scratch[pl.ds(1, n * 16, stride=2), :], 64, 1)
    return jnp.where(lower((n * 16, 128)), even, odd).reshape(n, 16, 128)


def fold(x):
    n = x.shape[0] // 32
    x = x.reshape(n, 2, 16, 128)
    return jnp.where(lower((n, 16, 128)), x[:, 0], x[:, 1])


def own_mask(pos, sizes, slot, local, nodes):
    row = lax.broadcasted_iota(jnp.int32, (16, 128), 0)
    lane = lax.broadcasted_iota(jnp.int32, (16, 128), 1)
    row_id = pos[0] * 32 + row + 16 * (lane >= 64).astype(jnp.int32)
    limit = jnp.where(local * 16 + pos[1] < nodes, sizes[slot], 0)
    return row_id < limit


def residue_kernel(height, slots, slot_base, pos, parent, pattern, sizes, recv, rhs, out):
    for s in range(slots):
        total = recv[0, s]
        for i in range(1, recv.shape[0]):
            total = total + recv[i, s]
        keep = own_mask(pos, sizes, slot_base + s, s, NODES[height])
        z = jnp.where(keep, rhs[s] - total, 0.0)
        for i in range(16):
            out[i, s] = z


def partial_kernel(height, slots, slot_base, pos, parent, pattern, sizes, *refs):
    recv = None
    if height > 0:
        recv, *refs = refs
    rhs, inverse, out, scratch = refs
    low = lower((16, 128))
    sides = from_own_order(rhs[...], scratch)
    for i in range(rhs.shape[0]):
        s = pl.program_id(0) * rhs.shape[0] + i
        z = sides[i]
        if recv is not None:
            total = recv[0, i]
            for k in range(1, recv.shape[0]):
                total = total + recv[k, i]
            z = z - total
        keep = own_mask(pos, sizes, slot_base + s, s, NODES[height])
        z = jnp.where(keep, z, 0.0)
        turned = pltpu.roll(z, 64, 1)
        twice = jnp.concatenate([jnp.where(low, z, turned), jnp.where(low, turned, z)], 0)
        out[:, i] = fold(dot3(inverse[i, 0], twice, ((0,), (0,))))


def solved_kernel(height, slots, slot_base, pos, parent, pattern, sizes, recv, out, sol):
    for s in range(slots):
        total = recv[0, s]
        for i in range(1, 16):
            total = total + recv[i, s]
        keep = own_mask(pos, sizes, slot_base + s, s, NODES[height])
        y = jnp.where(keep, total, 0.0)
        sol[s] = y
        for i in range(16):
            out[i, s] = y


def spread_kernel(height, slots, slot_base, source, first, end, pos, parent, pattern, sizes, *refs):
    refs = list(refs)
    given = refs.pop(0)
    inverse = refs.pop(0) if source == "z" else None
    panels = refs.pop(0)
    before = [refs.pop(0) for _ in range(first, end)] if height > 0 else []
    sol = refs.pop(0) if source == "z" else None
    kept = refs.pop(0) if source == "z" and end < LEVELS - 1 - height else None
    after = [refs.pop(0) for _ in range(first, end)]
    scratch = refs.pop(0)

    @pl.when(pl.program_id(0) == 0)
    def _():
        for i, ref in enumerate(after):
            ref[...] = before[i][...] if before else jnp.zeros_like(ref)

    for k in range(panels.shape[0]):
        s = pl.program_id(0) * panels.shape[0] + k
        slot = slot_base + s
        if source == "z":
            turned = given[:, k].reshape(256, 128).T
            z_t = jnp.concatenate([turned[:64], turned[64:]], 1)
            y_t = dot3(z_t, (inverse[k, :512], inverse[k, 512:]), ((1,), (0,)))
            limit = sizes[slot]
            y_t = jnp.where(lax.broadcasted_iota(jnp.int32, (64, 512), 1) < limit, y_t, 0.0)
            scratch[pl.ds(192 * k, 64), :] = y_t
            lanes = scratch[pl.ds(192 * k, 64), pl.ds(pl.multiple_of(pos[0] // 4 * 128, 128), 128)]
            own = jnp.concatenate([lanes, lanes], 0).T
            scratch[pl.ds(192 * k + 64, 128), pl.ds(0, 128)] = own
            own = scratch[pl.ds(pl.multiple_of(192 * k + 64 + pos[0] % 4 * 32, 32), 32), pl.ds(0, 128)]
            sol[k] = fold(own)[0]
            if kept is not None:
                kept[k] = y_t
        elif source == "t":
            y_t = given[k]
        block = panels[k, 0, first:end].reshape((end - first) * 32, 512)
        if source == "y":
            x = given[:, k]
            turned = pltpu.roll(x.reshape(256, 128), 64, 1).reshape(16, 16, 128)
            low = lower((16, 16, 128))
            halves = [jnp.where(low, x, turned)[:, None], jnp.where(low, turned, x)[:, None]]
            y = jnp.concatenate(halves, 1).reshape(512, 128)
            update = fold(dot3(block, y, ((1,), (0,))))
        else:
            update = fold(dot3(block, jnp.concatenate([y_t, y_t], 0), ((1,), (1,))))
        node = NODE_BASE[height] + jnp.minimum(s * 16 + pos[1], NODES[height] - 1)
        for d in range(end):
            node = parent[node]
            if d < first:
                continue
            target = height + 1 + d
            j = node - NODE_BASE[target]
            many = max(1, NODES[target] // 16)
            if target <= PAIRED:
                where = ((j + pos[1]) % 2 * 8 + j % 16 // 2) * many + j // 16
            else:
                where = (j % 16) * many + j // 16
            scale = pattern[slot * 7 + d].astype(jnp.float32)
            after[d - first][where] += scale * update[d - first]


def split_inverse_kernel(pos, parent, pattern, sizes, inverse, both):
    rows = inverse[:, 0].reshape(16, 2, 16, 512)
    rows = jnp.concatenate([rows[:, 0].reshape(256, 512), rows[:, 1].reshape(256, 512)], 0)
    both[0, :512], both[0, 512:] = split(rows)


def join_kernel(pos, parent, pattern, sizes, here, there, out):
    out[...] = (here[...] + there[...]).reshape(out.shape)


def pack_kernel(pos, parent, pattern, sizes, sides, inv5, inv6, inv7, panel5, panel6, *refs):
    *refs, scratch = refs
    half = len(refs) // 2 - 1
    folded, out = refs[half : half + 2]
    folded[...] = from_own_order(sides[...], scratch)
    for source, target in zip(refs[:half], refs[half + 2 :]):
        target[...] = source[:, 0]
    for level, inv, panel, at in ((0, inv5, panel5, 3), (1, inv6, panel6, 0), (2, inv7, None, 2)):
        slot = 16 + level
        size = sizes[slot]
        row = pos[0] * 32 + lax.broadcasted_iota(jnp.int32, (32, 512), 0)
        column = lax.broadcasted_iota(jnp.int32, (32, 512), 1)
        out[at] = jnp.where((row < size) & (column < size), inv[0, 0], 0.0)
        for d in range(2 - level):
            out[at + 1 + d] = panel[0, 0, d] * pattern[slot * 7 + d].astype(jnp.float32)


def choose_kernel(pos, parent, pattern, sizes, low, middle, high, out):
    for c in range(4):
        out[3 * c : 3 * c + 3] = low[c]
    for c in range(2):
        out[12 + 2 * c : 14 + 2 * c] = middle[c]
    out[16:17] = high[0]


def turn_kernel(pos, parent, pattern, sizes, p5, p6, p7, rhs, out, scratch):
    at = 0
    for level, ref in enumerate((p5, p6, p7)):
        for j in range(4 >> level):
            piece = ref[j] - jnp.where(pos[1] == j, rhs[16 + level], 0.0)
            scratch[pl.ds(at * 32, 16), :] = piece
            scratch[pl.ds(at * 32 + 16, 16), :] = pltpu.roll(piece, 64, 1)
            at += 1
    scratch[pl.ds(224, 32), :] = jnp.zeros((32, 128), jnp.float32)
    turned = scratch[pl.ds(0, 256), :].T
    for z in range(8):
        out[2 * z] = turned[8 * z : 8 * z + 8]
        out[2 * z + 1] = turned[8 * z : 8 * z + 8]


def sum_kernel(pos, parent, pattern, sizes, recv, out):
    total = recv[0]
    for i in range(1, 16):
        total = total + recv[i]
    for i in range(16):
        out[i] = total


def place(own, y, level, pos):
    lanes = pltpu.roll(y, (256 - (pos[0] % 8) * 32) % 256, 1)[:, :128]
    lane = lax.broadcasted_iota(jnp.int32, (8, 128), 1) // 32
    return jnp.where(lane == level, pltpu.roll(lanes, level * 32, 1), own)


def low_kernel(pos, parent, pattern, sizes, recv, block, out, left, z):
    step = pl.program_id(0)

    @pl.when(step == 0)
    def _():
        lane = lax.broadcasted_iota(jnp.int32, (8, 128), 1) // 32
        for n in range(7):
            for g in range(4):
                whole = jnp.zeros((8, 128), jnp.float32)
                for i in range(4):
                    piece = recv[4 * g + i][:, (n // 4) * 128 : (n // 4 + 1) * 128]
                    turned = pltpu.roll(piece, ((i - n % 4) * 32) % 128, 1)
                    whole = jnp.where(lane == i, turned, whole)
                if n < 4:
                    z[n, :, g * 128 : (g + 1) * 128] = -whole
                else:
                    left[n - 4, :, g * 128 : (g + 1) * 128] = jnp.where(pos[1] % 2 == 0, -whole, 0.0)
        out[...] = jnp.zeros_like(out)

    def matrix(i):
        return block[:, i].reshape(512, 256)

    solved = [dot3(z[2 * step + k], matrix(3 * k), ((1,), (0,))) for k in range(2)]
    near = [dot3(solved[k], matrix(3 * k + 1), ((1,), (1,))) for k in range(2)]
    far = [dot3(solved[k], matrix(3 * k + 2), ((1,), (1,))) for k in range(2)]
    left[2] = left[2] - (far[0] + far[1])
    for k in range(2):
        node = 2 * step + k
        out[node] = place(out[node], solved[k], 0, pos)
        target = parent[NODE_BASE[TOP] + node] - NODE_BASE[TOP + 1]
        left[target] = left[target] - near[k]


def middle_kernel(pos, parent, pattern, sizes, left, other, before, block, out, after):
    def matrix(i):
        return block[:, i].reshape(512, 256)

    solved = [dot3(left[k] + other[k], matrix(2 * k), ((1,), (0,))) for k in range(2)]
    update = [dot3(solved[k], matrix(2 * k + 1), ((1,), (1,))) for k in range(2)]
    out[...] = before[...]
    for k in range(2):
        out[k] = place(before[k], solved[k], 1, pos)
    after[...] = left[2] - (update[0] + update[1])


def root_kernel(pos, parent, pattern, sizes, left, other, before, block, out):
    solved = dot3(left[...] + other[...], block[:, 0].reshape(512, 256), ((1,), (0,)))
    out[...] = before[...]
    out[0] = place(before[0], solved, 2, pos)


def last_kernel(pos, parent, pattern, sizes, recv, *refs):
    *parts, out, scratch = refs
    columns = jnp.concatenate([recv[2 * i + pos[0] // 8] for i in range(8)], 0)
    turned = jnp.concatenate([columns, columns], 0).T
    parts = [ref[...] for ref in parts] + [fold(turned[:96])]
    out[...] = to_own_order(jnp.concatenate(parts, 0), scratch)


def on_device(right_side, inverse_rows, panels, pattern, node_sizes, parent):
    pos = jnp.stack([lax.axis_index("prow"), lax.axis_index("pcol")]).astype(jnp.int32)
    natural = right_side.reshape(19, 16, 128)
    scalars = jnp.concatenate([pos, parent, pattern.reshape(-1), node_sizes.reshape(-1)])
    slot_counts = [max(1, n // 16) for n in NODES]
    bases = [sum(slot_counts[:h]) for h in range(LEVELS)]
    def call(kernel, scratch, grid, in_specs, out_specs, out_shape, aliases, *args):
        args = [
            pltpu.with_memory_space_constraint(a, pltpu.HBM)
            if a is natural or (a.size > 1 << 18 and a.dtype == f32)
            else a
            for a in args
        ]
        return pl.pallas_call(
            functools.partial(with_parts, kernel),
            grid_spec=pltpu.PrefetchScalarGridSpec(
                num_scalar_prefetch=1,
                grid=grid,
                in_specs=in_specs,
                out_specs=out_specs,
                scratch_shapes=scratch,
            ),
            out_shape=out_shape,
            input_output_aliases={k + 1: v for k, v in aliases.items()},
            compiler_params=pltpu.CompilerParams(vmem_limit_bytes=VMEM_LIMIT),
        )(scalars, *args)

    def exchange(x, axis):
        return lax.all_to_all(x, axis, 0, 0, tiled=True)

    f32 = jnp.float32
    pending = []
    recv = None
    outputs = []
    cuts = [bases[h] for h in CUTS]
    rows = pl.BlockSpec((6, 32, 512), lambda *_: (0, 0, 0))

    def block(*lead):
        def spec(n, slot):
            return pl.BlockSpec((1, 1) + (n,) * len(lead) + (32, 512), lambda *_: (slot, 0) + lead + (0, 0))

        return spec

    spans = list(zip(cuts[:-1], cuts[1:]))
    all_sides = pl.BlockSpec((19, 16, 128), lambda *_: (0, 0, 0))
    tall = [pltpu.VMEM((19 * 32, 128), f32)]
    rhs, top, *wholes = call(
        pack_kernel,
        tall,
        (1,),
        [all_sides, block()(0, 16), block()(0, 17), block()(0, 18), block(0)(2, 16), block(0)(1, 17)]
        + [pl.BlockSpec((hi - lo, 1, 32, 512), lambda *_, i=lo // (hi - lo): (i, 0, 0, 0)) for lo, hi in spans],
        [all_sides, rows] + [pl.BlockSpec((hi - lo, 32, 512), lambda *_: (0, 0, 0)) for lo, hi in spans],
        [jax.ShapeDtypeStruct((19, 16, 128), f32), jax.ShapeDtypeStruct((6, 32, 512), f32)]
        + [jax.ShapeDtypeStruct((hi - lo, 32, 512), f32) for lo, hi in spans],
        {},
        natural,
        *[inverse_rows] * 3,
        *[panels] * 2,
        *[inverse_rows] * len(spans),
    )
    top = lax.all_gather(top, "pcol", axis=0)
    for height in range(TOP):
        count = slot_counts[height]
        base = bases[height]
        reach = LEVELS - 1 - height
        info = (height, count, base)
        whole = height >= GATHER_FROM
        piece = jax.ShapeDtypeStruct((16, count, 16, 128), f32)
        own = jax.ShapeDtypeStruct((count, 16, 128), f32)
        every = pl.BlockSpec((16, count, 16, 128), lambda *_: (0, 0, 0, 0))
        every_own = pl.BlockSpec((count, 16, 128), lambda *_: (0, 0, 0))
        rhs_all = pl.BlockSpec((count, 16, 128), lambda *_, b=base // count: (b, 0, 0))
        if whole:
            z = call(
                functools.partial(residue_kernel, *info),
                [],
                (1,),
                [pl.BlockSpec(recv.shape, lambda *_: (0, 0, 0, 0)), rhs_all],
                every,
                piece,
                {},
                recv,
                rhs,
            )
            gathered = exchange(z, "prow")
            lo, inverse = [pair for pair in inverses if pair[0] <= base][-1]
            inverse, _ = lax.optimization_barrier((inverse, z))
            inverse = call(
                split_inverse_kernel,
                [],
                (count,),
                [pl.BlockSpec((16, 1, 32, 512), lambda s, *_, b=base - lo: (0, b + s, 0, 0))],
                pl.BlockSpec((1, 1024, 512), lambda s, *_: (s, 0, 0)),
                jax.ShapeDtypeStruct((count, 1024, 512), jnp.bfloat16),
                {},
                inverse,
            )
        else:
            per = min(4, count)
            in_specs = [
                pl.BlockSpec((per, 16, 128), lambda s, *_, b=base // per: (b + s, 0, 0)),
                pl.BlockSpec((per, 1, 32, 512), lambda s, *_, b=base // per: (b + s, 0, 0, 0)),
            ]
            args = [natural, inverse_rows]
            if height > 0:
                in_specs = [pl.BlockSpec((recv.shape[0], per, 16, 128), lambda s, *_: (0, s, 0, 0))] + in_specs
                args = [recv] + args
            some = pl.BlockSpec((16, per, 16, 128), lambda s, *_: (0, s, 0, 0))
            kernel = functools.partial(partial_kernel, *info)
            parts = call(kernel, [pltpu.VMEM((per * 32, 128), f32)], (count // per,), in_specs, some, piece, {}, *args)
            parts = exchange(parts, "prow")
            if height == 0:
                wholes, parts = lax.optimization_barrier((wholes, parts))
                inverses = [(lo, lax.all_gather(part, "prow", axis=0)) for lo, part in zip(cuts[:-1], wholes)]
            y, sol = call(
                functools.partial(solved_kernel, *info), [], (1,), [every], [every, every_own], [piece, own], {}, parts
            )
            outputs.append(sol)
            gathered = exchange(y, "prow")
        if height == 1:
            chosen_from, _ = lax.optimization_barrier((top, y))
            halves = [(4, 3, 0, 1), (2, 2, 0, 0), (1, 1, 0, 2)]
            chosen = call(
                choose_kernel,
                [],
                (1,),
                [
                    pl.BlockSpec((m, n, 32, 256), lambda _, info, a=a, b=b: (a, b, 0, info[1] % 2))
                    for m, n, a, b in halves
                ],
                pl.BlockSpec((17, 32, 256), lambda *_: (0, 0, 0)),
                jax.ShapeDtypeStruct((17, 32, 256), f32),
                {},
                *[chosen_from] * 3,
            )
            top = lax.all_gather(chosen, "prow", axis=0)
        steps = [(0, 1), (1, reach)] if height + 1 < TOP else [(0, reach)]
        updated = []
        given, source = gathered, "z" if whole else "y"
        for start, end in steps:
            per = min(2, count)
            in_specs = [pl.BlockSpec((16, per, 16, 128), lambda s, *_: (0, s, 0, 0))]
            if source == "t":
                in_specs = [pl.BlockSpec((per, 64, 512), lambda s, *_: (s, 0, 0))]
            args = [given]
            out_specs, out_shape = [], []
            if source == "z":
                in_specs.append(pl.BlockSpec((per, 1024, 512), lambda s, *_: (s, 0, 0)))
                args.append(inverse)
                out_specs.append(pl.BlockSpec((per, 16, 128), lambda s, *_: (s, 0, 0)))
                out_shape.append(own)
                if end < reach:
                    out_specs.append(pl.BlockSpec((per, 64, 512), lambda s, *_: (s, 0, 0)))
                    out_shape.append(jax.ShapeDtypeStruct((count, 64, 512), f32))
            in_specs.append(
                pl.BlockSpec((per, 1, end, 32, 512), lambda s, *_, b=base // per: (b + s, 0, 0, 0, 0))
            )
            args.append(panels)
            aliases = {}
            for d in range(start, end):
                shape = (16 * slot_counts[height + 1 + d], 16, 128)
                spec = pl.BlockSpec(shape, lambda *_: (0, 0, 0))
                if height > 0:
                    aliases[len(in_specs)] = len(out_specs)
                    in_specs.append(spec)
                    args.append(pending[d])
                out_specs.append(spec)
                out_shape.append(jax.ShapeDtypeStruct(shape, f32))
            results = call(
                functools.partial(spread_kernel, *info, source, start, end),
                SCRATCH,
                (count // per,),
                in_specs,
                out_specs,
                out_shape,
                aliases,
                *args,
            )
            results = list(results)
            if source == "z":
                outputs.append(results.pop(0))
                if end < reach:
                    given, source = results.pop(0), "t"
            updated += results
        results = updated
        if height + 1 < TOP:
            following = slot_counts[height + 1]
            pending = results[1:]
            if height < PAIRED:
                half = pl.BlockSpec((8 * following, 16, 128), lambda *_: (0, 0, 0))
                there = lax.ppermute(results[0][8 * following :], "pcol", [(i, i ^ 1) for i in range(16)])
                joined = call(
                    join_kernel,
                    [],
                    (1,),
                    [half, half],
                    pl.BlockSpec((8, following, 16, 128), lambda *_: (0, 0, 0, 0)),
                    jax.ShapeDtypeStruct((8, following, 16, 128), f32),
                    {},
                    results[0],
                    there,
                )
                recv = lax.all_to_all(
                    joined,
                    "pcol",
                    0,
                    0,
                    tiled=True,
                    axis_index_groups=[[core + 2 * z for z in range(8)] for core in range(2)],
                )
            else:
                recv = exchange(results[0].reshape(16, following, 16, 128), "pcol")
    many = pl.BlockSpec((16, 16, 128), lambda *_: (0, 0, 0))
    sides = pl.BlockSpec((16, 8, 256), lambda *_: (0, 0, 0))
    sides_shape = jax.ShapeDtypeStruct((16, 8, 256), f32)
    turned = call(
        turn_kernel,
        [pltpu.VMEM((256, 128), f32)],
        (1,),
        [many] * 3 + [pl.BlockSpec((19, 16, 128), lambda *_: (0, 0, 0))],
        sides,
        sides_shape,
        {},
        *results,
        rhs,
    )
    total = call(sum_kernel, [], (1,), [sides], sides, sides_shape, {}, exchange(turned, "pcol"))
    gathered = exchange(total, "prow")
    def halves_from(start, n):
        return [pl.BlockSpec((16, n, 32, 256), lambda s, *_: (0, start // n + s, 0, 0))]

    def whole_of(*shape):
        return pl.BlockSpec(shape, lambda *_: (0,) * len(shape)), jax.ShapeDtypeStruct(shape, f32)

    def other_core(x):
        return lax.ppermute(x, "pcol", [(i, i ^ 1) for i in range(16)])

    found, found_shape = whole_of(16, 8, 128)
    three, three_shape = whole_of(3, 8, 512)
    single, single_shape = whole_of(8, 512)
    solved, left = call(
        low_kernel,
        [pltpu.VMEM((4, 8, 512), f32)],
        (2,),
        [sides] + halves_from(0, 6),
        [found, three],
        [found_shape, three_shape],
        {},
        gathered,
        top,
    )
    solved, left = call(
        middle_kernel,
        [],
        (1,),
        [three, three, found] + halves_from(12, 4),
        [found, single],
        [found_shape, single_shape],
        {},
        left,
        other_core(left),
        solved,
        top,
    )
    solved = call(
        root_kernel,
        [],
        (1,),
        [single, single, found] + halves_from(16, 1),
        found,
        found_shape,
        {},
        left,
        other_core(left),
        solved,
        top,
    )
    out = call(
        last_kernel,
        tall,
        (1,),
        [found] + [pl.BlockSpec(x.shape, lambda *_: (0, 0, 0)) for x in outputs],
        all_sides,
        jax.ShapeDtypeStruct((19, 16, 128), f32),
        {},
        exchange(solved, "pcol"),
        *outputs,
    )
    return out.reshape(19, 1, 2048)


def solution(mesh):
    in_specs = (
        P(None, "pcol", "prow"),
        P(None, "pcol", "prow", None),
        P(None, "pcol", None, "prow", None),
        P(None, "pcol", None),
        P(None, "pcol"),
        P(),
    )
    out_specs = P(None, "pcol", "prow")
    return jax.shard_map(
        on_device, mesh=mesh, in_specs=in_specs, out_specs=out_specs, check_vma=False
    )
```

```python
import functools

import jax
import jax.numpy as jnp
from jax import lax
from jax.experimental import pallas as pl
from jax.experimental.pallas import tpu as pltpu
from jax.sharding import PartitionSpec as P

LEVELS = 8
LEAVES = 128
GATHER_FROM = 2
CUTS = (2, 5)
SCRATCH = [pltpu.VMEM((384, 512), jnp.float32)]
PAIRED = 2
TOP = 5
VMEM_LIMIT = 24 * 1024 * 1024

NODES = [LEAVES >> h for h in range(LEVELS)]
NODE_BASE = [2 * LEAVES - 2 * (LEAVES >> h) for h in range(LEVELS)]


class Part:
    def __init__(self, ref, start):
        self.ref, self.start = ref, start

    def __getitem__(self, index):
        return self.ref[index + self.start]


def with_parts(kernel, *refs):
    return kernel(*[Part(refs[0], start) for start in (0, 2, 256, 389)], *refs[1:])


def split(x):
    high = x.astype(jnp.bfloat16)
    low = (x - high.astype(jnp.float32)).astype(jnp.bfloat16)
    return high, low


def dot3(a, b, dims):
    bh, bl = b if isinstance(b, tuple) else split(b)
    dot = functools.partial(
        lax.dot_general, dimension_numbers=(dims, ((), ())), preferred_element_type=jnp.float32
    )
    n = a.shape[0]
    if n <= 64 and dims[0] == (1,):
        high = a.astype(jnp.bfloat16).astype(jnp.float32)
        both = jnp.concatenate([high, a - high], 0).astype(jnp.bfloat16)
        first = dot(both, bh)
        second = dot(high.astype(jnp.bfloat16), bl)
        return first[:n] + (first[n:] + second)
    ah, al = split(a)
    return dot(ah, bh) + (dot(ah, bl) + dot(al, bh))


def lower(shape):
    return lax.broadcasted_iota(jnp.int32, shape, len(shape) - 1) < 64


def from_own_order(x, scratch):
    n = x.shape[0]
    x = x.reshape(n * 16, 128)
    scratch[pl.ds(0, n * 16, stride=2), :] = x
    scratch[pl.ds(1, n * 16, stride=2), :] = pltpu.roll(x, 64, 1)
    rows = scratch[pl.ds(0, n * 32), :].reshape(n, 2, 16, 128)
    other = pltpu.roll(rows[:, 1].reshape(n * 16, 128), 64, 1).reshape(n, 16, 128)
    return jnp.where(lower((n, 16, 128)), rows[:, 0], other)


def to_own_order(x, scratch):
    n = x.shape[0]
    turned = pltpu.roll(x.reshape(n * 16, 128), 64, 1).reshape(n, 1, 16, 128)
    scratch[pl.ds(0, n * 32), :] = jnp.concatenate([x.reshape(n, 1, 16, 128), turned], 1).reshape(n * 32, 128)
    even = scratch[pl.ds(0, n * 16, stride=2), :]
    odd = pltpu.roll(scratch[pl.ds(1, n * 16, stride=2), :], 64, 1)
    return jnp.where(lower((n * 16, 128)), even, odd).reshape(n, 16, 128)


def fold(x):
    n = x.shape[0] // 32
    x = x.reshape(n, 2, 16, 128)
    return jnp.where(lower((n, 16, 128)), x[:, 0], x[:, 1])


def own_mask(pos, sizes, slot, local, nodes):
    row = lax.broadcasted_iota(jnp.int32, (16, 128), 0)
    lane = lax.broadcasted_iota(jnp.int32, (16, 128), 1)
    row_id = pos[0] * 32 + row + 16 * (lane >= 64).astype(jnp.int32)
    limit = jnp.where(local * 16 + pos[1] < nodes, sizes[slot], 0)
    return row_id < limit


def residue_kernel(height, slots, slot_base, pos, parent, pattern, sizes, recv, rhs, out):
    for s in range(slots):
        total = recv[0, s]
        for i in range(1, recv.shape[0]):
            total = total + recv[i, s]
        keep = own_mask(pos, sizes, slot_base + s, s, NODES[height])
        z = jnp.where(keep, rhs[s] - total, 0.0)
        for i in range(16):
            out[i, s] = z


def partial_kernel(height, slots, slot_base, pos, parent, pattern, sizes, *refs):
    recv = None
    if height > 0:
        recv, *refs = refs
    rhs, inverse, out, scratch = refs
    low = lower((16, 128))
    sides = from_own_order(rhs[...], scratch)
    for i in range(rhs.shape[0]):
        s = pl.program_id(0) * rhs.shape[0] + i
        z = sides[i]
        if recv is not None:
            total = recv[0, i]
            for k in range(1, recv.shape[0]):
                total = total + recv[k, i]
            z = z - total
        keep = own_mask(pos, sizes, slot_base + s, s, NODES[height])
        z = jnp.where(keep, z, 0.0)
        turned = pltpu.roll(z, 64, 1)
        twice = jnp.concatenate([jnp.where(low, z, turned), jnp.where(low, turned, z)], 0)
        out[:, i] = fold(dot3(inverse[i, 0], twice, ((0,), (0,))))


def solved_kernel(height, slots, slot_base, pos, parent, pattern, sizes, recv, out, sol):
    for s in range(slots):
        total = recv[0, s]
        for i in range(1, 16):
            total = total + recv[i, s]
        keep = own_mask(pos, sizes, slot_base + s, s, NODES[height])
        y = jnp.where(keep, total, 0.0)
        sol[s] = y
        for i in range(16):
            out[i, s] = y


def spread_kernel(height, slots, slot_base, source, first, end, pos, parent, pattern, sizes, *refs):
    refs = list(refs)
    given = refs.pop(0)
    inverse = refs.pop(0) if source == "z" else None
    panels = refs.pop(0)
    before = [refs.pop(0) for _ in range(first, end)] if height > 0 else []
    sol = refs.pop(0) if source == "z" else None
    kept = refs.pop(0) if source == "z" and end < LEVELS - 1 - height else None
    after = [refs.pop(0) for _ in range(first, end)]
    scratch = refs.pop(0)

    @pl.when(pl.program_id(0) == 0)
    def _():
        for i, ref in enumerate(after):
            ref[...] = before[i][...] if before else jnp.zeros_like(ref)

    for k in range(panels.shape[0]):
        s = pl.program_id(0) * panels.shape[0] + k
        slot = slot_base + s
        if source == "z":
            turned = given[:, k].reshape(256, 128).T
            z_t = jnp.concatenate([turned[:64], turned[64:]], 1)
            y_t = dot3(z_t, (inverse[k, :512], inverse[k, 512:]), ((1,), (0,)))
            limit = sizes[slot]
            y_t = jnp.where(lax.broadcasted_iota(jnp.int32, (64, 512), 1) < limit, y_t, 0.0)
            scratch[pl.ds(192 * k, 64), :] = y_t
            lanes = scratch[pl.ds(192 * k, 64), pl.ds(pl.multiple_of(pos[0] // 4 * 128, 128), 128)]
            own = jnp.concatenate([lanes, lanes], 0).T
            scratch[pl.ds(192 * k + 64, 128), pl.ds(0, 128)] = own
            own = scratch[pl.ds(pl.multiple_of(192 * k + 64 + pos[0] % 4 * 32, 32), 32), pl.ds(0, 128)]
            sol[k] = fold(own)[0]
            if kept is not None:
                kept[k] = y_t
        elif source == "t":
            y_t = given[k]
        block = panels[k, 0, first:end].reshape((end - first) * 32, 512)
        if source == "y":
            x = given[:, k]
            turned = pltpu.roll(x.reshape(256, 128), 64, 1).reshape(16, 16, 128)
            low = lower((16, 16, 128))
            halves = [jnp.where(low, x, turned)[:, None], jnp.where(low, turned, x)[:, None]]
            y = jnp.concatenate(halves, 1).reshape(512, 128)
            update = fold(dot3(block, y, ((1,), (0,))))
        else:
            update = fold(dot3(block, jnp.concatenate([y_t, y_t], 0), ((1,), (1,))))
        node = NODE_BASE[height] + jnp.minimum(s * 16 + pos[1], NODES[height] - 1)
        for d in range(end):
            node = parent[node]
            if d < first:
                continue
            target = height + 1 + d
            j = node - NODE_BASE[target]
            many = max(1, NODES[target] // 16)
            if target <= PAIRED:
                where = ((j + pos[1]) % 2 * 8 + j % 16 // 2) * many + j // 16
            else:
                where = (j % 16) * many + j // 16
            scale = pattern[slot * 7 + d].astype(jnp.float32)
            after[d - first][where] += scale * update[d - first]


def split_inverse_kernel(pos, parent, pattern, sizes, inverse, both):
    rows = inverse[:, 0].reshape(16, 2, 16, 512)
    rows = jnp.concatenate([rows[:, 0].reshape(256, 512), rows[:, 1].reshape(256, 512)], 0)
    both[0, :512], both[0, 512:] = split(rows)


def near_kernel(pos, parent, pattern, sizes, block, out):
    out[0] = block[:, 0].reshape(512, 256)


def join_kernel(pos, parent, pattern, sizes, here, there, out):
    out[...] = (here[...] + there[...]).reshape(out.shape)


def pack_kernel(pos, parent, pattern, sizes, sides, inv5, inv6, inv7, panel5, panel6, *refs):
    *refs, scratch = refs
    half = len(refs) // 2 - 1
    folded, out = refs[half : half + 2]
    folded[...] = from_own_order(sides[...], scratch)
    for source, target in zip(refs[:half], refs[half + 2 :]):
        target[...] = source[:, 0]
    for level, inv, panel, at in ((0, inv5, panel5, 3), (1, inv6, panel6, 0), (2, inv7, None, 2)):
        slot = 16 + level
        size = sizes[slot]
        row = pos[0] * 32 + lax.broadcasted_iota(jnp.int32, (32, 512), 0)
        column = lax.broadcasted_iota(jnp.int32, (32, 512), 1)
        out[at] = jnp.where((row < size) & (column < size), inv[0, 0], 0.0)
        for d in range(2 - level):
            out[at + 1 + d] = panel[0, 0, d] * pattern[slot * 7 + d].astype(jnp.float32)


def choose_kernel(pos, parent, pattern, sizes, low, middle, high, out):
    for c in range(4):
        out[3 * c : 3 * c + 3] = low[c]
    for c in range(2):
        out[12 + 2 * c : 14 + 2 * c] = middle[c]
    out[16:17] = high[0]


def turn_kernel(pos, parent, pattern, sizes, p5, p6, p7, rhs, out, scratch):
    at = 0
    for level, ref in enumerate((p5, p6, p7)):
        for j in range(4 >> level):
            piece = ref[j] - jnp.where(pos[1] == j, rhs[16 + level], 0.0)
            scratch[pl.ds(at * 32, 16), :] = piece
            scratch[pl.ds(at * 32 + 16, 16), :] = pltpu.roll(piece, 64, 1)
            at += 1
    scratch[pl.ds(224, 32), :] = jnp.zeros((32, 128), jnp.float32)
    turned = scratch[pl.ds(0, 256), :].T
    for z in range(8):
        out[2 * z] = turned[8 * z : 8 * z + 8]
        out[2 * z + 1] = turned[8 * z : 8 * z + 8]


def sum_kernel(pos, parent, pattern, sizes, recv, out):
    total = recv[0]
    for i in range(1, 16):
        total = total + recv[i]
    for i in range(16):
        out[i] = total


def place(own, y, level, pos):
    lanes = pltpu.roll(y, (256 - (pos[0] % 8) * 32) % 256, 1)[:, :128]
    lane = lax.broadcasted_iota(jnp.int32, (8, 128), 1) // 32
    return jnp.where(lane == level, pltpu.roll(lanes, level * 32, 1), own)


def low_kernel(pos, parent, pattern, sizes, recv, block, out, left, z):
    step = pl.program_id(0)

    @pl.when(step == 0)
    def _():
        lane = lax.broadcasted_iota(jnp.int32, (8, 128), 1) // 32
        for n in range(7):
            for g in range(4):
                whole = jnp.zeros((8, 128), jnp.float32)
                for i in range(4):
                    piece = recv[4 * g + i][:, (n // 4) * 128 : (n // 4 + 1) * 128]
                    turned = pltpu.roll(piece, ((i - n % 4) * 32) % 128, 1)
                    whole = jnp.where(lane == i, turned, whole)
                if n < 4:
                    z[n, :, g * 128 : (g + 1) * 128] = -whole
                else:
                    left[n - 4, :, g * 128 : (g + 1) * 128] = jnp.where(pos[1] % 2 == 0, -whole, 0.0)
        out[...] = jnp.zeros_like(out)

    def matrix(i):
        return block[:, i].reshape(512, 256)

    solved = [dot3(z[2 * step + k], matrix(3 * k), ((1,), (0,))) for k in range(2)]
    near = [dot3(solved[k], matrix(3 * k + 1), ((1,), (1,))) for k in range(2)]
    far = [dot3(solved[k], matrix(3 * k + 2), ((1,), (1,))) for k in range(2)]
    left[2] = left[2] - (far[0] + far[1])
    for k in range(2):
        node = 2 * step + k
        out[node] = place(out[node], solved[k], 0, pos)
        target = parent[NODE_BASE[TOP] + node] - NODE_BASE[TOP + 1]
        left[target] = left[target] - near[k]


def middle_kernel(pos, parent, pattern, sizes, left, other, before, block, out, after):
    def matrix(i):
        return block[i]

    solved = [dot3(left[k] + other[k], matrix(2 * k), ((1,), (0,))) for k in range(2)]
    update = [dot3(solved[k], matrix(2 * k + 1), ((1,), (1,))) for k in range(2)]
    out[...] = before[...]
    for k in range(2):
        out[k] = place(before[k], solved[k], 1, pos)
    after[...] = left[2] - (update[0] + update[1])


def root_kernel(pos, parent, pattern, sizes, left, other, before, block, out):
    solved = dot3(left[...] + other[...], block[0], ((1,), (0,)))
    out[...] = before[...]
    out[0] = place(before[0], solved, 2, pos)


def last_kernel(pos, parent, pattern, sizes, recv, *refs):
    *parts, out, scratch = refs
    columns = jnp.concatenate([recv[2 * i + pos[0] // 8] for i in range(8)], 0)
    turned = jnp.concatenate([columns, columns], 0).T
    parts = [ref[...] for ref in parts] + [fold(turned[:96])]
    out[...] = to_own_order(jnp.concatenate(parts, 0), scratch)


def on_device(right_side, inverse_rows, panels, pattern, node_sizes, parent):
    pos = jnp.stack([lax.axis_index("prow"), lax.axis_index("pcol")]).astype(jnp.int32)
    natural = right_side.reshape(19, 16, 128)
    scalars = jnp.concatenate([pos, parent, pattern.reshape(-1), node_sizes.reshape(-1)])
    slot_counts = [max(1, n // 16) for n in NODES]
    bases = [sum(slot_counts[:h]) for h in range(LEVELS)]
    near = []

    def call(kernel, scratch, grid, in_specs, out_specs, out_shape, aliases, *args):
        args = [
            pltpu.with_memory_space_constraint(a, pltpu.HBM)
            if a is natural or (a.size > 1 << 18 and a.dtype == f32 and not any(a is b for b in near))
            else a
            for a in args
        ]
        return pl.pallas_call(
            functools.partial(with_parts, kernel),
            grid_spec=pltpu.PrefetchScalarGridSpec(
                num_scalar_prefetch=1,
                grid=grid,
                in_specs=in_specs,
                out_specs=out_specs,
                scratch_shapes=scratch,
            ),
            out_shape=out_shape,
            input_output_aliases={k + 1: v for k, v in aliases.items()},
            compiler_params=pltpu.CompilerParams(vmem_limit_bytes=VMEM_LIMIT),
        )(scalars, *args)

    def exchange(x, axis):
        return lax.all_to_all(x, axis, 0, 0, tiled=True)

    f32 = jnp.float32
    pending = []
    recv = None
    outputs = []
    cuts = [bases[h] for h in CUTS]
    rows = pl.BlockSpec((6, 32, 512), lambda *_: (0, 0, 0))

    def block(*lead):
        def spec(n, slot):
            return pl.BlockSpec((1, 1) + (n,) * len(lead) + (32, 512), lambda *_: (slot, 0) + lead + (0, 0))

        return spec

    spans = list(zip(cuts[:-1], cuts[1:]))
    all_sides = pl.BlockSpec((19, 16, 128), lambda *_: (0, 0, 0))
    tall = [pltpu.VMEM((19 * 32, 128), f32)]
    rhs, top, *wholes = call(
        pack_kernel,
        tall,
        (1,),
        [all_sides, block()(0, 16), block()(0, 17), block()(0, 18), block(0)(2, 16), block(0)(1, 17)]
        + [pl.BlockSpec((hi - lo, 1, 32, 512), lambda *_, i=lo // (hi - lo): (i, 0, 0, 0)) for lo, hi in spans],
        [all_sides, rows] + [pl.BlockSpec((hi - lo, 32, 512), lambda *_: (0, 0, 0)) for lo, hi in spans],
        [jax.ShapeDtypeStruct((19, 16, 128), f32), jax.ShapeDtypeStruct((6, 32, 512), f32)]
        + [jax.ShapeDtypeStruct((hi - lo, 32, 512), f32) for lo, hi in spans],
        {},
        natural,
        *[inverse_rows] * 3,
        *[panels] * 2,
        *[inverse_rows] * len(spans),
    )
    top = lax.all_gather(top, "pcol", axis=0)
    for height in range(TOP):
        count = slot_counts[height]
        base = bases[height]
        reach = LEVELS - 1 - height
        info = (height, count, base)
        whole = height >= GATHER_FROM
        piece = jax.ShapeDtypeStruct((16, count, 16, 128), f32)
        own = jax.ShapeDtypeStruct((count, 16, 128), f32)
        every = pl.BlockSpec((16, count, 16, 128), lambda *_: (0, 0, 0, 0))
        every_own = pl.BlockSpec((count, 16, 128), lambda *_: (0, 0, 0))
        rhs_all = pl.BlockSpec((count, 16, 128), lambda *_, b=base // count: (b, 0, 0))
        if whole:
            z = call(
                functools.partial(residue_kernel, *info),
                [],
                (1,),
                [pl.BlockSpec(recv.shape, lambda *_: (0, 0, 0, 0)), rhs_all],
                every,
                piece,
                {},
                recv,
                rhs,
            )
            gathered = exchange(z, "prow")
            lo, inverse = [pair for pair in inverses if pair[0] <= base][-1]
            inverse, _ = lax.optimization_barrier((inverse, z))
            inverse = call(
                split_inverse_kernel,
                [],
                (count,),
                [pl.BlockSpec((16, 1, 32, 512), lambda s, *_, b=base - lo: (0, b + s, 0, 0))],
                pl.BlockSpec((1, 1024, 512), lambda s, *_: (s, 0, 0)),
                jax.ShapeDtypeStruct((count, 1024, 512), jnp.bfloat16),
                {},
                inverse,
            )
        else:
            per = min(4, count)
            in_specs = [
                pl.BlockSpec((per, 16, 128), lambda s, *_, b=base // per: (b + s, 0, 0)),
                pl.BlockSpec((per, 1, 32, 512), lambda s, *_, b=base // per: (b + s, 0, 0, 0)),
            ]
            args = [natural, inverse_rows]
            if height > 0:
                in_specs = [pl.BlockSpec((recv.shape[0], per, 16, 128), lambda s, *_: (0, s, 0, 0))] + in_specs
                args = [recv] + args
            some = pl.BlockSpec((16, per, 16, 128), lambda s, *_: (0, s, 0, 0))
            kernel = functools.partial(partial_kernel, *info)
            parts = call(kernel, [pltpu.VMEM((per * 32, 128), f32)], (count // per,), in_specs, some, piece, {}, *args)
            parts = exchange(parts, "prow")
            if height == 0:
                wholes, parts = lax.optimization_barrier((wholes, parts))
                inverses = [(lo, lax.all_gather(part, "prow", axis=0)) for lo, part in zip(cuts[:-1], wholes)]
            y, sol = call(
                functools.partial(solved_kernel, *info), [], (1,), [every], [every, every_own], [piece, own], {}, parts
            )
            outputs.append(sol)
            gathered = exchange(y, "prow")
        if height == 1:
            chosen_from, _ = lax.optimization_barrier((top, y))
            halves = [(4, 3, 0, 1), (2, 2, 0, 0), (1, 1, 0, 2)]
            chosen = call(
                choose_kernel,
                [],
                (1,),
                [
                    pl.BlockSpec((m, n, 32, 256), lambda _, info, a=a, b=b: (a, b, 0, info[1] % 2))
                    for m, n, a, b in halves
                ],
                pl.BlockSpec((17, 32, 256), lambda *_: (0, 0, 0)),
                jax.ShapeDtypeStruct((17, 32, 256), f32),
                {},
                *[chosen_from] * 3,
            )
            top = lax.all_gather(chosen, "prow", axis=0)
        steps = [(0, 1), (1, reach)] if height + 1 < TOP else [(0, reach)]
        updated = []
        given, source = gathered, "z" if whole else "y"
        for start, end in steps:
            per = min(2, count)
            in_specs = [pl.BlockSpec((16, per, 16, 128), lambda s, *_: (0, s, 0, 0))]
            if source == "t":
                in_specs = [pl.BlockSpec((per, 64, 512), lambda s, *_: (s, 0, 0))]
            args = [given]
            out_specs, out_shape = [], []
            if source == "z":
                in_specs.append(pl.BlockSpec((per, 1024, 512), lambda s, *_: (s, 0, 0)))
                args.append(inverse)
                out_specs.append(pl.BlockSpec((per, 16, 128), lambda s, *_: (s, 0, 0)))
                out_shape.append(own)
                if end < reach:
                    out_specs.append(pl.BlockSpec((per, 64, 512), lambda s, *_: (s, 0, 0)))
                    out_shape.append(jax.ShapeDtypeStruct((count, 64, 512), f32))
            in_specs.append(
                pl.BlockSpec((per, 1, end, 32, 512), lambda s, *_, b=base // per: (b + s, 0, 0, 0, 0))
            )
            args.append(panels)
            aliases = {}
            for d in range(start, end):
                shape = (16 * slot_counts[height + 1 + d], 16, 128)
                spec = pl.BlockSpec(shape, lambda *_: (0, 0, 0))
                if height > 0:
                    aliases[len(in_specs)] = len(out_specs)
                    in_specs.append(spec)
                    args.append(pending[d])
                out_specs.append(spec)
                out_shape.append(jax.ShapeDtypeStruct(shape, f32))
            results = call(
                functools.partial(spread_kernel, *info, source, start, end),
                SCRATCH,
                (count // per,),
                in_specs,
                out_specs,
                out_shape,
                aliases,
                *args,
            )
            results = list(results)
            if source == "z":
                outputs.append(results.pop(0))
                if end < reach:
                    given, source = results.pop(0), "t"
            updated += results
        results = updated
        if height + 1 < TOP:
            following = slot_counts[height + 1]
            pending = results[1:]
            if height < PAIRED:
                half = pl.BlockSpec((8 * following, 16, 128), lambda *_: (0, 0, 0))
                there = lax.ppermute(results[0][8 * following :], "pcol", [(i, i ^ 1) for i in range(16)])
                joined = call(
                    join_kernel,
                    [],
                    (1,),
                    [half, half],
                    pl.BlockSpec((8, following, 16, 128), lambda *_: (0, 0, 0, 0)),
                    jax.ShapeDtypeStruct((8, following, 16, 128), f32),
                    {},
                    results[0],
                    there,
                )
                recv = lax.all_to_all(
                    joined,
                    "pcol",
                    0,
                    0,
                    tiled=True,
                    axis_index_groups=[[core + 2 * z for z in range(8)] for core in range(2)],
                )
            else:
                recv = exchange(results[0].reshape(16, following, 16, 128), "pcol")
    many = pl.BlockSpec((16, 16, 128), lambda *_: (0, 0, 0))
    sides = pl.BlockSpec((16, 8, 256), lambda *_: (0, 0, 0))
    sides_shape = jax.ShapeDtypeStruct((16, 8, 256), f32)
    turned = call(
        turn_kernel,
        [pltpu.VMEM((256, 128), f32)],
        (1,),
        [many] * 3 + [pl.BlockSpec((19, 16, 128), lambda *_: (0, 0, 0))],
        sides,
        sides_shape,
        {},
        *results,
        rhs,
    )
    total = call(sum_kernel, [], (1,), [sides], sides, sides_shape, {}, exchange(turned, "pcol"))
    gathered = exchange(total, "prow")
    top, _ = lax.optimization_barrier((top, total))
    upper = call(
        near_kernel,
        [],
        (5,),
        [pl.BlockSpec((16, 1, 32, 256), lambda s, *_: (0, 12 + s, 0, 0))],
        pl.BlockSpec((1, 512, 256), lambda s, *_: (s, 0, 0)),
        jax.ShapeDtypeStruct((5, 512, 256), f32),
        {},
        top,
    )
    gathered, upper = lax.optimization_barrier((gathered, upper))
    near.append(upper)
    def whole_of(*shape):
        return pl.BlockSpec(shape, lambda *_: (0,) * len(shape)), jax.ShapeDtypeStruct(shape, f32)

    def other_core(x):
        return lax.ppermute(x, "pcol", [(i, i ^ 1) for i in range(16)])

    found, found_shape = whole_of(16, 8, 128)
    three, three_shape = whole_of(3, 8, 512)
    single, single_shape = whole_of(8, 512)
    solved, left = call(
        low_kernel,
        [pltpu.VMEM((4, 8, 512), f32)],
        (2,),
        [sides, pl.BlockSpec((16, 6, 32, 256), lambda s, *_: (0, s, 0, 0))],
        [found, three],
        [found_shape, three_shape],
        {},
        gathered,
        top,
    )
    solved, left = call(
        middle_kernel,
        [],
        (1,),
        [three, three, found, pl.BlockSpec((4, 512, 256), lambda *_: (0, 0, 0))],
        [found, single],
        [found_shape, single_shape],
        {},
        left,
        other_core(left),
        solved,
        upper,
    )
    solved = call(
        root_kernel,
        [],
        (1,),
        [single, single, found, pl.BlockSpec((1, 512, 256), lambda *_: (4, 0, 0))],
        found,
        found_shape,
        {},
        left,
        other_core(left),
        solved,
        upper,
    )
    out = call(
        last_kernel,
        tall,
        (1,),
        [found] + [pl.BlockSpec(x.shape, lambda *_: (0, 0, 0)) for x in outputs],
        all_sides,
        jax.ShapeDtypeStruct((19, 16, 128), f32),
        {},
        exchange(solved, "pcol"),
        *outputs,
    )
    return out.reshape(19, 1, 2048)


def solution(mesh):
    in_specs = (
        P(None, "pcol", "prow"),
        P(None, "pcol", "prow", None),
        P(None, "pcol", None, "prow", None),
        P(None, "pcol", None),
        P(None, "pcol"),
        P(),
    )
    out_specs = P(None, "pcol", "prow")
    return jax.shard_map(
        on_device, mesh=mesh, in_specs=in_specs, out_specs=out_specs, check_vma=False
    )
```

```python
import functools

import jax
import jax.numpy as jnp
from jax import lax
from jax.experimental import pallas as pl
from jax.experimental.pallas import tpu as pltpu
from jax.sharding import PartitionSpec as P

LEVELS = 8
LEAVES = 128
GATHER_FROM = 2
CUTS = (2, 5)
SCRATCH = [pltpu.VMEM((384, 512), jnp.float32)]
PAIRED = 2
TOP = 5
VMEM_LIMIT = 24 * 1024 * 1024

NODES = [LEAVES >> h for h in range(LEVELS)]
NODE_BASE = [2 * LEAVES - 2 * (LEAVES >> h) for h in range(LEVELS)]


class Part:
    def __init__(self, ref, start):
        self.ref, self.start = ref, start

    def __getitem__(self, index):
        return self.ref[index + self.start]


def with_parts(kernel, *refs):
    return kernel(*[Part(refs[0], start) for start in (0, 2, 256, 389)], *refs[1:])


def split(x):
    high = x.astype(jnp.bfloat16)
    low = (x - high.astype(jnp.float32)).astype(jnp.bfloat16)
    return high, low


def dot3(a, b, dims):
    bh, bl = b if isinstance(b, tuple) else split(b)
    dot = functools.partial(
        lax.dot_general, dimension_numbers=(dims, ((), ())), preferred_element_type=jnp.float32
    )
    n = a.shape[0]
    if n <= 64 and dims[0] == (1,):
        high = a.astype(jnp.bfloat16).astype(jnp.float32)
        both = jnp.concatenate([high, a - high], 0).astype(jnp.bfloat16)
        first = dot(both, bh)
        second = dot(high.astype(jnp.bfloat16), bl)
        return first[:n] + (first[n:] + second)
    ah, al = split(a)
    return dot(ah, bh) + (dot(ah, bl) + dot(al, bh))


def lower(shape):
    return lax.broadcasted_iota(jnp.int32, shape, len(shape) - 1) < 64


def from_own_order(x, scratch):
    n = x.shape[0]
    x = x.reshape(n * 16, 128)
    scratch[pl.ds(0, n * 16, stride=2), :] = x
    scratch[pl.ds(1, n * 16, stride=2), :] = pltpu.roll(x, 64, 1)
    rows = scratch[pl.ds(0, n * 32), :].reshape(n, 2, 16, 128)
    other = pltpu.roll(rows[:, 1].reshape(n * 16, 128), 64, 1).reshape(n, 16, 128)
    return jnp.where(lower((n, 16, 128)), rows[:, 0], other)


def to_own_order(x, scratch):
    n = x.shape[0]
    turned = pltpu.roll(x.reshape(n * 16, 128), 64, 1).reshape(n, 1, 16, 128)
    scratch[pl.ds(0, n * 32), :] = jnp.concatenate([x.reshape(n, 1, 16, 128), turned], 1).reshape(n * 32, 128)
    even = scratch[pl.ds(0, n * 16, stride=2), :]
    odd = pltpu.roll(scratch[pl.ds(1, n * 16, stride=2), :], 64, 1)
    return jnp.where(lower((n * 16, 128)), even, odd).reshape(n, 16, 128)


def fold(x):
    n = x.shape[0] // 32
    x = x.reshape(n, 2, 16, 128)
    return jnp.where(lower((n, 16, 128)), x[:, 0], x[:, 1])


def own_mask(pos, sizes, slot, local, nodes):
    row = lax.broadcasted_iota(jnp.int32, (16, 128), 0)
    lane = lax.broadcasted_iota(jnp.int32, (16, 128), 1)
    row_id = pos[0] * 32 + row + 16 * (lane >= 64).astype(jnp.int32)
    limit = jnp.where(local * 16 + pos[1] < nodes, sizes[slot], 0)
    return row_id < limit


def residue_kernel(height, slots, slot_base, pos, parent, pattern, sizes, recv, rhs, out):
    for s in range(slots):
        total = recv[0, s]
        for i in range(1, recv.shape[0]):
            total = total + recv[i, s]
        keep = own_mask(pos, sizes, slot_base + s, s, NODES[height])
        z = jnp.where(keep, rhs[s] - total, 0.0)
        for i in range(16):
            out[i, s] = z


def partial_kernel(height, slots, slot_base, pos, parent, pattern, sizes, *refs):
    recv = None
    if height > 0:
        recv, *refs = refs
    rhs, inverse, out, scratch = refs
    low = lower((16, 128))
    sides = from_own_order(rhs[...], scratch)
    for i in range(rhs.shape[0]):
        s = pl.program_id(0) * rhs.shape[0] + i
        z = sides[i]
        if recv is not None:
            total = recv[0, i]
            for k in range(1, recv.shape[0]):
                total = total + recv[k, i]
            z = z - total
        keep = own_mask(pos, sizes, slot_base + s, s, NODES[height])
        z = jnp.where(keep, z, 0.0)
        turned = pltpu.roll(z, 64, 1)
        twice = jnp.concatenate([jnp.where(low, z, turned), jnp.where(low, turned, z)], 0)
        out[:, i] = fold(dot3(inverse[i, 0], twice, ((0,), (0,))))


def solved_kernel(height, slots, slot_base, pos, parent, pattern, sizes, recv, out, sol):
    for s in range(slots):
        total = recv[0, s]
        for i in range(1, 16):
            total = total + recv[i, s]
        keep = own_mask(pos, sizes, slot_base + s, s, NODES[height])
        y = jnp.where(keep, total, 0.0)
        sol[s] = y
        for i in range(16):
            out[i, s] = y


def spread_kernel(height, slots, slot_base, source, first, end, pos, parent, pattern, sizes, *refs):
    refs = list(refs)
    given = refs.pop(0)
    inverse = refs.pop(0) if source == "z" else None
    panels = refs.pop(0)
    before = [refs.pop(0) for _ in range(first, end)] if height > 0 else []
    sol = refs.pop(0) if source == "z" else None
    kept = refs.pop(0) if source == "z" and end < LEVELS - 1 - height else None
    after = [refs.pop(0) for _ in range(first, end)]
    scratch = refs.pop(0)

    @pl.when(pl.program_id(0) == 0)
    def _():
        for i, ref in enumerate(after):
            ref[...] = before[i][...] if before else jnp.zeros_like(ref)

    for k in range(panels.shape[0]):
        s = pl.program_id(0) * panels.shape[0] + k
        slot = slot_base + s
        if source == "z":
            turned = given[:, k].reshape(256, 128).T
            z_t = jnp.concatenate([turned[:64], turned[64:]], 1)
            y_t = dot3(z_t, (inverse[k, :512], inverse[k, 512:]), ((1,), (0,)))
            limit = sizes[slot]
            y_t = jnp.where(lax.broadcasted_iota(jnp.int32, (64, 512), 1) < limit, y_t, 0.0)
            scratch[pl.ds(192 * k, 64), :] = y_t
            lanes = scratch[pl.ds(192 * k, 64), pl.ds(pl.multiple_of(pos[0] // 4 * 128, 128), 128)]
            own = jnp.concatenate([lanes, lanes], 0).T
            scratch[pl.ds(192 * k + 64, 128), pl.ds(0, 128)] = own
            own = scratch[pl.ds(pl.multiple_of(192 * k + 64 + pos[0] % 4 * 32, 32), 32), pl.ds(0, 128)]
            sol[k] = fold(own)[0]
            if kept is not None:
                kept[k] = y_t
        elif source == "t":
            y_t = given[k]
        block = panels[k, 0, first:end].reshape((end - first) * 32, 512)
        if source == "y":
            x = given[:, k]
            turned = pltpu.roll(x.reshape(256, 128), 64, 1).reshape(16, 16, 128)
            low = lower((16, 16, 128))
            halves = [jnp.where(low, x, turned)[:, None], jnp.where(low, turned, x)[:, None]]
            y = jnp.concatenate(halves, 1).reshape(512, 128)
            update = fold(dot3(block, y, ((1,), (0,))))
        else:
            update = fold(dot3(block, jnp.concatenate([y_t, y_t], 0), ((1,), (1,))))
        node = NODE_BASE[height] + jnp.minimum(s * 16 + pos[1], NODES[height] - 1)
        for d in range(end):
            node = parent[node]
            if d < first:
                continue
            target = height + 1 + d
            j = node - NODE_BASE[target]
            many = max(1, NODES[target] // 16)
            if target <= PAIRED:
                where = ((j + pos[1]) % 2 * 8 + j % 16 // 2) * many + j // 16
            else:
                where = (j % 16) * many + j // 16
            scale = pattern[slot * 7 + d].astype(jnp.float32)
            after[d - first][where] += scale * update[d - first]


def split_inverse_kernel(pos, parent, pattern, sizes, inverse, both):
    rows = inverse[:, 0].reshape(16, 2, 16, 512)
    rows = jnp.concatenate([rows[:, 0].reshape(256, 512), rows[:, 1].reshape(256, 512)], 0)
    both[0, :512], both[0, 512:] = split(rows)


def near_kernel(pos, parent, pattern, sizes, block, out):
    out[0] = block[:, 0].reshape(512, 256)


def join_kernel(pos, parent, pattern, sizes, here, there, out):
    out[...] = (here[...] + there[...]).reshape(out.shape)


def pack_kernel(pos, parent, pattern, sizes, sides, inv5, inv6, inv7, panel5, panel6, *refs):
    *refs, scratch = refs
    half = len(refs) // 2 - 1
    folded, out = refs[half : half + 2]
    folded[...] = from_own_order(sides[...], scratch)
    for source, target in zip(refs[:half], refs[half + 2 :]):
        target[...] = source[:, 0]
    for level, inv, panel, at in ((0, inv5, panel5, 3), (1, inv6, panel6, 0), (2, inv7, None, 2)):
        slot = 16 + level
        size = sizes[slot]
        row = pos[0] * 32 + lax.broadcasted_iota(jnp.int32, (32, 512), 0)
        column = lax.broadcasted_iota(jnp.int32, (32, 512), 1)
        out[at] = jnp.where((row < size) & (column < size), inv[0, 0], 0.0)
        for d in range(2 - level):
            out[at + 1 + d] = panel[0, 0, d] * pattern[slot * 7 + d].astype(jnp.float32)


def choose_kernel(pos, parent, pattern, sizes, low, middle, high, out):
    for c in range(4):
        out[3 * c : 3 * c + 3] = low[c]
    for c in range(2):
        out[12 + 2 * c : 14 + 2 * c] = middle[c]
    out[16:17] = high[0]


def solved_and_choose_kernel(height, slots, slot_base, pos, parent, pattern, sizes, recv, *refs):
    *blocks, out, sol, chosen = refs
    solved_kernel(height, slots, slot_base, pos, parent, pattern, sizes, recv, out, sol)
    choose_kernel(pos, parent, pattern, sizes, *blocks, chosen)


def turn_kernel(pos, parent, pattern, sizes, p5, p6, p7, rhs, out, scratch):
    at = 0
    for level, ref in enumerate((p5, p6, p7)):
        for j in range(4 >> level):
            piece = ref[j] - jnp.where(pos[1] == j, rhs[16 + level], 0.0)
            scratch[pl.ds(at * 32, 16), :] = piece
            scratch[pl.ds(at * 32 + 16, 16), :] = pltpu.roll(piece, 64, 1)
            at += 1
    scratch[pl.ds(224, 32), :] = jnp.zeros((32, 128), jnp.float32)
    turned = scratch[pl.ds(0, 256), :].T
    for z in range(8):
        out[2 * z] = turned[8 * z : 8 * z + 8]
        out[2 * z + 1] = turned[8 * z : 8 * z + 8]


def sum_kernel(pos, parent, pattern, sizes, recv, out):
    total = recv[0]
    for i in range(1, 16):
        total = total + recv[i]
    for i in range(16):
        out[i] = total


def place(own, y, level, pos):
    lanes = pltpu.roll(y, (256 - (pos[0] % 8) * 32) % 256, 1)[:, :128]
    lane = lax.broadcasted_iota(jnp.int32, (8, 128), 1) // 32
    return jnp.where(lane == level, pltpu.roll(lanes, level * 32, 1), own)


def low_kernel(pos, parent, pattern, sizes, recv, block, out, left, z):
    step = pl.program_id(0)

    @pl.when(step == 0)
    def _():
        lane = lax.broadcasted_iota(jnp.int32, (8, 128), 1) // 32
        for n in range(7):
            for g in range(4):
                whole = jnp.zeros((8, 128), jnp.float32)
                for i in range(4):
                    piece = recv[4 * g + i][:, (n // 4) * 128 : (n // 4 + 1) * 128]
                    turned = pltpu.roll(piece, ((i - n % 4) * 32) % 128, 1)
                    whole = jnp.where(lane == i, turned, whole)
                if n < 4:
                    z[n, :, g * 128 : (g + 1) * 128] = -whole
                else:
                    left[n - 4, :, g * 128 : (g + 1) * 128] = jnp.where(pos[1] % 2 == 0, -whole, 0.0)
        out[...] = jnp.zeros_like(out)

    def matrix(i):
        return block[:, i].reshape(512, 256)

    solved = [dot3(z[2 * step + k], matrix(3 * k), ((1,), (0,))) for k in range(2)]
    near = [dot3(solved[k], matrix(3 * k + 1), ((1,), (1,))) for k in range(2)]
    far = [dot3(solved[k], matrix(3 * k + 2), ((1,), (1,))) for k in range(2)]
    left[2] = left[2] - (far[0] + far[1])
    for k in range(2):
        node = 2 * step + k
        out[node] = place(out[node], solved[k], 0, pos)
        target = parent[NODE_BASE[TOP] + node] - NODE_BASE[TOP + 1]
        left[target] = left[target] - near[k]


def middle_kernel(pos, parent, pattern, sizes, left, other, before, block, out, after):
    def matrix(i):
        return block[i]

    solved = [dot3(left[k] + other[k], matrix(2 * k), ((1,), (0,))) for k in range(2)]
    update = [dot3(solved[k], matrix(2 * k + 1), ((1,), (1,))) for k in range(2)]
    out[...] = before[...]
    for k in range(2):
        out[k] = place(before[k], solved[k], 1, pos)
    after[...] = left[2] - (update[0] + update[1])


def root_kernel(pos, parent, pattern, sizes, left, other, before, block, out):
    solved = dot3(left[...] + other[...], block[0], ((1,), (0,)))
    out[...] = before[...]
    out[0] = place(before[0], solved, 2, pos)


def last_kernel(pos, parent, pattern, sizes, recv, *refs):
    *parts, out, scratch = refs
    columns = jnp.concatenate([recv[2 * i + pos[0] // 8] for i in range(8)], 0)
    turned = jnp.concatenate([columns, columns], 0).T
    parts = [ref[...] for ref in parts] + [fold(turned[:96])]
    out[...] = to_own_order(jnp.concatenate(parts, 0), scratch)


def on_device(right_side, inverse_rows, panels, pattern, node_sizes, parent):
    pos = jnp.stack([lax.axis_index("prow"), lax.axis_index("pcol")]).astype(jnp.int32)
    natural = right_side.reshape(19, 16, 128)
    scalars = jnp.concatenate([pos, parent, pattern.reshape(-1), node_sizes.reshape(-1)])
    slot_counts = [max(1, n // 16) for n in NODES]
    bases = [sum(slot_counts[:h]) for h in range(LEVELS)]
    near = []

    def call(kernel, scratch, grid, in_specs, out_specs, out_shape, aliases, *args):
        args = [
            pltpu.with_memory_space_constraint(a, pltpu.HBM)
            if a is natural or (a.size > 1 << 18 and a.dtype == f32 and not any(a is b for b in near))
            else a
            for a in args
        ]
        return pl.pallas_call(
            functools.partial(with_parts, kernel),
            grid_spec=pltpu.PrefetchScalarGridSpec(
                num_scalar_prefetch=1,
                grid=grid,
                in_specs=in_specs,
                out_specs=out_specs,
                scratch_shapes=scratch,
            ),
            out_shape=out_shape,
            input_output_aliases={k + 1: v for k, v in aliases.items()},
            compiler_params=pltpu.CompilerParams(vmem_limit_bytes=VMEM_LIMIT),
        )(scalars, *args)

    def exchange(x, axis):
        return lax.all_to_all(x, axis, 0, 0, tiled=True)

    f32 = jnp.float32
    pending = []
    recv = None
    outputs = []
    cuts = [bases[h] for h in CUTS]
    rows = pl.BlockSpec((6, 32, 512), lambda *_: (0, 0, 0))

    def block(*lead):
        def spec(n, slot):
            return pl.BlockSpec((1, 1) + (n,) * len(lead) + (32, 512), lambda *_: (slot, 0) + lead + (0, 0))

        return spec

    spans = list(zip(cuts[:-1], cuts[1:]))
    all_sides = pl.BlockSpec((19, 16, 128), lambda *_: (0, 0, 0))
    tall = [pltpu.VMEM((19 * 32, 128), f32)]
    rhs, top, *wholes = call(
        pack_kernel,
        tall,
        (1,),
        [all_sides, block()(0, 16), block()(0, 17), block()(0, 18), block(0)(2, 16), block(0)(1, 17)]
        + [pl.BlockSpec((hi - lo, 1, 32, 512), lambda *_, i=lo // (hi - lo): (i, 0, 0, 0)) for lo, hi in spans],
        [all_sides, rows] + [pl.BlockSpec((hi - lo, 32, 512), lambda *_: (0, 0, 0)) for lo, hi in spans],
        [jax.ShapeDtypeStruct((19, 16, 128), f32), jax.ShapeDtypeStruct((6, 32, 512), f32)]
        + [jax.ShapeDtypeStruct((hi - lo, 32, 512), f32) for lo, hi in spans],
        {},
        natural,
        *[inverse_rows] * 3,
        *[panels] * 2,
        *[inverse_rows] * len(spans),
    )
    top = lax.all_gather(top, "pcol", axis=0)
    for height in range(TOP):
        count = slot_counts[height]
        base = bases[height]
        reach = LEVELS - 1 - height
        info = (height, count, base)
        whole = height >= GATHER_FROM
        piece = jax.ShapeDtypeStruct((16, count, 16, 128), f32)
        own = jax.ShapeDtypeStruct((count, 16, 128), f32)
        every = pl.BlockSpec((16, count, 16, 128), lambda *_: (0, 0, 0, 0))
        every_own = pl.BlockSpec((count, 16, 128), lambda *_: (0, 0, 0))
        rhs_all = pl.BlockSpec((count, 16, 128), lambda *_, b=base // count: (b, 0, 0))
        if whole:
            z = call(
                functools.partial(residue_kernel, *info),
                [],
                (1,),
                [pl.BlockSpec(recv.shape, lambda *_: (0, 0, 0, 0)), rhs_all],
                every,
                piece,
                {},
                recv,
                rhs,
            )
            gathered = exchange(z, "prow")
            lo, inverse = [pair for pair in inverses if pair[0] <= base][-1]
            inverse, _ = lax.optimization_barrier((inverse, z))
            inverse = call(
                split_inverse_kernel,
                [],
                (count,),
                [pl.BlockSpec((16, 1, 32, 512), lambda s, *_, b=base - lo: (0, b + s, 0, 0))],
                pl.BlockSpec((1, 1024, 512), lambda s, *_: (s, 0, 0)),
                jax.ShapeDtypeStruct((count, 1024, 512), jnp.bfloat16),
                {},
                inverse,
            )
        else:
            per = min(4, count)
            in_specs = [
                pl.BlockSpec((per, 16, 128), lambda s, *_, b=base // per: (b + s, 0, 0)),
                pl.BlockSpec((per, 1, 32, 512), lambda s, *_, b=base // per: (b + s, 0, 0, 0)),
            ]
            args = [natural, inverse_rows]
            if height > 0:
                in_specs = [pl.BlockSpec((recv.shape[0], per, 16, 128), lambda s, *_: (0, s, 0, 0))] + in_specs
                args = [recv] + args
            some = pl.BlockSpec((16, per, 16, 128), lambda s, *_: (0, s, 0, 0))
            kernel = functools.partial(partial_kernel, *info)
            parts = call(kernel, [pltpu.VMEM((per * 32, 128), f32)], (count // per,), in_specs, some, piece, {}, *args)
            parts = exchange(parts, "prow")
            if height == 0:
                wholes, parts = lax.optimization_barrier((wholes, parts))
                inverses = [(lo, lax.all_gather(part, "prow", axis=0)) for lo, part in zip(cuts[:-1], wholes)]
            if height == 1:
                halves = [(4, 3, 0, 1), (2, 2, 0, 0), (1, 1, 0, 2)]
                y, sol, chosen = call(
                    functools.partial(solved_and_choose_kernel, *info),
                    [],
                    (1,),
                    [every]
                    + [
                        pl.BlockSpec((m, n, 32, 256), lambda _, info, a=a, b=b: (a, b, 0, info[1] % 2))
                        for m, n, a, b in halves
                    ],
                    [every, every_own, pl.BlockSpec((17, 32, 256), lambda *_: (0, 0, 0))],
                    [piece, own, jax.ShapeDtypeStruct((17, 32, 256), f32)],
                    {},
                    parts,
                    *[top] * 3,
                )
                top = lax.all_gather(chosen, "prow", axis=0)
            else:
                kernel = functools.partial(solved_kernel, *info)
                y, sol = call(kernel, [], (1,), [every], [every, every_own], [piece, own], {}, parts)
            outputs.append(sol)
            gathered = exchange(y, "prow")
        steps = [(0, 1), (1, reach)] if height + 1 < TOP else [(0, reach)]
        updated = []
        given, source = gathered, "z" if whole else "y"
        for start, end in steps:
            per = min(2, count)
            in_specs = [pl.BlockSpec((16, per, 16, 128), lambda s, *_: (0, s, 0, 0))]
            if source == "t":
                in_specs = [pl.BlockSpec((per, 64, 512), lambda s, *_: (s, 0, 0))]
            args = [given]
            out_specs, out_shape = [], []
            if source == "z":
                in_specs.append(pl.BlockSpec((per, 1024, 512), lambda s, *_: (s, 0, 0)))
                args.append(inverse)
                out_specs.append(pl.BlockSpec((per, 16, 128), lambda s, *_: (s, 0, 0)))
                out_shape.append(own)
                if end < reach:
                    out_specs.append(pl.BlockSpec((per, 64, 512), lambda s, *_: (s, 0, 0)))
                    out_shape.append(jax.ShapeDtypeStruct((count, 64, 512), f32))
            in_specs.append(
                pl.BlockSpec((per, 1, end, 32, 512), lambda s, *_, b=base // per: (b + s, 0, 0, 0, 0))
            )
            args.append(panels)
            aliases = {}
            for d in range(start, end):
                shape = (16 * slot_counts[height + 1 + d], 16, 128)
                spec = pl.BlockSpec(shape, lambda *_: (0, 0, 0))
                if height > 0:
                    aliases[len(in_specs)] = len(out_specs)
                    in_specs.append(spec)
                    args.append(pending[d])
                out_specs.append(spec)
                out_shape.append(jax.ShapeDtypeStruct(shape, f32))
            results = call(
                functools.partial(spread_kernel, *info, source, start, end),
                SCRATCH,
                (count // per,),
                in_specs,
                out_specs,
                out_shape,
                aliases,
                *args,
            )
            results = list(results)
            if source == "z":
                outputs.append(results.pop(0))
                if end < reach:
                    given, source = results.pop(0), "t"
            updated += results
        results = updated
        if height + 1 < TOP:
            following = slot_counts[height + 1]
            pending = results[1:]
            if height < PAIRED:
                half = pl.BlockSpec((8 * following, 16, 128), lambda *_: (0, 0, 0))
                there = lax.ppermute(results[0][8 * following :], "pcol", [(i, i ^ 1) for i in range(16)])
                joined = call(
                    join_kernel,
                    [],
                    (1,),
                    [half, half],
                    pl.BlockSpec((8, following, 16, 128), lambda *_: (0, 0, 0, 0)),
                    jax.ShapeDtypeStruct((8, following, 16, 128), f32),
                    {},
                    results[0],
                    there,
                )
                recv = lax.all_to_all(
                    joined,
                    "pcol",
                    0,
                    0,
                    tiled=True,
                    axis_index_groups=[[core + 2 * z for z in range(8)] for core in range(2)],
                )
            else:
                recv = exchange(results[0].reshape(16, following, 16, 128), "pcol")
    many = pl.BlockSpec((16, 16, 128), lambda *_: (0, 0, 0))
    sides = pl.BlockSpec((16, 8, 256), lambda *_: (0, 0, 0))
    sides_shape = jax.ShapeDtypeStruct((16, 8, 256), f32)
    turned = call(
        turn_kernel,
        [pltpu.VMEM((256, 128), f32)],
        (1,),
        [many] * 3 + [pl.BlockSpec((19, 16, 128), lambda *_: (0, 0, 0))],
        sides,
        sides_shape,
        {},
        *results,
        rhs,
    )
    total = call(sum_kernel, [], (1,), [sides], sides, sides_shape, {}, exchange(turned, "pcol"))
    gathered = exchange(total, "prow")
    top, _ = lax.optimization_barrier((top, total))
    upper = call(
        near_kernel,
        [],
        (5,),
        [pl.BlockSpec((16, 1, 32, 256), lambda s, *_: (0, 12 + s, 0, 0))],
        pl.BlockSpec((1, 512, 256), lambda s, *_: (s, 0, 0)),
        jax.ShapeDtypeStruct((5, 512, 256), f32),
        {},
        top,
    )
    gathered, upper = lax.optimization_barrier((gathered, upper))
    near.append(upper)
    def whole_of(*shape):
        return pl.BlockSpec(shape, lambda *_: (0,) * len(shape)), jax.ShapeDtypeStruct(shape, f32)

    def other_core(x):
        return lax.ppermute(x, "pcol", [(i, i ^ 1) for i in range(16)])

    found, found_shape = whole_of(16, 8, 128)
    three, three_shape = whole_of(3, 8, 512)
    single, single_shape = whole_of(8, 512)
    solved, left = call(
        low_kernel,
        [pltpu.VMEM((4, 8, 512), f32)],
        (2,),
        [sides, pl.BlockSpec((16, 6, 32, 256), lambda s, *_: (0, s, 0, 0))],
        [found, three],
        [found_shape, three_shape],
        {},
        gathered,
        top,
    )
    solved, left = call(
        middle_kernel,
        [],
        (1,),
        [three, three, found, pl.BlockSpec((4, 512, 256), lambda *_: (0, 0, 0))],
        [found, single],
        [found_shape, single_shape],
        {},
        left,
        other_core(left),
        solved,
        upper,
    )
    solved = call(
        root_kernel,
        [],
        (1,),
        [single, single, found, pl.BlockSpec((1, 512, 256), lambda *_: (4, 0, 0))],
        found,
        found_shape,
        {},
        left,
        other_core(left),
        solved,
        upper,
    )
    out = call(
        last_kernel,
        tall,
        (1,),
        [found] + [pl.BlockSpec(x.shape, lambda *_: (0, 0, 0)) for x in outputs],
        all_sides,
        jax.ShapeDtypeStruct((19, 16, 128), f32),
        {},
        exchange(solved, "pcol"),
        *outputs,
    )
    return out.reshape(19, 1, 2048)


def solution(mesh):
    in_specs = (
        P(None, "pcol", "prow"),
        P(None, "pcol", "prow", None),
        P(None, "pcol", None, "prow", None),
        P(None, "pcol", None),
        P(None, "pcol"),
        P(),
    )
    out_specs = P(None, "pcol", "prow")
    return jax.shard_map(
        on_device, mesh=mesh, in_specs=in_specs, out_specs=out_specs, check_vma=False
    )
```
